128 devices in a mesh: gx: 8 (over x, core), yz: 16 (over z, y).
Axes of the slice: x: 4, y: 4, z: 4, core: 2. Of those that a mesh axis runs over, the one named last changes fastest.
Arguments:
- perm_class: int32 [256, 512, 512], P('gx', 'yz'), may hold values from 0 to 7
- class_drag: float32 [8], replicated, may hold values from 0.05 to 20
- force: float32 [256, 512, 512], P('gx', 'yz'), may hold values from -6 to 6
- coarse_inverse: float32 [128, 128], replicated, may hold values from -0.5 to 0.5
- coarse_owner: int32 [128], replicated, may hold values from 0 to 127, each once
Outputs:
- velocity: float32 [256, 512, 512], P('gx', 'yz')
- mult_x: float32 [8, 512, 512], P('gx', 'yz')
- mult_y: float32 [256, 16, 512], P('gx', 'yz')
The draws below stay inside these ranges and needn't reach their ends.
Inputs may be any that keep to these rules, and one draw needn't show every extreme that they name: coarse_owner is a permutation: each coarse row belongs to exactly one subdomain.
All inputs are finite; a program needn't handle non-finite values.
Results may differ from the reference program's by a relative error of at most 0.0001.
Values sent between devices are 32-bit elements; how exact they have to be, the bound alone decides.
A program may use at most 128 MiB of HBM per device.

```python
import math
import jax
import jax.numpy as jnp
from jax import lax

CX = 32
CY = 32
CLASSES = 8
SWEEPS = 8
ITERS = 2
SUB_X = 8
SUB_Y = 16
NX = 256
NY = 512
NZ = 512


def touch_ends(array, key, low, top_value):
    longest = array.shape.index(max(array.shape))
    spots = []
    for shift in (0, 1):
        where = [jax.random.randint(jax.random.fold_in(key, axis), (), 0, length) for axis, length in enumerate(array.shape)]
        where[longest] = (where[longest] + shift) % array.shape[longest]
        spots.append(tuple(where))
    return array.at[spots[0]].set(low).at[spots[1]].set(top_value)


def block_levels(stream_key, shape, shards, low, top_value):
    def one(position, shards_of):
        steps = jax.random.uniform(jax.random.fold_in(jax.random.fold_in(stream_key, 6), position), (shards_of,), jnp.float32, low / len(shards), top_value / len(shards))
        return jnp.repeat(jnp.exp(steps), shape[position] // shards_of).reshape((-1,) + (1,) * (len(shape) - position - 1))

    loudness = one(*shards[0])
    for cut in shards[1:]:
        loudness = loudness * one(*cut)
    return loudness


def scatter_about(key, extent, deviation, limit, pieces=(), kind=jnp.bfloat16):
    array = jax.random.normal(key, extent, jnp.float32) * deviation
    if len(pieces) > 0:
        array = block_levels(key, extent, pieces, -0.22, 0.18) * array
    return jnp.clip(array, min=-limit, max=limit).astype(kind)


def setup_inputs(seed: int = 0) -> dict:
    key_of = jax.random.split(jax.random.key(seed), 6)
    perm_class = touch_ends(jax.random.randint(key_of[0], (NX, NY, NZ), 0, CLASSES), jax.random.fold_in(key_of[0], 1), 0, CLASSES - 1).astype(jnp.int32)
    class_drag = jnp.clip(jnp.exp(jax.random.uniform(key_of[1], (CLASSES,), jnp.float32, math.log(0.05), math.log(20.0))), 0.05, 20.0)
    force = scatter_about(key_of[2], (NX, NY, NZ), 1.0, 6.0, ((0, 8), (1, 16)), jnp.float32)
    coarse_inverse = scatter_about(key_of[3], (SUB_X * SUB_Y, SUB_X * SUB_Y), (SUB_X * SUB_Y) ** -0.5, 0.5, (), jnp.float32)
    coarse_owner = jax.random.permutation(key_of[4], SUB_X * SUB_Y).astype(jnp.int32)
    return dict(perm_class=perm_class, class_drag=class_drag, force=force, coarse_inverse=coarse_inverse, coarse_owner=coarse_owner)


def operate(field, drag_field):
    padded = jnp.pad(field, ((0, 0), (1, 1), (0, 0), (1, 1), (1, 1)))
    beside = padded[:, 2:, :, 1:-1, 1:-1] + padded[:, :-2, :, 1:-1, 1:-1]
    beside = beside + padded[:, 1:-1, :, 2:, 1:-1] + padded[:, 1:-1, :, :-2, 1:-1]
    beside = beside + padded[:, 1:-1, :, 1:-1, 2:] + padded[:, 1:-1, :, 1:-1, :-2]
    return (6.0 + drag_field) * field - beside

def subsum(values):
    return lax.optimization_barrier(jnp.sum(values, axis=(1, 3, 4), keepdims=True))

def inner_solve(right_side, start_field, drag_field):
    solution = start_field
    residual = right_side - operate(solution, drag_field)
    direction = residual
    norm_now = subsum(residual * residual)
    for sweep_index in range(SWEEPS):
        image = operate(direction, drag_field)
        alpha = norm_now / subsum(direction * image)
        solution = solution + alpha * direction
        residual = residual - alpha * image
        norm_next = subsum(residual * residual)
        direction = residual + norm_next / norm_now * direction
        norm_now = norm_next
    return solution

def spread(weights, values):
    return weights[None, :, None, :, None] * values[:, None, :, None, :]

def reference(perm_class, class_drag, force, coarse_inverse, coarse_owner):
    shape_five = (SUB_X, CX, SUB_Y, CY, NZ)
    drag_field = class_drag[perm_class].reshape(shape_five)
    force_five = force.reshape(shape_five)
    lam_x = jnp.zeros((SUB_X, SUB_Y, CY, NZ), jnp.float32)
    lam_y = jnp.zeros((SUB_X, CX, SUB_Y, NZ), jnp.float32)
    solution = jnp.zeros(shape_five, jnp.float32)
    wide_x = jnp.arange(CX, dtype=jnp.float32) / (CX - 1)
    wide_y = jnp.arange(CY, dtype=jnp.float32) / (CY - 1)
    area_a = (1.0 - wide_x)[:, None] * (1.0 - wide_y)[None, :]
    area_b = (1.0 - wide_x)[:, None] * wide_y[None, :]
    area_c = wide_x[:, None] * (1.0 - wide_y)[None, :]
    area_d = wide_x[:, None] * wide_y[None, :]
    coupling = coarse_inverse[coarse_owner][:, coarse_owner]
    total_if = float((SUB_X - 1) * NY * NZ + NX * (SUB_Y - 1) * NZ)
    for outer_index in range(ITERS):
        load = jnp.zeros(shape_five, jnp.float32)
        load = load.at[:, CX - 1].add(-lam_x)
        load = load.at[1:, 0].add(lam_x[:-1])
        load = load.at[:, :, :, CY - 1].add(-lam_y)
        load = load.at[:, :, 1:, 0].add(lam_y[:, :, :-1])
        solution = inner_solve(force_five + load, solution, drag_field)
        corners = jnp.stack([solution[:, 0, :, 0], solution[:, 0, :, CY - 1], solution[:, CX - 1, :, 0], solution[:, CX - 1, :, CY - 1]], axis=2)
        corners = corners.reshape(SUB_X * SUB_Y, 4, NZ)
        correction = jnp.einsum('st,tcz->scz', coupling, corners, precision=lax.Precision.HIGHEST)
        correction = correction.reshape(SUB_X, SUB_Y, 4, NZ)
        added = spread(area_a, correction[:, :, 0]) + spread(area_b, correction[:, :, 1])
        added = added + spread(area_c, correction[:, :, 2])
        added = added + spread(area_d, correction[:, :, 3])
        solution = solution + added
        jump_x = solution[:-1, CX - 1] - solution[1:, 0]
        jump_x = jnp.pad(jump_x, ((0, 1), (0, 0), (0, 0), (0, 0)))
        jump_y = solution[:, :, :-1, CY - 1] - solution[:, :, 1:, 0]
        jump_y = jnp.pad(jump_y, ((0, 0), (0, 0), (0, 1), (0, 0)))
        total = jnp.sum(jump_x * jump_x) + jnp.sum(jump_y * jump_y)
        step_size = 0.5 / jnp.sqrt(total / total_if + 1e-06)
        lam_x = lam_x + step_size * jump_x
        lam_y = lam_y + step_size * jump_y
    return (solution.reshape(NX, NY, NZ), lam_x.reshape(SUB_X, NY, NZ), lam_y.reshape(NX, SUB_Y, NZ))
```

```python
import functools

import jax
import jax.numpy as jnp
from jax import lax
from jax.experimental import pallas as pl
from jax.experimental.pallas import tpu as pltpu
from jax.sharding import PartitionSpec as P

CLASSES = 8
SWEEPS = 8
ITERS = 2
F32 = jnp.float32
MESH = pl.DeviceIdType.MESH
PLANE = 128
UNROLL = 8


def rows(x):
    return pl.ds(pl.multiple_of(x * PLANE, PLANE), PLANE)


def tiles(value):
    return value.reshape(4, 4, 8, 128)


def beside_yz(cur):
    lane = lax.broadcasted_iota(jnp.int32, (4, 4, 8, 128), 3)
    sub = lax.broadcasted_iota(jnp.int32, (4, 1, 8, 128), 2)
    gap = jnp.zeros((1, 4, 8, 128), F32)
    up = pltpu.roll(cur, 1, 3)
    down = pltpu.roll(cur, 127, 3)
    left = jnp.where(lane == 0, jnp.concatenate([gap, up[:-1]], axis=0), up)
    right = jnp.where(lane == 127, jnp.concatenate([down[1:], gap], axis=0), down)
    before = jnp.where(sub == 0, 0.0, pltpu.roll(cur[:, 3:4], 1, 2))
    after = jnp.where(sub == 7, 0.0, pltpu.roll(cur[:, 0:1], 7, 2))
    low = jnp.concatenate([before, cur[:, 0:3]], axis=1)
    high = jnp.concatenate([cur[:, 1:4], after], axis=1)
    return (high + low) + (left + right)


def total_of(a):
    a = jnp.sum(jnp.sum(a, axis=0, keepdims=True), axis=1, keepdims=True)
    return jnp.broadcast_to(a, (8, 128))


def splat(a):
    return a[None, None]


def sweep_pass(k, first, a, b, U, W):
    def fresh(x):
        u = tiles(W[rows(x), :]) - splat(a) * tiles(U[k, rows(x), :])
        u = u - splat(b) * tiles(U[k - 1, rows(x), :])
        U[k + 1, rows(x), :] = u.reshape(PLANE, 128)
        return u

    def step(x, acc):
        uu, uw = acc
        if first:
            above = tiles(U[k + 1, rows(x + 2), :])
        else:
            above = fresh(x + 2)
        cur = tiles(U[k + 1, rows(x + 1), :])
        below = tiles(U[k + 1, rows(x), :])
        w = tiles(U[0, rows(x + 1), :]) * cur - ((above + below) + beside_yz(cur))
        W[rows(x + 1), :] = w.reshape(PLANE, 128)
        return uu + jnp.sum(cur * cur, axis=(0, 1)), uw + jnp.sum(cur * w, axis=(0, 1))

    if not first:
        fresh(1)
    zero = jnp.zeros((8, 128), F32)
    uu, uw = lax.fori_loop(0, 32, step, (zero, zero), unroll=UNROLL)
    g = total_of(uu)
    return g, total_of(uw) / g


def y_weights(width):
    t = lax.broadcasted_iota(jnp.int32, (1, 4, 8, 128), 1)
    s = lax.broadcasted_iota(jnp.int32, (1, 4, 8, 128), 2)
    return (4 * s + t).astype(F32) / (width - 1)


def kernel(
    ni, nj, perm, drag, force, cinv, owner,
    xpre, corr_out, lamx_out, lamy_out,
    U, W, X, fst, pst, cf, wsp, cinv_s, cbuf, G, PB, R, FS, FR, CS, CR, TS, T1, T2, LAM, JMP,
    in_sem, ci_sem, out_sem, sg, rg, sr, rr, sf, rf, sc, rc, s1, r1, s2, r2,
):
    i = lax.axis_index("gx")
    j = lax.axis_index("yz")
    zero = jnp.zeros((8, 128), F32)
    plane0 = jnp.zeros((PLANE, 128), F32)

    barrier = pltpu.get_barrier_semaphore()
    for d in range(1, ni):
        pl.semaphore_signal(barrier, inc=1, device_id={"gx": lax.rem(i + d, ni)}, device_id_type=MESH)
    for d in range(1, nj):
        pl.semaphore_signal(barrier, inc=1, device_id={"yz": lax.rem(j + d, nj)}, device_id_type=MESH)

    loads = []
    for c in range(4):
        cols = pl.ds(c * 128, 128)
        loads.append((
            pltpu.make_async_copy(perm.at[:, cols], pst.at[c], in_sem.at[2 * c]),
            pltpu.make_async_copy(force.at[:, cols], fst.at[c], in_sem.at[2 * c + 1]),
        ))
        for copy in loads[-1]:
            copy.start()
    weights_copy = pltpu.make_async_copy(cinv, cinv_s, ci_sem)
    weights_copy.start()

    for k in range(SWEEPS + 2):
        U[k, rows(0), :] = plane0
        U[k, rows(33), :] = plane0
    W[rows(33), :] = plane0

    level = [6.0 + drag[c] for c in range(CLASSES)]
    for c in range(4):
        for copy in loads[c]:
            copy.wait()

        def stage(x, carry, c=c):
            base = pl.multiple_of(x * 32, 32)
            for t in range(4):
                cls = pst[c, pl.ds(base + t, 8, stride=4), :]
                b0, b1, b2 = (cls & 1) != 0, (cls & 2) != 0, (cls & 4) != 0
                pairs = [jnp.where(b0, level[n + 1], level[n]) for n in range(0, 8, 2)]
                quads = [jnp.where(b1, pairs[1], pairs[0]), jnp.where(b1, pairs[3], pairs[2])]
                at = pl.ds(pl.multiple_of((x + 1) * PLANE + c * 32 + t * 8, 8), 8)
                U[0, at, :] = jnp.where(b2, quads[1], quads[0])
                U[1, at, :] = fst[c, pl.ds(base + t, 8, stride=4), :]
            return carry

        lax.fori_loop(0, 32, stage, 0, unroll=4)

    weights_copy.wait()
    for sx in range(ni):
        row = owner[sx * nj + j]

        def fill(ty, carry, sx=sx, row=row):
            wsp[sx, ty] = jnp.full((8, 128), cinv_s[row, owner[i * nj + ty]], F32)
            return carry

        lax.fori_loop(0, nj, fill, 0, unroll=4)

    has_right = (i < ni - 1).astype(F32)
    has_left = (i > 0).astype(F32)
    has_upper = (j < nj - 1).astype(F32)
    has_lower = (j > 0).astype(F32)
    wy = y_weights(32)
    wx8 = lax.broadcasted_iota(jnp.int32, (32, 128), 0).astype(F32) / 31.0
    right, left = {"gx": lax.rem(i + 1, ni)}, {"gx": lax.rem(i + ni - 1, ni)}
    upper, lower = {"yz": lax.rem(j + 1, nj)}, {"yz": lax.rem(j + nj - 1, nj)}
    sends = []

    def remote(src, dst, ssem, rsem, dev):
        return pltpu.make_async_remote_copy(
            src_ref=src, dst_ref=dst, send_sem=ssem, recv_sem=rsem, device_id=dev, device_id_type=MESH
        )

    for it in range(ITERS):
        g, a = sweep_pass(0, True, zero, zero, U, W)
        cf[0], cf[8] = a, zero

        def body(k, carry):
            g, a, b = carry
            gn, an = sweep_pass(k, False, a, b, U, W)
            bn = gn / g
            cf[k] = an
            cf[8 + k] = bn
            return gn, an, bn

        g, a, b = lax.fori_loop(1, SWEEPS, body, (g, a, zero))

        av = [cf[k] for k in range(SWEEPS)]
        bv = [cf[8 + k] for k in range(SWEEPS)]
        inv, z = [1.0 / av[0]], [jnp.ones((8, 128), F32)]
        for k in range(1, SWEEPS):
            z.append(-z[k - 1] * inv[k - 1])
            inv.append(1.0 / (av[k] - bv[k] * inv[k - 1]))
        y = [None] * SWEEPS
        y[SWEEPS - 1] = z[SWEEPS - 1] * inv[SWEEPS - 1]
        for k in range(SWEEPS - 2, -1, -1):
            y[k] = (z[k] - bv[k + 1] * y[k + 1]) * inv[k]

        for n, x in ((0, 0), (1, 31)):
            f = None if it == 0 else tiles(X[rows(x), :])
            for k in range(SWEEPS):
                term = splat(y[k]) * tiles(U[k + 1, rows(x + 1), :])
                f = term if f is None else f + term
            FS[it, n] = f.reshape(PLANE, 128)
            for m, (t, s) in enumerate(((0, 0), (3, 7))):
                for c in range(4):
                    cbuf[it, pl.ds((2 * n + m) * 4 + c, 1), :] = f[c, t, s : s + 1, :]
        G[it, j] = cbuf[it]
        if it == 0:
            pl.semaphore_wait(barrier, ni + nj - 2)
        gather = []
        for d in range(1, nj):
            dev = {"yz": lax.rem(j + d, nj)}
            copy = remote(cbuf.at[it], G.at[it, j], sg.at[it, d], rg.at[it, d], dev)
            copy.start()
            sends.append(copy)
            came = G.at[it, lax.rem(j + nj - d, nj)]
            gather.append(remote(cbuf.at[it], came, sg.at[it, d], rg.at[it, d], dev))
        for n, (t, s) in enumerate(((0, 0), (3, 7))):
            for c in range(4):
                for h in range(4):
                    r0 = h * 8 * PLANE + c * 32 + t * 8 + s
                    f = None if it == 0 else X[pl.ds(r0, 8, stride=PLANE), :]
                    for k in range(SWEEPS):
                        term = y[k] * U[k + 1, pl.ds(PLANE + r0, 8, stride=PLANE), :]
                        f = term if f is None else f + term
                    FS[it, 2 + n, pl.ds(c * 32 + h * 8, 8), :] = f
        faces = []
        for src, dst, dev in ((1, 0, right), (0, 1, left), (3, 2, upper), (2, 3, lower)):
            copy = remote(FS.at[it, src], FR.at[it, dst], sf.at[it, dst], rf.at[it, dst], dev)
            copy.start()
            faces.append(copy)
        sends.extend(faces)

        def gather_x(x, carry):
            f = None if it == 0 else tiles(X[rows(x), :])
            for k in range(SWEEPS):
                term = splat(y[k]) * tiles(U[k + 1, rows(x + 1), :])
                f = term if f is None else f + term
            if it == 0:
                X[rows(x), :] = f.reshape(PLANE, 128)
                u = tiles(W[rows(x + 1), :]) - splat(a) * tiles(U[8, rows(x + 1), :])
                u = u - splat(b) * tiles(U[7, rows(x + 1), :])
                U[1, rows(x + 1), :] = (splat(-y[7]) * u).reshape(PLANE, 128)
            else:
                for c in range(4):
                    for t in range(4):
                        fst[c, pl.ds(x * 32 + t, 8, stride=4), :] = f[c, t]
            return carry

        lax.fori_loop(0, 32, gather_x, 0, unroll=4)
        if it == ITERS - 1:
            out_copy = pltpu.make_async_copy(fst, xpre, out_sem)
            out_copy.start()

        for copy in gather:
            copy.wait_recv()
        for sx in range(ni):
            lo, hi = zero, zero
            for ty in range(nj):
                wt = wsp[sx, ty]
                lo = lo + wt * G[it, ty, 0:8, :]
                hi = hi + wt * G[it, ty, 8:16, :]
            PB[it, sx, 0:8, :] = lo
            PB[it, sx, 8:16, :] = hi
        R[it, i] = PB[it, i]
        parts = []
        for d in range(1, ni):
            to = lax.rem(i + d, ni)
            copy = remote(PB.at[it, to], R.at[it, i], sr.at[it, d], rr.at[it, d], {"gx": to})
            copy.start()
            sends.append(copy)
            came = R.at[it, lax.rem(i + ni - d, ni)]
            parts.append(remote(PB.at[it, to], came, sr.at[it, d], rr.at[it, d], {"gx": to}))
        for copy in parts:
            copy.wait_recv()
        own = R[it, 0]
        for n in range(1, ni):
            own = own + R[it, n]
        CS[it] = own
        nbr = []
        for dst, dev in ((0, right), (1, left), (2, upper), (3, lower)):
            copy = remote(CS.at[it], CR.at[it, dst], sc.at[it, dst], rc.at[it, dst], dev)
            copy.start()
            nbr.append(copy)
        sends.extend(nbr)

        def row(block, c, chunk):
            return block[c * 4 + chunk : c * 4 + chunk + 1, :]

        def along_y(block, c0, c1):
            out = []
            for chunk in range(4):
                p = row(block, c0, chunk)[None, None]
                q = row(block, c1, chunk)[None, None]
                out.append((1.0 - wy) * p + wy * q)
            return jnp.concatenate(out, axis=0)

        def along_x(block, c0, c1):
            out = []
            for chunk in range(4):
                out.append((1.0 - wx8) * row(block, c0, chunk) + wx8 * row(block, c1, chunk))
            return jnp.concatenate(out, axis=0)

        for copy in faces:
            copy.wait_recv()
        for copy in nbr:
            copy.wait_recv()
        sq = zero
        for n, (fun, c0, c1, d0, d1, sign, has) in enumerate((
            (along_y, 0, 1, 2, 3, -1.0, has_left),
            (along_y, 2, 3, 0, 1, 1.0, has_right),
            (along_x, 0, 2, 1, 3, -1.0, has_lower),
            (along_x, 1, 3, 0, 2, 1.0, has_upper),
        )):
            mine = FS[it, n] + fun(own, c0, c1).reshape(PLANE, 128)
            theirs = FR[it, n] + fun(CR[it, n], d0, d1).reshape(PLANE, 128)
            jump = (mine - theirs) * (sign * has)
            JMP[n] = jump
            if sign > 0:
                sq = sq + jnp.sum((jump * jump).reshape(16, 8, 128), axis=0)
        TS[it, 0] = sq
        T1[it, i] = sq
        some = []
        for d in range(1, ni):
            dev = {"gx": lax.rem(i + d, ni)}
            copy = remote(TS.at[it, 0], T1.at[it, i], s1.at[it, d], r1.at[it, d], dev)
            copy.start()
            sends.append(copy)
            came = T1.at[it, lax.rem(i + ni - d, ni)]
            some.append(remote(TS.at[it, 0], came, s1.at[it, d], r1.at[it, d], dev))

        def share():
            for copy in some:
                copy.wait_recv()
            part = T1[it, 0]
            for n in range(1, ni):
                part = part + T1[it, n]
            TS[it, 1] = part
            T2[it, j] = part
            for d in range(1, nj):
                dev = {"yz": lax.rem(j + d, nj)}
                copy = remote(TS.at[it, 1], T2.at[it, j], s2.at[it, d], r2.at[it, d], dev)
                copy.start()
                sends.append(copy)
                came = T2.at[it, lax.rem(j + nj - d, nj)]
                rest.append(remote(TS.at[it, 1], came, s2.at[it, d], r2.at[it, d], dev))

        rest = []
        share()
        if it == 0:
            start = along_y(own, 0, 1)
            slope = along_y(own, 2, 3) - start
            m_start = beside_yz(start)
            m_slope = beside_yz(slope)

            def corrected(x, carry):
                wx = x.astype(F32) / 31.0
                e = start + wx * slope
                beside = m_start + wx * m_slope + 2.0 * e
                diag = tiles(U[0, rows(x + 1), :])
                U[1, rows(x + 1), :] = (
                    tiles(U[1, rows(x + 1), :]) - (diag * e - beside)
                ).reshape(PLANE, 128)
                X[rows(x), :] = (tiles(X[rows(x), :]) + e).reshape(PLANE, 128)
                return carry

            lax.fori_loop(0, 32, corrected, 0)
            U[1, rows(1), :] = U[1, rows(1), :] - (start - slope / 31.0).reshape(PLANE, 128)
            U[1, rows(32), :] = U[1, rows(32), :] - (start + slope * (32.0 / 31.0)).reshape(PLANE, 128)
        for copy in rest:
            copy.wait_recv()
        total = T2[it, 0]
        for n in range(1, nj):
            total = total + T2[it, n]
        count = (ni - 1) * nj * 32 * 512 + ni * 32 * (nj - 1) * 512
        step = 0.5 / jnp.sqrt(total_of(total) / float(count) + 1e-6)
        for n in range(4):
            lam = (JMP[n].reshape(16, 8, 128) * step[None]).reshape(PLANE, 128)
            if it > 0:
                lam = LAM[n] + lam
            LAM[n] = lam
        if it == 0:
            U[1, rows(32), :] = U[1, rows(32), :] - LAM[1]
            U[1, rows(1), :] = U[1, rows(1), :] + LAM[0]
            for n, (t, s, sign) in ((3, (3, 7, -1.0)), (2, (0, 0, 1.0))):
                for c in range(4):
                    for h in range(4):
                        at = pl.ds(PLANE + h * 8 * PLANE + c * 32 + t * 8 + s, 8, stride=PLANE)
                        U[1, at, :] = U[1, at, :] + sign * LAM[n, pl.ds(c * 32 + h * 8, 8), :]
        else:
            corr_out[...] = own
            lamy_out[...] = LAM[3]
            for c in range(4):
                for t in range(4):
                    lamx_out[pl.ds(c * 32 + t, 8, stride=4), :] = LAM[1, pl.ds(c * 32 + t * 8, 8), :]
    for copy in sends:
        copy.wait_send()
    out_copy.wait()


def finish_kernel(xpre, corr, lamx, lamy, vel, mx, my):
    step = pl.program_id(0)
    wide = vel.shape[0]
    wx = (lax.broadcasted_iota(jnp.int32, (wide, 32, 128), 0) + step * wide).astype(F32) / 31.0
    wy = lax.broadcasted_iota(jnp.int32, (wide, 32, 128), 1).astype(F32) / 31.0
    for c in range(4):
        at = pl.ds(c * 128, 128)
        c0, c1, c2, c3 = (corr[n * 4 + c : n * 4 + c + 1, :][None] for n in range(4))
        e = (1.0 - wx) * ((1.0 - wy) * c0 + wy * c1) + wx * ((1.0 - wy) * c2 + wy * c3)
        vel[:, :, at] = xpre[c].reshape(wide, 32, 128) + e

    @pl.when(step == 0)
    def _():
        for c in range(4):
            at = pl.ds(c * 128, 128)
            mx[:, at] = lamx[pl.ds(c * 32, 32), :]
            my[:, at] = lamy[pl.ds(c * 32, 32), :]


def on_device(ni, nj, perm_class, class_drag, force, coarse_inverse, coarse_owner):
    hbm = pl.BlockSpec(memory_space=pl.ANY)
    vmem = pl.BlockSpec(memory_space=pltpu.VMEM)
    smem = pl.BlockSpec(memory_space=pltpu.SMEM)
    dma = pltpu.SemaphoreType.DMA
    xpre, corr, lamx, lamy = pl.pallas_call(
        functools.partial(kernel, ni, nj),
        out_shape=(
            jax.ShapeDtypeStruct((4, 1024, 128), F32),
            jax.ShapeDtypeStruct((16, 128), F32),
            jax.ShapeDtypeStruct((128, 128), F32),
            jax.ShapeDtypeStruct((128, 128), F32),
        ),
        in_specs=[hbm, smem, hbm, hbm, smem],
        out_specs=(hbm, vmem, vmem, vmem),
        scratch_shapes=[
            pltpu.VMEM((SWEEPS + 2, 34 * PLANE, 128), F32),
            pltpu.VMEM((34 * PLANE, 128), F32),
            pltpu.VMEM((32 * PLANE, 128), F32),
            pltpu.VMEM((4, 1024, 128), F32),
            pltpu.VMEM((4, 1024, 128), jnp.int32),
            pltpu.VMEM((16, 8, 128), F32),
            pltpu.VMEM((ni, nj, 8, 128), F32),
            pltpu.SMEM((ni * nj, ni * nj), F32),
            pltpu.VMEM((ITERS, 16, 128), F32),
            pltpu.VMEM((ITERS, nj, 16, 128), F32),
            pltpu.VMEM((ITERS, ni, 16, 128), F32),
            pltpu.VMEM((ITERS, ni, 16, 128), F32),
            pltpu.VMEM((ITERS, 4, PLANE, 128), F32),
            pltpu.VMEM((ITERS, 4, PLANE, 128), F32),
            pltpu.VMEM((ITERS, 16, 128), F32),
            pltpu.VMEM((ITERS, 4, 16, 128), F32),
            pltpu.VMEM((ITERS, 2, 8, 128), F32),
            pltpu.VMEM((ITERS, ni, 8, 128), F32),
            pltpu.VMEM((ITERS, nj, 8, 128), F32),
            pltpu.VMEM((4, PLANE, 128), F32),
            pltpu.VMEM((4, PLANE, 128), F32),
            dma((8,)), dma, dma,
            dma((ITERS, nj)), dma((ITERS, nj)),
            dma((ITERS, ni)), dma((ITERS, ni)),
            dma((ITERS, 4)), dma((ITERS, 4)),
            dma((ITERS, 4)), dma((ITERS, 4)),
            dma((ITERS, ni)), dma((ITERS, ni)),
            dma((ITERS, nj)), dma((ITERS, nj)),
        ],
        compiler_params=pltpu.CompilerParams(
            collective_id=0, has_side_effects=True, vmem_limit_bytes=56 * 2**20
        ),
        name="solve",
    )(perm_class.reshape(1024, 512), class_drag, force.reshape(1024, 512), coarse_inverse, coarse_owner)
    steps, wide = 4, 8
    velocity, mult_x, mult_y = pl.pallas_call(
        finish_kernel,
        grid=(steps,),
        out_shape=(
            jax.ShapeDtypeStruct((32, 32, 512), F32),
            jax.ShapeDtypeStruct((32, 512), F32),
            jax.ShapeDtypeStruct((32, 512), F32),
        ),
        in_specs=[
            pl.BlockSpec((4, 32 * wide, 128), lambda n: (0, n, 0)),
            pl.BlockSpec((16, 128), lambda n: (0, 0)),
            pl.BlockSpec((128, 128), lambda n: (0, 0)),
            pl.BlockSpec((128, 128), lambda n: (0, 0)),
        ],
        out_specs=(
            pl.BlockSpec((wide, 32, 512), lambda n: (n, 0, 0)),
            pl.BlockSpec((32, 512), lambda n: (0, 0)),
            pl.BlockSpec((32, 512), lambda n: (0, 0)),
        ),
        compiler_params=pltpu.CompilerParams(vmem_limit_bytes=16 * 2**20),
        name="finish",
    )(xpre, corr, lamx, lamy)
    return velocity, mult_x[None], mult_y[:, None]


def solution(mesh):
    return jax.shard_map(
        functools.partial(on_device, mesh.shape["gx"], mesh.shape["yz"]),
        mesh=mesh,
        in_specs=(P("gx", "yz", None), P(), P("gx", "yz", None), P(), P()),
        out_specs=(P("gx", "yz", None), P("gx", "yz", None), P("gx", "yz", None)),
        check_vma=False,
    )
```

```python
import functools

import jax
import jax.numpy as jnp
from jax import lax
from jax.experimental import pallas as pl
from jax.experimental.pallas import tpu as pltpu
from jax.sharding import PartitionSpec as P

CLASSES = 8
SWEEPS = 8
ITERS = 2
F32 = jnp.float32
MESH = pl.DeviceIdType.MESH
PLANE = 128
UNROLL = 16


def rows(x):
    return pl.ds(pl.multiple_of(x * PLANE, PLANE), PLANE)


def tiles(value):
    return value.reshape(4, 4, 8, 128)


def beside_yz(cur):
    lane = lax.broadcasted_iota(jnp.int32, (4, 4, 8, 128), 3)
    sub = lax.broadcasted_iota(jnp.int32, (4, 1, 8, 128), 2)
    gap = jnp.zeros((1, 4, 8, 128), F32)
    up = pltpu.roll(cur, 1, 3)
    down = pltpu.roll(cur, 127, 3)
    left = jnp.where(lane == 0, jnp.concatenate([gap, up[:-1]], axis=0), up)
    right = jnp.where(lane == 127, jnp.concatenate([down[1:], gap], axis=0), down)
    before = jnp.where(sub == 0, 0.0, pltpu.roll(cur[:, 3:4], 1, 2))
    after = jnp.where(sub == 7, 0.0, pltpu.roll(cur[:, 0:1], 7, 2))
    low = jnp.concatenate([before, cur[:, 0:3]], axis=1)
    high = jnp.concatenate([cur[:, 1:4], after], axis=1)
    return (high + low) + (left + right)


def total_of(a):
    a = jnp.sum(jnp.sum(a, axis=0, keepdims=True), axis=1, keepdims=True)
    return jnp.broadcast_to(a, (8, 128))


def splat(a):
    return a[None, None]


def sweep_pass(k, first, a, b, U, W):
    def fresh(x):
        u = tiles(W[rows(x), :]) - splat(a) * tiles(U[k, rows(x), :])
        u = u - splat(b) * tiles(U[k - 1, rows(x), :])
        U[k + 1, rows(x), :] = u.reshape(PLANE, 128)
        return u

    def step(x, acc):
        uu, uw = acc
        if first:
            above = tiles(U[k + 1, rows(x + 2), :])
        else:
            above = fresh(x + 2)
        cur = tiles(U[k + 1, rows(x + 1), :])
        below = tiles(U[k + 1, rows(x), :])
        w = tiles(U[0, rows(x + 1), :]) * cur - ((above + below) + beside_yz(cur))
        W[rows(x + 1), :] = w.reshape(PLANE, 128)
        return uu + jnp.sum(cur * cur, axis=(0, 1)), uw + jnp.sum(cur * w, axis=(0, 1))

    if not first:
        fresh(1)
    zero = jnp.zeros((8, 128), F32)
    uu, uw = lax.fori_loop(0, 32, step, (zero, zero), unroll=UNROLL)
    g = total_of(uu)
    return g, total_of(uw) / g


def y_weights(width):
    t = lax.broadcasted_iota(jnp.int32, (1, 4, 8, 128), 1)
    s = lax.broadcasted_iota(jnp.int32, (1, 4, 8, 128), 2)
    return (4 * s + t).astype(F32) / (width - 1)


def kernel(
    ni, nj, perm, drag, force, cinv, owner,
    xpre, corr_out, lamx_out, lamy_out,
    U, W, X, fst, pst, cf, wsp, cinv_s, cbuf, G, PB, R, FS, FR, TS, TR, LAM, JMP,
    in_sem, ci_sem, sg, rg, sr, rr, sf, rf, st, rt,
):
    i = lax.axis_index("gx")
    j = lax.axis_index("yz")
    zero = jnp.zeros((8, 128), F32)
    plane0 = jnp.zeros((PLANE, 128), F32)

    barrier = pltpu.get_barrier_semaphore()

    def greet(n, carry):
        dev = {"gx": lax.rem(i + n // nj, ni), "yz": lax.rem(j + n % nj, nj)}
        pl.semaphore_signal(barrier, inc=1, device_id=dev, device_id_type=MESH)
        return carry

    lax.fori_loop(1, ni * nj, greet, 0)

    loads = []
    for c in range(4):
        cols = pl.ds(c * 128, 128)
        loads.append((
            pltpu.make_async_copy(perm.at[:, cols], pst.at[c], in_sem.at[2 * c]),
            pltpu.make_async_copy(force.at[:, cols], fst.at[c], in_sem.at[2 * c + 1]),
        ))
        for copy in loads[-1]:
            copy.start()
    weights_copy = pltpu.make_async_copy(cinv, cinv_s, ci_sem)
    weights_copy.start()

    for k in range(SWEEPS + 2):
        U[k, rows(0), :] = plane0
        U[k, rows(33), :] = plane0
    W[rows(33), :] = plane0

    level = [6.0 + drag[c] for c in range(CLASSES)]
    for c in range(4):
        for copy in loads[c]:
            copy.wait()

        def stage(x, carry, c=c):
            base = pl.multiple_of(x * 32, 32)
            for t in range(4):
                cls = pst[c, pl.ds(base + t, 8, stride=4), :]
                b0, b1, b2 = (cls & 1) != 0, (cls & 2) != 0, (cls & 4) != 0
                pairs = [jnp.where(b0, level[n + 1], level[n]) for n in range(0, 8, 2)]
                quads = [jnp.where(b1, pairs[1], pairs[0]), jnp.where(b1, pairs[3], pairs[2])]
                at = pl.ds(pl.multiple_of((x + 1) * PLANE + c * 32 + t * 8, 8), 8)
                U[0, at, :] = jnp.where(b2, quads[1], quads[0])
                U[1, at, :] = fst[c, pl.ds(base + t, 8, stride=4), :]
            return carry

        lax.fori_loop(0, 32, stage, 0, unroll=4)

    has_right = (i < ni - 1).astype(F32)
    has_left = (i > 0).astype(F32)
    has_upper = (j < nj - 1).astype(F32)
    has_lower = (j > 0).astype(F32)
    wy = y_weights(32)
    wx8 = lax.broadcasted_iota(jnp.int32, (32, 128), 0).astype(F32) / 31.0
    right, left = {"gx": lax.rem(i + 1, ni)}, {"gx": lax.rem(i + ni - 1, ni)}
    upper, lower = {"yz": lax.rem(j + 1, nj)}, {"yz": lax.rem(j + nj - 1, nj)}
    sends = []

    def remote(src, dst, ssem, rsem, dev):
        return pltpu.make_async_remote_copy(
            src_ref=src, dst_ref=dst, send_sem=ssem, recv_sem=rsem, device_id=dev, device_id_type=MESH
        )

    for it in range(ITERS):
        g, a = sweep_pass(0, True, zero, zero, U, W)
        cf[0], cf[8] = a, zero

        def body(k, carry):
            g, a, b = carry
            gn, an = sweep_pass(k, False, a, b, U, W)
            bn = gn / g
            cf[k] = an
            cf[8 + k] = bn
            return gn, an, bn

        g, a, b = lax.fori_loop(1, SWEEPS, body, (g, a, zero))

        av = [cf[k] for k in range(SWEEPS)]
        bv = [cf[8 + k] for k in range(SWEEPS)]
        inv, z = [1.0 / av[0]], [jnp.ones((8, 128), F32)]
        for k in range(1, SWEEPS):
            z.append(-z[k - 1] * inv[k - 1])
            inv.append(1.0 / (av[k] - bv[k] * inv[k - 1]))
        y = [None] * SWEEPS
        y[SWEEPS - 1] = z[SWEEPS - 1] * inv[SWEEPS - 1]
        for k in range(SWEEPS - 2, -1, -1):
            y[k] = (z[k] - bv[k + 1] * y[k + 1]) * inv[k]

        for n, x in ((0, 0), (1, 31)):
            for m, (t, r) in enumerate(((0, 0), (3, 7))):
                for c in range(4):
                    at = c * 32 + t * 8
                    f = None if it == 0 else X[pl.ds(x * PLANE + at, 8), :]
                    for k in range(SWEEPS):
                        term = y[k] * U[k + 1, pl.ds((x + 1) * PLANE + at, 8), :]
                        f = term if f is None else f + term
                    cbuf[it, pl.ds((2 * n + m) * 4 + c, 1), :] = f[r : r + 1, :]
        G[it, j] = cbuf[it]
        if it == 0:
            pl.semaphore_wait(barrier, ni * nj - 1)
        gather = []
        for d in range(1, nj):
            dev = {"yz": lax.rem(j + d, nj)}
            copy = remote(cbuf.at[it], G.at[it, j], sg.at[it, d], rg.at[it, d], dev)
            copy.start()
            sends.append(copy)
            came = G.at[it, lax.rem(j + nj - d, nj)]
            gather.append(remote(cbuf.at[it], came, sg.at[it, d], rg.at[it, d], dev))
        def gather_x(x, carry):
            f = None if it == 0 else tiles(X[rows(x), :])
            for k in range(SWEEPS):
                term = splat(y[k]) * tiles(U[k + 1, rows(x + 1), :])
                f = term if f is None else f + term
            for c in range(4):
                FS[it, 2, pl.ds(c * 32 + x, 1), :] = f[c, 0, 0:1, :]
                FS[it, 3, pl.ds(c * 32 + x, 1), :] = f[c, 3, 7:8, :]
            if it == 0:
                X[rows(x), :] = f.reshape(PLANE, 128)
                u = tiles(W[rows(x + 1), :]) - splat(a) * tiles(U[8, rows(x + 1), :])
                u = u - splat(b) * tiles(U[7, rows(x + 1), :])
                U[1, rows(x + 1), :] = (splat(-y[7]) * u).reshape(PLANE, 128)
            else:
                X[rows(x), :] = f.reshape(PLANE, 128)
                for c in range(4):
                    for t in range(4):
                        xpre[c, pl.ds(x * 32 + t, 8, stride=4), :] = f[c, t]
            return carry

        lax.fori_loop(0, 32, gather_x, 0, unroll=4)
        FS[it, 0] = X[rows(0), :]
        FS[it, 1] = X[rows(31), :]
        faces = []
        for src, dst, dev in ((1, 0, right), (0, 1, left), (3, 2, upper), (2, 3, lower)):
            copy = remote(FS.at[it, src], FR.at[it, dst], sf.at[it, dst], rf.at[it, dst], dev)
            copy.start()
            faces.append(copy)
        sends.extend(faces)
        if it == 0:
            weights_copy.wait()
            for n in range(3):
                jn = lax.rem(j + nj - 1 + n, nj)
                for sx in range(ni):

                    def fill(ty, carry, n=n, sx=sx, at=owner[sx * nj + jn]):
                        wsp[n, sx, ty] = jnp.full((8, 128), cinv_s[at, owner[i * nj + ty]], F32)
                        return carry

                    lax.fori_loop(0, nj, fill, 0, unroll=4)

        for copy in gather:
            copy.wait_recv()
        sub = lax.broadcasted_iota(jnp.int32, (8, 128), 0) < 4
        for sx in range(ni):

            def term(ty, acc, sx=sx):
                lo, hi, down, up = acc
                g01, g23 = G[it, ty, 0:8, :], G[it, ty, 8:16, :]
                g13 = jnp.where(sub, pltpu.roll(g01, 4, 0), g23)
                g02 = jnp.where(sub, g01, pltpu.roll(g23, 4, 0))
                w = wsp[1, sx, ty]
                return lo + w * g01, hi + w * g23, down + wsp[0, sx, ty] * g13, up + wsp[2, sx, ty] * g02

            lo, hi, down, up = lax.fori_loop(0, nj, term, (zero,) * 4, unroll=8)
            PB[it, sx, 0:8, :] = lo
            PB[it, sx, 8:16, :] = hi
            PB[it, (sx + 1) % ni, 16:24, :] = hi
            PB[it, (sx - 1) % ni, 24:32, :] = lo
            PB[it, sx, 32:40, :] = down
            PB[it, sx, 40:48, :] = up
        R[it, i] = PB[it, i]
        parts = []
        for d in range(1, ni):
            to = lax.rem(i + d, ni)
            copy = remote(PB.at[it, to], R.at[it, i], sr.at[it, d], rr.at[it, d], {"gx": to})
            copy.start()
            sends.append(copy)
            came = R.at[it, lax.rem(i + ni - d, ni)]
            parts.append(remote(PB.at[it, to], came, sr.at[it, d], rr.at[it, d], {"gx": to}))
        for copy in faces:
            copy.wait_recv()
        for copy in parts:
            copy.wait_recv()
        sums = R[it, 0]
        for n in range(1, ni):
            sums = sums + R[it, n]
        own = sums[0:16]
        other = [sums[16 + 8 * n : 24 + 8 * n] for n in range(4)]

        def row(block, c, chunk):
            return block[c * 4 + chunk : c * 4 + chunk + 1, :]

        def along_y(block, c0, c1):
            out = []
            for chunk in range(4):
                p = row(block, c0, chunk)[None, None]
                q = row(block, c1, chunk)[None, None]
                out.append((1.0 - wy) * p + wy * q)
            return jnp.concatenate(out, axis=0)

        def along_x(block, c0, c1):
            out = []
            for chunk in range(4):
                out.append((1.0 - wx8) * row(block, c0, chunk) + wx8 * row(block, c1, chunk))
            return jnp.concatenate(out, axis=0)

        sq = zero
        for n, (fun, c0, c1, sign, has) in enumerate((
            (along_y, 0, 1, -1.0, has_left),
            (along_y, 2, 3, 1.0, has_right),
            (along_x, 0, 2, -1.0, has_lower),
            (along_x, 1, 3, 1.0, has_upper),
        )):
            mine = FS[it, n] + fun(own, c0, c1).reshape(PLANE, 128)
            theirs = FR[it, n] + fun(other[n], 0, 1).reshape(PLANE, 128)
            jump = (mine - theirs) * (sign * has)
            JMP[n] = jump
            if sign > 0:
                sq = sq + jnp.sum((jump * jump).reshape(16, 8, 128), axis=0)
        me = i * nj + j
        row_sum = jnp.sum(sq, axis=0, keepdims=True)
        TS[it] = row_sum
        TR[it, pl.ds(me, 1), :] = row_sum

        def tell(n, carry):
            dev = {"gx": lax.rem(i + n // nj, ni), "yz": lax.rem(j + n % nj, nj)}
            remote(TS.at[it], TR.at[it, pl.ds(me, 1)], st.at[it], rt.at[it], dev).start()
            return carry

        lax.fori_loop(1, ni * nj, tell, 0)
        all_but_one = TR.at[it, pl.ds(0, ni * nj - 1)]
        told = remote(all_but_one, all_but_one, st.at[it], rt.at[it], right)
        sends.append(told)
        if it == 0:
            start = along_y(own, 0, 1)
            slope = along_y(own, 2, 3) - start
            m_start = beside_yz(start)
            m_slope = beside_yz(slope)

            def corrected(x, carry):
                wx = x.astype(F32) / 31.0
                e = start + wx * slope
                beside = m_start + wx * m_slope + 2.0 * e
                diag = tiles(U[0, rows(x + 1), :])
                U[1, rows(x + 1), :] = (
                    tiles(U[1, rows(x + 1), :]) - (diag * e - beside)
                ).reshape(PLANE, 128)
                X[rows(x), :] = (tiles(X[rows(x), :]) + e).reshape(PLANE, 128)
                return carry

            lax.fori_loop(0, 32, corrected, 0)
            U[1, rows(1), :] = U[1, rows(1), :] - (start - slope / 31.0).reshape(PLANE, 128)
            U[1, rows(32), :] = U[1, rows(32), :] - (start + slope * (32.0 / 31.0)).reshape(PLANE, 128)
        told.wait_recv()
        total = jnp.sum(TR[it].reshape(ni * nj // 8, 8, 128), axis=0)
        count = (ni - 1) * nj * 32 * 512 + ni * 32 * (nj - 1) * 512
        step = 0.5 / jnp.sqrt(total_of(total) / float(count) + 1e-6)
        for n in range(4):
            lam = (JMP[n].reshape(16, 8, 128) * step[None]).reshape(PLANE, 128)
            if it > 0:
                lam = LAM[n] + lam
            LAM[n] = lam
        if it == 0:
            U[1, rows(32), :] = U[1, rows(32), :] - LAM[1]
            U[1, rows(1), :] = U[1, rows(1), :] + LAM[0]
            for n, (t, s, sign) in ((3, (3, 7, -1.0)), (2, (0, 0, 1.0))):
                for c in range(4):
                    for h in range(4):
                        at = pl.ds(PLANE + h * 8 * PLANE + c * 32 + t * 8 + s, 8, stride=PLANE)
                        U[1, at, :] = U[1, at, :] + sign * LAM[n, pl.ds(c * 32 + h * 8, 8), :]
        else:
            corr_out[...] = own
            lamy_out[...] = LAM[3]
            for c in range(4):
                for t in range(4):
                    lamx_out[pl.ds(c * 32 + t, 8, stride=4), :] = LAM[1, pl.ds(c * 32 + t * 8, 8), :]
    for copy in sends:
        copy.wait_send()


def finish_kernel(wide, xpre, corr, lamx, lamy, vel, mx, my):
    step = pl.program_id(0)
    wx = (lax.broadcasted_iota(jnp.int32, (wide, 32, 128), 0) + step * wide).astype(F32) / 31.0
    wy = lax.broadcasted_iota(jnp.int32, (wide, 32, 128), 1).astype(F32) / 31.0
    for c in range(4):
        at = pl.ds(c * 128, 128)
        c0, c1, c2, c3 = (corr[n * 4 + c : n * 4 + c + 1, :][None] for n in range(4))
        e = (1.0 - wx) * ((1.0 - wy) * c0 + wy * c1) + wx * ((1.0 - wy) * c2 + wy * c3)
        part = xpre[c, pl.ds(pl.multiple_of(step * 32 * wide, 32 * wide), 32 * wide), :]
        vel[:, :, at] = part.reshape(wide, 32, 128) + e

    @pl.when(step == 0)
    def _():
        for c in range(4):
            at = pl.ds(c * 128, 128)
            mx[:, at] = lamx[pl.ds(c * 32, 32), :]
            my[:, :, at] = lamy[pl.ds(c * 32, 32), :].reshape(32, 1, 128)


def on_device(ni, nj, perm_class, class_drag, force, coarse_inverse, coarse_owner):
    hbm = pl.BlockSpec(memory_space=pl.ANY)
    vmem = pl.BlockSpec(memory_space=pltpu.VMEM)
    smem = pl.BlockSpec(memory_space=pltpu.SMEM)
    dma = pltpu.SemaphoreType.DMA
    xpre, corr, lamx, lamy = pl.pallas_call(
        functools.partial(kernel, ni, nj),
        out_shape=(
            pltpu.VMEM((4, 1024, 128), F32),
            pltpu.VMEM((16, 128), F32),
            pltpu.VMEM((128, 128), F32),
            pltpu.VMEM((128, 128), F32),
        ),
        in_specs=[hbm, smem, hbm, hbm, smem],
        out_specs=(vmem, vmem, vmem, vmem),
        scratch_shapes=[
            pltpu.VMEM((SWEEPS + 2, 34 * PLANE, 128), F32),
            pltpu.VMEM((34 * PLANE, 128), F32),
            pltpu.VMEM((32 * PLANE, 128), F32),
            pltpu.VMEM((4, 1024, 128), F32),
            pltpu.VMEM((4, 1024, 128), jnp.int32),
            pltpu.VMEM((16, 8, 128), F32),
            pltpu.VMEM((3, ni, nj, 8, 128), F32),
            pltpu.SMEM((ni * nj, ni * nj), F32),
            pltpu.VMEM((ITERS, 16, 128), F32),
            pltpu.VMEM((ITERS, nj, 16, 128), F32),
            pltpu.VMEM((ITERS, ni, 48, 128), F32),
            pltpu.VMEM((ITERS, ni, 48, 128), F32),
            pltpu.VMEM((ITERS, 4, PLANE, 128), F32),
            pltpu.VMEM((ITERS, 4, PLANE, 128), F32),
            pltpu.VMEM((ITERS, 1, 128), F32),
            pltpu.VMEM((ITERS, ni * nj, 128), F32),
            pltpu.VMEM((4, PLANE, 128), F32),
            pltpu.VMEM((4, PLANE, 128), F32),
            dma((8,)), dma,
            dma((ITERS, nj)), dma((ITERS, nj)),
            dma((ITERS, ni)), dma((ITERS, ni)),
            dma((ITERS, 4)), dma((ITERS, 4)),
            dma((ITERS,)), dma((ITERS,)),
        ],
        compiler_params=pltpu.CompilerParams(
            collective_id=0, has_side_effects=True, vmem_limit_bytes=56 * 2**20
        ),
        name="solve",
    )(perm_class.reshape(1024, 512), class_drag, force.reshape(1024, 512), coarse_inverse, coarse_owner)
    steps, wide = 4, 8
    velocity, mult_x, mult_y = pl.pallas_call(
        functools.partial(finish_kernel, wide),
        grid=(steps,),
        out_shape=(
            jax.ShapeDtypeStruct((32, 32, 512), F32),
            jax.ShapeDtypeStruct((32, 512), F32),
            jax.ShapeDtypeStruct((32, 1, 512), F32),
        ),
        in_specs=[vmem] * 4,
        out_specs=(
            pl.BlockSpec((wide, 32, 512), lambda n: (n, 0, 0)),
            pl.BlockSpec((32, 512), lambda n: (0, 0)),
            pl.BlockSpec((32, 1, 512), lambda n: (0, 0, 0)),
        ),
        compiler_params=pltpu.CompilerParams(vmem_limit_bytes=16 * 2**20),
        name="finish",
    )(xpre, corr, lamx, lamy)
    return velocity, mult_x[None], mult_y


def solution(mesh):
    return jax.shard_map(
        functools.partial(on_device, mesh.shape["gx"], mesh.shape["yz"]),
        mesh=mesh,
        in_specs=(P("gx", "yz", None), P(), P("gx", "yz", None), P(), P()),
        out_specs=(P("gx", "yz", None), P("gx", "yz", None), P("gx", "yz", None)),
        check_vma=False,
    )
```

```python
import functools

import jax
import jax.numpy as jnp
from jax import lax
from jax.experimental import pallas as pl
from jax.experimental.pallas import tpu as pltpu
from jax.sharding import PartitionSpec as P

CLASSES = 8
SWEEPS = 8
ITERS = 2
F32 = jnp.float32
MESH = pl.DeviceIdType.MESH
BF16 = jnp.bfloat16
PLANE = 128
UNROLL = 16


def rows(x):
    return pl.ds(pl.multiple_of(x * PLANE, PLANE), PLANE)


def tiles(value):
    return value.reshape(4, 4, 8, 128)


def beside_yz(cur):
    lane = lax.broadcasted_iota(jnp.int32, (4, 1, 8, 128), 3)
    sub = lax.broadcasted_iota(jnp.int32, (1, 4, 8, 128), 2)
    left = jnp.where(lane == 0, 0.0, pltpu.roll(cur[:, 3:4], 1, 3))
    right = jnp.where(lane == 127, 0.0, pltpu.roll(cur[:, 0:1], 127, 3))
    before = jnp.where(sub == 0, 0.0, pltpu.roll(cur[3:4], 1, 2))
    after = jnp.where(sub == 7, 0.0, pltpu.roll(cur[0:1], 7, 2))
    low = jnp.concatenate([before, cur[0:3]], axis=0)
    high = jnp.concatenate([cur[1:4], after], axis=0)
    nearer = jnp.concatenate([left, cur[:, 0:3]], axis=1)
    further = jnp.concatenate([cur[:, 1:4], right], axis=1)
    return (high + low) + (nearer + further)


def three(a):
    high = a.astype(BF16)
    rest = a - high.astype(F32)
    middle = rest.astype(BF16)
    return high, middle, (rest - middle.astype(F32)).astype(BF16)


def reorder(a, perm, back):
    dims = (((1,), (1 if back else 0,)), ((), ()))
    out = None
    for piece in three(a):
        term = lax.dot_general(piece, perm, dims, preferred_element_type=F32)
        out = term if out is None else out + term
    return out


def total_of(a):
    a = jnp.sum(jnp.sum(a, axis=0, keepdims=True), axis=1, keepdims=True)
    return jnp.broadcast_to(a, (8, 128))


def splat(a):
    return a[None, None]


def part(x, t):
    return pl.ds(pl.multiple_of(x * PLANE, PLANE) + t * 32, 32)


def quad(value):
    return value.reshape(4, 8, 128)


def sweep_pass(k, first, a, b, U, W):
    lane = lax.broadcasted_iota(jnp.int32, (1, 8, 128), 2)
    sub = lax.broadcasted_iota(jnp.int32, (4, 8, 128), 1)

    def fresh(x, t):
        u = quad(W[part(x, t), :]) - a[None] * quad(U[k, part(x, t), :])
        u = u - b[None] * quad(U[k - 1, part(x, t), :])
        U[k + 1, part(x, t), :] = u.reshape(32, 128)
        return u

    def step(x, acc):
        uu, uw = acc
        for t in range(4):
            if first:
                above = quad(U[k + 1, part(x + 2, t), :])
            else:
                above = fresh(x + 2, t)
            cur = quad(U[k + 1, part(x + 1, t), :])
            below = quad(U[k + 1, part(x, t), :])
            low = quad(U[k + 1, part(x + 1, (t + 3) % 4), :])
            high = quad(U[k + 1, part(x + 1, (t + 1) % 4), :])
            if t == 0:
                low = jnp.where(sub == 0, 0.0, pltpu.roll(low, 1, 1))
            if t == 3:
                high = jnp.where(sub == 7, 0.0, pltpu.roll(high, 7, 1))
            left = jnp.where(lane == 0, 0.0, pltpu.roll(cur[3:4], 1, 2))
            right = jnp.where(lane == 127, 0.0, pltpu.roll(cur[0:1], 127, 2))
            left = jnp.concatenate([left, cur[0:3]], axis=0)
            right = jnp.concatenate([cur[1:4], right], axis=0)
            beside = ((above + below) + (high + low)) + (left + right)
            w = quad(U[0, part(x + 1, t), :]) * cur - beside
            W[part(x + 1, t), :] = w.reshape(32, 128)
            uu, uw = uu + cur * cur, uw + cur * w
        return uu, uw

    if not first:
        for t in range(4):
            fresh(1, t)
    zero = jnp.zeros((4, 8, 128), F32)
    uu, uw = lax.fori_loop(0, 32, step, (zero, zero), unroll=UNROLL)
    g = total_of(jnp.sum(uu, axis=0))
    return g, total_of(jnp.sum(uw, axis=0)) / g


def y_weights(width):
    t = lax.broadcasted_iota(jnp.int32, (4, 1, 8, 128), 0)
    s = lax.broadcasted_iota(jnp.int32, (4, 1, 8, 128), 2)
    return (4 * s + t).astype(F32) / (width - 1)


def kernel(
    ni, nj, perm, drag, force, cinv, owner,
    xpre, corr_out, lamx_out, lamy_out,
    U, W, X, fst, pst, cf, wsp, cinv_s, cbuf, G, PB, R, FS, FR, TS, TR, LAM, JMP, PM, CC,
    in_sem, ci_sem, sg, rg, sr, rr, sf, rf, st, rt,
):
    i = lax.axis_index("gx")
    j = lax.axis_index("yz")
    zero = jnp.zeros((8, 128), F32)
    plane0 = jnp.zeros((PLANE, 128), F32)

    barrier = pltpu.get_barrier_semaphore()

    def greet(n, carry):
        dev = {"gx": lax.rem(i + n // nj, ni), "yz": lax.rem(j + n % nj, nj)}
        pl.semaphore_signal(barrier, inc=1, device_id=dev, device_id_type=MESH)
        return carry

    lax.fori_loop(1, ni * nj, greet, 0)

    wide = 8

    def chunk_copies(n):
        at = pl.ds(pl.multiple_of(n * wide * 32, wide * 32), wide * 32)
        out = []
        for c in range(4):
            cols = pl.ds(c * 128, 128)
            out.append(pltpu.make_async_copy(perm.at[at, cols], pst.at[c, at], in_sem.at[n, c]))
            out.append(pltpu.make_async_copy(force.at[at, cols], fst.at[c, at], in_sem.at[n, 4 + c]))
        return out

    for n in range(32 // wide):
        for copy in chunk_copies(n):
            copy.start()
    weights_copy = pltpu.make_async_copy(cinv, cinv_s, ci_sem)
    weights_copy.start()

    for k in range(SWEEPS + 2):
        U[k, rows(0), :] = plane0
        U[k, rows(33), :] = plane0
    W[rows(33), :] = plane0

    for n in range(4):
        zin = lax.broadcasted_iota(jnp.int32, (512, 128), 0)
        lane = lax.broadcasted_iota(jnp.int32, (512, 128), 1)
        PM[:, pl.ds(n * 128, 128)] = jnp.where(zin == 4 * lane + n, 1.0, 0.0).astype(BF16)

    level = [6.0 + drag[c] for c in range(CLASSES)]

    def stage(n, carry):
        for copy in chunk_copies(n):
            copy.wait()
        perm_matrix = PM[...]

        def gathered(ref):
            out = []
            for x in range(wide):
                for t in range(4):
                    at = pl.ds(n * wide * 32 + x * 32 + t, 8, stride=4)
                    out.append(jnp.concatenate([ref[c, at, :] for c in range(4)], axis=1))
            return jnp.concatenate(out, axis=0)

        classes = gathered(pst).astype(F32).astype(BF16)
        classes = jnp.dot(classes, perm_matrix, preferred_element_type=F32)
        field = reorder(gathered(fst), perm_matrix, False)
        for x in range(wide):
            for t in range(4):
                for k in range(4):
                    r, l = slice(x * 32 + t * 8, x * 32 + t * 8 + 8), slice(k * 128, k * 128 + 128)
                    at = pl.ds(pl.multiple_of((n * wide + x + 1) * PLANE, PLANE) + t * 32 + k * 8, 8)
                    cls = classes[r, l].astype(jnp.int32)
                    b0, b1, b2 = (cls & 1) != 0, (cls & 2) != 0, (cls & 4) != 0
                    pairs = [jnp.where(b0, level[m + 1], level[m]) for m in range(0, 8, 2)]
                    quads = [jnp.where(b1, pairs[1], pairs[0]), jnp.where(b1, pairs[3], pairs[2])]
                    U[0, at, :] = jnp.where(b2, quads[1], quads[0])
                    U[1, at, :] = field[r, l]
        return carry

    lax.fori_loop(0, 32 // wide, stage, 0)

    has_right = (i < ni - 1).astype(F32)
    has_left = (i > 0).astype(F32)
    has_upper = (j < nj - 1).astype(F32)
    has_lower = (j > 0).astype(F32)
    wy = y_weights(32)
    wx8 = lax.broadcasted_iota(jnp.int32, (32, 128), 0).astype(F32) / 31.0
    right, left = {"gx": lax.rem(i + 1, ni)}, {"gx": lax.rem(i + ni - 1, ni)}
    upper, lower = {"yz": lax.rem(j + 1, nj)}, {"yz": lax.rem(j + nj - 1, nj)}
    sends = []

    def remote(src, dst, ssem, rsem, dev):
        return pltpu.make_async_remote_copy(
            src_ref=src, dst_ref=dst, send_sem=ssem, recv_sem=rsem, device_id=dev, device_id_type=MESH
        )

    for it in range(ITERS):
        g, a = sweep_pass(0, True, zero, zero, U, W)
        cf[0], cf[8] = a, zero

        def body(k, carry):
            g, a, b = carry
            gn, an = sweep_pass(k, False, a, b, U, W)
            bn = gn / g
            cf[k] = an
            cf[8 + k] = bn
            return gn, an, bn

        g, a, b = lax.fori_loop(1, SWEEPS, body, (g, a, zero))

        av = [cf[k] for k in range(SWEEPS)]
        bv = [cf[8 + k] for k in range(SWEEPS)]
        inv, z = [1.0 / av[0]], [jnp.ones((8, 128), F32)]
        for k in range(1, SWEEPS):
            z.append(-z[k - 1] * inv[k - 1])
            inv.append(1.0 / (av[k] - bv[k] * inv[k - 1]))
        y = [None] * SWEEPS
        y[SWEEPS - 1] = z[SWEEPS - 1] * inv[SWEEPS - 1]
        for k in range(SWEEPS - 2, -1, -1):
            y[k] = (z[k] - bv[k + 1] * y[k + 1]) * inv[k]

        for n, x in ((0, 0), (1, 31)):
            for m, (t, r) in enumerate(((0, 0), (3, 7))):
                for c in range(4):
                    at = t * 32 + c * 8
                    f = None if it == 0 else X[pl.ds(x * PLANE + at, 8), :]
                    for k in range(SWEEPS):
                        term = y[k] * U[k + 1, pl.ds((x + 1) * PLANE + at, 8), :]
                        f = term if f is None else f + term
                    cbuf[it, pl.ds((2 * n + m) * 4 + c, 1), :] = f[r : r + 1, :]
        G[it, j] = cbuf[it]
        if it == 0:
            pl.semaphore_wait(barrier, ni * nj - 1)
        gather = []
        for d in range(1, nj):
            dev = {"yz": lax.rem(j + d, nj)}
            copy = remote(cbuf.at[it], G.at[it, j], sg.at[it, d], rg.at[it, d], dev)
            copy.start()
            sends.append(copy)
            came = G.at[it, lax.rem(j + nj - d, nj)]
            gather.append(remote(cbuf.at[it], came, sg.at[it, d], rg.at[it, d], dev))
        def gather_x(x, carry):
            f = None if it == 0 else tiles(X[rows(x), :])
            for k in range(SWEEPS):
                term = splat(y[k]) * tiles(U[k + 1, rows(x + 1), :])
                f = term if f is None else f + term
            for c in range(4):
                FS[it, 2, pl.ds(c * 32 + x, 1), :] = f[0, c, 0:1, :]
                FS[it, 3, pl.ds(c * 32 + x, 1), :] = f[3, c, 7:8, :]
            if it == 0:
                X[rows(x), :] = f.reshape(PLANE, 128)
                u = tiles(W[rows(x + 1), :]) - splat(a) * tiles(U[8, rows(x + 1), :])
                u = u - splat(b) * tiles(U[7, rows(x + 1), :])
                U[1, rows(x + 1), :] = (splat(-y[7]) * u).reshape(PLANE, 128)
            else:
                X[rows(x), :] = f.reshape(PLANE, 128)
            return carry

        lax.fori_loop(0, 32, gather_x, 0, unroll=4)
        FS[it, 0] = X[rows(0), :]
        FS[it, 1] = X[rows(31), :]
        faces = []
        for src, dst, dev in ((1, 0, right), (0, 1, left), (3, 2, upper), (2, 3, lower)):
            copy = remote(FS.at[it, src], FR.at[it, dst], sf.at[it, dst], rf.at[it, dst], dev)
            copy.start()
            faces.append(copy)
        sends.extend(faces)
        if it == 0:
            weights_copy.wait()
            for n in range(3):
                jn = lax.rem(j + nj - 1 + n, nj)
                for sx in range(ni):

                    def fill(ty, carry, n=n, sx=sx, at=owner[sx * nj + jn]):
                        wsp[n, sx, ty] = jnp.full((8, 128), cinv_s[at, owner[i * nj + ty]], F32)
                        return carry

                    lax.fori_loop(0, nj, fill, 0, unroll=4)

        else:

            def restore(n, carry):
                field = []
                for x in range(wide):
                    for t in range(4):
                        at = pl.multiple_of((n * wide + x) * PLANE, PLANE) + t * 32
                        field.append(jnp.concatenate([X[pl.ds(at + k * 8, 8), :] for k in range(4)], axis=1))
                field = reorder(jnp.concatenate(field, axis=0), PM[...], True)
                for x in range(wide):
                    for t in range(4):
                        for c in range(4):
                            at = pl.ds((n * wide + x) * 32 + t, 8, stride=4)
                            r = x * 32 + t * 8
                            xpre[c, at, :] = field[r : r + 8, c * 128 : c * 128 + 128]
                return carry

            lax.fori_loop(0, 32 // wide, restore, 0)

        for copy in gather:
            copy.wait_recv()
        sub = lax.broadcasted_iota(jnp.int32, (8, 128), 0) < 4
        for sx in range(ni):

            def term(ty, acc, sx=sx):
                lo, hi, down, up = acc
                g01, g23 = G[it, ty, 0:8, :], G[it, ty, 8:16, :]
                g13 = jnp.where(sub, pltpu.roll(g01, 4, 0), g23)
                g02 = jnp.where(sub, g01, pltpu.roll(g23, 4, 0))
                w = wsp[1, sx, ty]
                return lo + w * g01, hi + w * g23, down + wsp[0, sx, ty] * g13, up + wsp[2, sx, ty] * g02

            lo, hi, down, up = lax.fori_loop(0, nj, term, (zero,) * 4, unroll=8)
            PB[it, sx, 0:8, :] = lo
            PB[it, sx, 8:16, :] = hi
            PB[it, (sx + 1) % ni, 16:24, :] = hi
            PB[it, (sx - 1) % ni, 24:32, :] = lo
            PB[it, sx, 32:40, :] = down
            PB[it, sx, 40:48, :] = up
        R[it, i] = PB[it, i]
        parts = []
        for d in range(1, ni):
            to = lax.rem(i + d, ni)
            copy = remote(PB.at[it, to], R.at[it, i], sr.at[it, d], rr.at[it, d], {"gx": to})
            copy.start()
            sends.append(copy)
            came = R.at[it, lax.rem(i + ni - d, ni)]
            parts.append(remote(PB.at[it, to], came, sr.at[it, d], rr.at[it, d], {"gx": to}))
        for copy in faces:
            copy.wait_recv()
        for copy in parts:
            copy.wait_recv()
        sums = R[it, 0]
        for n in range(1, ni):
            sums = sums + R[it, n]
        own = sums[0:16]
        other = [sums[16 + 8 * n : 24 + 8 * n] for n in range(4)]

        def row(block, c, chunk):
            return block[c * 4 + chunk : c * 4 + chunk + 1, :]

        def along_y(block, c0, c1):
            out = []
            for chunk in range(4):
                p = row(block, c0, chunk)[None, None]
                q = row(block, c1, chunk)[None, None]
                out.append((1.0 - wy) * p + wy * q)
            return jnp.concatenate(out, axis=1)

        def along_x(block, c0, c1):
            out = []
            for chunk in range(4):
                out.append((1.0 - wx8) * row(block, c0, chunk) + wx8 * row(block, c1, chunk))
            return jnp.concatenate(out, axis=0)

        sq = zero
        for n, (fun, c0, c1, sign, has) in enumerate((
            (along_y, 0, 1, -1.0, has_left),
            (along_y, 2, 3, 1.0, has_right),
            (along_x, 0, 2, -1.0, has_lower),
            (along_x, 1, 3, 1.0, has_upper),
        )):
            mine = FS[it, n] + fun(own, c0, c1).reshape(PLANE, 128)
            theirs = FR[it, n] + fun(other[n], 0, 1).reshape(PLANE, 128)
            jump = (mine - theirs) * (sign * has)
            JMP[n] = jump
            if sign > 0:
                sq = sq + jnp.sum((jump * jump).reshape(16, 8, 128), axis=0)
        me = i * nj + j
        row_sum = jnp.sum(sq, axis=0, keepdims=True)
        TS[it] = row_sum
        TR[it, pl.ds(me, 1), :] = row_sum

        def tell(n, carry):
            dev = {"gx": lax.rem(i + n // nj, ni), "yz": lax.rem(j + n % nj, nj)}
            remote(TS.at[it], TR.at[it, pl.ds(me, 1)], st.at[it], rt.at[it], dev).start()
            return carry

        lax.fori_loop(1, ni * nj, tell, 0)
        all_but_one = TR.at[it, pl.ds(0, ni * nj - 1)]
        told = remote(all_but_one, all_but_one, st.at[it], rt.at[it], right)
        sends.append(told)
        if it == 0:
            start = along_y(own, 0, 1)
            slope = along_y(own, 2, 3) - start
            m_start = beside_yz(start)
            m_slope = beside_yz(slope)

            def corrected(x, carry):
                wx = x.astype(F32) / 31.0
                e = start + wx * slope
                beside = m_start + wx * m_slope + 2.0 * e
                diag = tiles(U[0, rows(x + 1), :])
                U[1, rows(x + 1), :] = (
                    tiles(U[1, rows(x + 1), :]) - (diag * e - beside)
                ).reshape(PLANE, 128)
                X[rows(x), :] = (tiles(X[rows(x), :]) + e).reshape(PLANE, 128)
                return carry

            lax.fori_loop(0, 32, corrected, 0)
            U[1, rows(1), :] = U[1, rows(1), :] - (start - slope / 31.0).reshape(PLANE, 128)
            U[1, rows(32), :] = U[1, rows(32), :] - (start + slope * (32.0 / 31.0)).reshape(PLANE, 128)
        if it == ITERS - 1:
            CC[...] = jnp.zeros((8, 512), F32)
            for c in range(4):
                for k in range(4):
                    CC[pl.ds(c, 1), pl.ds(k * 128, 128)] = row(own, c, k)
            corr_out[...] = reorder(CC[...], PM[...], True)
        told.wait_recv()
        total = jnp.sum(TR[it].reshape(ni * nj // 8, 8, 128), axis=0)
        count = (ni - 1) * nj * 32 * 512 + ni * 32 * (nj - 1) * 512
        step = 0.5 / jnp.sqrt(total_of(total) / float(count) + 1e-6)
        for n in range(4):
            lam = (JMP[n].reshape(16, 8, 128) * step[None]).reshape(PLANE, 128)
            if it > 0:
                lam = LAM[n] + lam
            LAM[n] = lam
        if it == 0:
            U[1, rows(32), :] = U[1, rows(32), :] - LAM[1]
            U[1, rows(1), :] = U[1, rows(1), :] + LAM[0]
            for n, (t, s, sign) in ((3, (3, 7, -1.0)), (2, (0, 0, 1.0))):
                for c in range(4):
                    for h in range(4):
                        at = pl.ds(PLANE + h * 8 * PLANE + t * 32 + c * 8 + s, 8, stride=PLANE)
                        U[1, at, :] = U[1, at, :] + sign * LAM[n, pl.ds(c * 32 + h * 8, 8), :]
        else:
            lam_x = LAM[1].reshape(4, 4, 8, 128)
            lam_x = jnp.concatenate([lam_x[:, k].reshape(32, 128) for k in range(4)], axis=1)
            lam_y = jnp.concatenate([LAM[3, pl.ds(k * 32, 32), :] for k in range(4)], axis=1)
            both = reorder(jnp.concatenate([lam_x, lam_y], axis=0), PM[...], True)
            for c in range(4):
                lamy_out[pl.ds(c * 32, 32), :] = both[32:64, c * 128 : c * 128 + 128]
                for t in range(4):
                    part_of = both[t * 8 : t * 8 + 8, c * 128 : c * 128 + 128]
                    lamx_out[pl.ds(c * 32 + t, 8, stride=4), :] = part_of
    for copy in sends:
        copy.wait_send()


def finish_kernel(wide, xpre, corr, lamx, lamy, vel, mx, my):
    step = pl.program_id(0)
    wx = (lax.broadcasted_iota(jnp.int32, (wide, 32, 128), 0) + step * wide).astype(F32) / 31.0
    wy = lax.broadcasted_iota(jnp.int32, (wide, 32, 128), 1).astype(F32) / 31.0
    for c in range(4):
        at = pl.ds(c * 128, 128)
        c0, c1, c2, c3 = (corr[n : n + 1, at][None] for n in range(4))
        e = (1.0 - wx) * ((1.0 - wy) * c0 + wy * c1) + wx * ((1.0 - wy) * c2 + wy * c3)
        part = xpre[c, pl.ds(pl.multiple_of(step * 32 * wide, 32 * wide), 32 * wide), :]
        vel[:, :, at] = part.reshape(wide, 32, 128) + e

    @pl.when(step == 0)
    def _():
        for c in range(4):
            at = pl.ds(c * 128, 128)
            mx[:, at] = lamx[pl.ds(c * 32, 32), :]
            my[:, :, at] = lamy[pl.ds(c * 32, 32), :].reshape(32, 1, 128)


def on_device(ni, nj, perm_class, class_drag, force, coarse_inverse, coarse_owner):
    hbm = pl.BlockSpec(memory_space=pl.ANY)
    vmem = pl.BlockSpec(memory_space=pltpu.VMEM)
    smem = pl.BlockSpec(memory_space=pltpu.SMEM)
    dma = pltpu.SemaphoreType.DMA
    xpre, corr, lamx, lamy = pl.pallas_call(
        functools.partial(kernel, ni, nj),
        out_shape=(
            pltpu.VMEM((4, 1024, 128), F32),
            pltpu.VMEM((8, 512), F32),
            pltpu.VMEM((128, 128), F32),
            pltpu.VMEM((128, 128), F32),
        ),
        in_specs=[hbm, smem, hbm, hbm, smem],
        out_specs=(vmem, vmem, vmem, vmem),
        scratch_shapes=[
            pltpu.VMEM((SWEEPS + 2, 34 * PLANE, 128), F32),
            pltpu.VMEM((34 * PLANE, 128), F32),
            pltpu.VMEM((32 * PLANE, 128), F32),
            pltpu.VMEM((4, 1024, 128), F32),
            pltpu.VMEM((4, 1024, 128), jnp.int32),
            pltpu.VMEM((16, 8, 128), F32),
            pltpu.VMEM((3, ni, nj, 8, 128), F32),
            pltpu.SMEM((ni * nj, ni * nj), F32),
            pltpu.VMEM((ITERS, 16, 128), F32),
            pltpu.VMEM((ITERS, nj, 16, 128), F32),
            pltpu.VMEM((ITERS, ni, 48, 128), F32),
            pltpu.VMEM((ITERS, ni, 48, 128), F32),
            pltpu.VMEM((ITERS, 4, PLANE, 128), F32),
            pltpu.VMEM((ITERS, 4, PLANE, 128), F32),
            pltpu.VMEM((ITERS, 1, 128), F32),
            pltpu.VMEM((ITERS, ni * nj, 128), F32),
            pltpu.VMEM((4, PLANE, 128), F32),
            pltpu.VMEM((4, PLANE, 128), F32),
            pltpu.VMEM((512, 512), BF16),
            pltpu.VMEM((8, 512), F32),
            dma((4, 8)), dma,
            dma((ITERS, nj)), dma((ITERS, nj)),
            dma((ITERS, ni)), dma((ITERS, ni)),
            dma((ITERS, 4)), dma((ITERS, 4)),
            dma((ITERS,)), dma((ITERS,)),
        ],
        compiler_params=pltpu.CompilerParams(
            collective_id=0, has_side_effects=True, vmem_limit_bytes=56 * 2**20
        ),
        name="solve",
    )(perm_class.reshape(1024, 512), class_drag, force.reshape(1024, 512), coarse_inverse, coarse_owner)
    steps, wide = 4, 8
    velocity, mult_x, mult_y = pl.pallas_call(
        functools.partial(finish_kernel, wide),
        grid=(steps,),
        out_shape=(
            jax.ShapeDtypeStruct((32, 32, 512), F32),
            jax.ShapeDtypeStruct((32, 512), F32),
            jax.ShapeDtypeStruct((32, 1, 512), F32),
        ),
        in_specs=[vmem] * 4,
        out_specs=(
            pl.BlockSpec((wide, 32, 512), lambda n: (n, 0, 0)),
            pl.BlockSpec((32, 512), lambda n: (0, 0)),
            pl.BlockSpec((32, 1, 512), lambda n: (0, 0, 0)),
        ),
        compiler_params=pltpu.CompilerParams(vmem_limit_bytes=16 * 2**20),
        name="finish",
    )(xpre, corr, lamx, lamy)
    return velocity, mult_x[None], mult_y


def solution(mesh):
    return jax.shard_map(
        functools.partial(on_device, mesh.shape["gx"], mesh.shape["yz"]),
        mesh=mesh,
        in_specs=(P("gx", "yz", None), P(), P("gx", "yz", None), P(), P()),
        out_specs=(P("gx", "yz", None), P("gx", "yz", None), P("gx", "yz", None)),
        check_vma=False,
    )
```

```python
import functools

import jax
import jax.numpy as jnp
from jax import lax
from jax.experimental import pallas as pl
from jax.experimental.pallas import tpu as pltpu
from jax.sharding import PartitionSpec as P

CLASSES = 8
SWEEPS = 8
ITERS = 2
F32 = jnp.float32
MESH = pl.DeviceIdType.MESH
BF16 = jnp.bfloat16
PLANE = 128
UNROLL = 32


def rows(x):
    return pl.ds(pl.multiple_of(x * PLANE, PLANE), PLANE)


def tiles(value):
    return value.reshape(4, 4, 8, 128)


def beside_yz(cur):
    lane = lax.broadcasted_iota(jnp.int32, (4, 1, 8, 128), 3)
    sub = lax.broadcasted_iota(jnp.int32, (1, 4, 8, 128), 2)
    left = jnp.where(lane == 0, 0.0, pltpu.roll(cur[:, 3:4], 1, 3))
    right = jnp.where(lane == 127, 0.0, pltpu.roll(cur[:, 0:1], 127, 3))
    before = jnp.where(sub == 0, 0.0, pltpu.roll(cur[3:4], 1, 2))
    after = jnp.where(sub == 7, 0.0, pltpu.roll(cur[0:1], 7, 2))
    low = jnp.concatenate([before, cur[0:3]], axis=0)
    high = jnp.concatenate([cur[1:4], after], axis=0)
    nearer = jnp.concatenate([left, cur[:, 0:3]], axis=1)
    further = jnp.concatenate([cur[:, 1:4], right], axis=1)
    return (high + low) + (nearer + further)


def three(a):
    high = a.astype(BF16)
    rest = a - high.astype(F32)
    middle = rest.astype(BF16)
    return high, middle, (rest - middle.astype(F32)).astype(BF16)


def reorder(a, perm, back):
    dims = (((1,), (1 if back else 0,)), ((), ()))
    out = None
    for piece in three(a):
        term = lax.dot_general(piece, perm, dims, preferred_element_type=F32)
        out = term if out is None else out + term
    return out


def total_of(a):
    a = jnp.sum(jnp.sum(a, axis=0, keepdims=True), axis=1, keepdims=True)
    return jnp.broadcast_to(a, (8, 128))


def splat(a):
    return a[None, None]


def part(x, t):
    return pl.ds(pl.multiple_of(x * PLANE, PLANE) + t * 32, 32)


def quad(value):
    return value.reshape(4, 8, 128)


def sweep_pass(k, first, a, b, U, W):
    lane = lax.broadcasted_iota(jnp.int32, (1, 8, 128), 2)
    sub = lax.broadcasted_iota(jnp.int32, (4, 8, 128), 1)

    def fresh(x, t):
        u = quad(W[part(x, t), :]) - a[None] * quad(U[k, part(x, t), :])
        u = u - b[None] * quad(U[k - 1, part(x, t), :])
        U[k + 1, part(x, t), :] = u.reshape(32, 128)
        return u

    def step(x, acc):
        uu, uw = acc
        for t in range(4):
            if first:
                above = quad(U[k + 1, part(x + 2, t), :])
            else:
                above = fresh(x + 2, t)
            cur = quad(U[k + 1, part(x + 1, t), :])
            below = quad(U[k + 1, part(x, t), :])
            low = quad(U[k + 1, part(x + 1, (t + 3) % 4), :])
            high = quad(U[k + 1, part(x + 1, (t + 1) % 4), :])
            if t == 0:
                low = jnp.where(sub == 0, 0.0, pltpu.roll(low, 1, 1))
            if t == 3:
                high = jnp.where(sub == 7, 0.0, pltpu.roll(high, 7, 1))
            left = jnp.where(lane == 0, 0.0, pltpu.roll(cur[3:4], 1, 2))
            right = jnp.where(lane == 127, 0.0, pltpu.roll(cur[0:1], 127, 2))
            left = jnp.concatenate([left, cur[0:3]], axis=0)
            right = jnp.concatenate([cur[1:4], right], axis=0)
            beside = ((above + below) + (high + low)) + (left + right)
            w = quad(U[0, part(x + 1, t), :]) * cur - beside
            W[part(x + 1, t), :] = w.reshape(32, 128)
            uu, uw = uu + cur * cur, uw + cur * w
        return uu, uw

    if not first:
        for t in range(4):
            fresh(1, t)
    zero = jnp.zeros((4, 8, 128), F32)
    uu, uw = lax.fori_loop(0, 32, step, (zero, zero), unroll=UNROLL)
    g = total_of(jnp.sum(uu, axis=0))
    return g, total_of(jnp.sum(uw, axis=0)) / g


def y_weights(width):
    t = lax.broadcasted_iota(jnp.int32, (4, 1, 8, 128), 0)
    s = lax.broadcasted_iota(jnp.int32, (4, 1, 8, 128), 2)
    return (4 * s + t).astype(F32) / (width - 1)


def kernel(
    ni, nj, perm, drag, force, cinv, owner,
    xpre, lamx_out, lamy_out,
    U, W, X, fst, pst, cf, wsp, cinv_s, cbuf, G, PB, R, FS, FR, TS, TR, LAM, JMP, PM, CC,
    in_sem, ci_sem, sg, rg, sr, rr, sf, rf, st, rt,
):
    i = lax.axis_index("gx")
    j = lax.axis_index("yz")
    zero = jnp.zeros((8, 128), F32)
    plane0 = jnp.zeros((PLANE, 128), F32)

    barrier = pltpu.get_barrier_semaphore()

    def greet(n, carry):
        dev = {"gx": lax.rem(i + n // nj, ni), "yz": lax.rem(j + n % nj, nj)}
        pl.semaphore_signal(barrier, inc=1, device_id=dev, device_id_type=MESH)
        return carry

    lax.fori_loop(1, ni * nj, greet, 0)

    wide = 8

    def chunk_copies(n):
        at = pl.ds(pl.multiple_of(n * wide * 32, wide * 32), wide * 32)
        out = []
        for c in range(4):
            cols = pl.ds(c * 128, 128)
            out.append(pltpu.make_async_copy(perm.at[at, cols], pst.at[c, at], in_sem.at[n, c]))
            out.append(pltpu.make_async_copy(force.at[at, cols], fst.at[c, at], in_sem.at[n, 4 + c]))
        return out

    for n in range(32 // wide):
        for copy in chunk_copies(n):
            copy.start()
    weights_copy = pltpu.make_async_copy(cinv, cinv_s, ci_sem)
    weights_copy.start()

    for k in range(SWEEPS + 2):
        U[k, rows(0), :] = plane0
        U[k, rows(33), :] = plane0
    W[rows(33), :] = plane0

    for n in range(4):
        zin = lax.broadcasted_iota(jnp.int32, (512, 128), 0)
        lane = lax.broadcasted_iota(jnp.int32, (512, 128), 1)
        PM[:, pl.ds(n * 128, 128)] = jnp.where(zin == 4 * lane + n, 1.0, 0.0).astype(BF16)

    lane8 = lax.broadcasted_iota(jnp.int32, (8, 128), 1)
    level = zero
    for c in range(CLASSES):
        level = jnp.where(lane8 == c, 6.0 + drag[c], level)

    def stage(n, carry):
        for copy in chunk_copies(n):
            copy.wait()
        perm_matrix = PM[...]

        def gathered(ref):
            out = []
            for x in range(wide):
                for t in range(4):
                    at = pl.ds(n * wide * 32 + x * 32 + t, 8, stride=4)
                    out.append(jnp.concatenate([ref[c, at, :] for c in range(4)], axis=1))
            return jnp.concatenate(out, axis=0)

        classes = gathered(pst).astype(F32).astype(BF16)
        classes = jnp.dot(classes, perm_matrix, preferred_element_type=F32)
        field = reorder(gathered(fst), perm_matrix, False)
        for x in range(wide):
            for t in range(4):
                for k in range(4):
                    r, l = slice(x * 32 + t * 8, x * 32 + t * 8 + 8), slice(k * 128, k * 128 + 128)
                    at = pl.ds(pl.multiple_of((n * wide + x + 1) * PLANE, PLANE) + t * 32 + k * 8, 8)
                    cls = classes[r, l].astype(jnp.int32)
                    U[0, at, :] = jnp.take_along_axis(level, cls, axis=1, mode="promise_in_bounds")
                    U[1, at, :] = field[r, l]
        return carry

    lax.fori_loop(0, 32 // wide, stage, 0)

    has_right = (i < ni - 1).astype(F32)
    has_left = (i > 0).astype(F32)
    has_upper = (j < nj - 1).astype(F32)
    has_lower = (j > 0).astype(F32)
    wy = y_weights(32)
    wx8 = lax.broadcasted_iota(jnp.int32, (32, 128), 0).astype(F32) / 31.0
    right, left = {"gx": lax.rem(i + 1, ni)}, {"gx": lax.rem(i + ni - 1, ni)}
    upper, lower = {"yz": lax.rem(j + 1, nj)}, {"yz": lax.rem(j + nj - 1, nj)}
    ring = (2, 1, 3, 0)
    gx_of = [lax.rem(i // 2 + ax, ni // 2) * 2 + lax.rem(i % 2 + core, 2) for ax in ring[-ni // 2 :] for core in (1, 0)]
    yz_of = [lax.rem(j // 4 + az, nj // 4) * 4 + lax.rem(j % 4 + ay, 4) for az in ring[-nj // 4 :] for ay in ring]
    far = []
    for p in range(ni):
        for q in range(nj):
            hops = sum((2, 1, 1, 0)[n] for n in (p // 2, q // 4, q % 4))
            far.append((-hops, p, q))
    everyone = [{"gx": gx_of[p], "yz": yz_of[q]} for _, p, q in sorted(far)[:-1] if (p, q) != (ni - 1, nj - 1)]
    sends = []

    def remote(src, dst, ssem, rsem, dev):
        return pltpu.make_async_remote_copy(
            src_ref=src, dst_ref=dst, send_sem=ssem, recv_sem=rsem, device_id=dev, device_id_type=MESH
        )

    for it in range(ITERS):
        g, a = sweep_pass(0, True, zero, zero, U, W)
        cf[0], cf[8] = a, zero

        def body(k, carry):
            g, a, b = carry
            gn, an = sweep_pass(k, False, a, b, U, W)
            bn = gn / g
            cf[k] = an
            cf[8 + k] = bn
            return gn, an, bn

        g, a, b = lax.fori_loop(1, SWEEPS, body, (g, a, zero))

        av = [cf[k] for k in range(SWEEPS)]
        bv = [cf[8 + k] for k in range(SWEEPS)]
        inv, z = [1.0 / av[0]], [jnp.ones((8, 128), F32)]
        for k in range(1, SWEEPS):
            z.append(-z[k - 1] * inv[k - 1])
            inv.append(1.0 / (av[k] - bv[k] * inv[k - 1]))
        y = [None] * SWEEPS
        y[SWEEPS - 1] = z[SWEEPS - 1] * inv[SWEEPS - 1]
        for k in range(SWEEPS - 2, -1, -1):
            y[k] = (z[k] - bv[k + 1] * y[k + 1]) * inv[k]

        for n, x in ((0, 0), (1, 31)):
            for m, (t, r) in enumerate(((0, 0), (3, 7))):
                for c in range(4):
                    at = t * 32 + c * 8
                    f = None if it == 0 else X[pl.ds(x * PLANE + at, 8), :]
                    for k in range(SWEEPS):
                        term = y[k] * U[k + 1, pl.ds((x + 1) * PLANE + at, 8), :]
                        f = term if f is None else f + term
                    cbuf[it, pl.ds((2 * n + m) * 4 + c, 1), :] = f[r : r + 1, :]
        G[it, j] = cbuf[it]
        if it == 0:
            pl.semaphore_wait(barrier, ni * nj - 1)
        gather = []
        for d in sorted(range(1, nj), key=lambda d: -abs((d + 2) % 4 - 2) - abs((d // 4 + 2) % 4 - 2)):
            dev = {"yz": lax.rem(j + d, nj)}
            copy = remote(cbuf.at[it], G.at[it, j], sg.at[it, d], rg.at[it, d], dev)
            copy.start()
            sends.append(copy)
            came = G.at[it, lax.rem(j + nj - d, nj)]
            gather.append(remote(cbuf.at[it], came, sg.at[it, d], rg.at[it, d], dev))
        def gather_x(x, carry):
            f = None if it == 0 else tiles(X[rows(x), :])
            for k in range(SWEEPS):
                term = splat(y[k]) * tiles(U[k + 1, rows(x + 1), :])
                f = term if f is None else f + term
            for c in range(4):
                FS[it, 2, pl.ds(c * 32 + x, 1), :] = f[0, c, 0:1, :]
                FS[it, 3, pl.ds(c * 32 + x, 1), :] = f[3, c, 7:8, :]
            if it == 0:
                X[rows(x), :] = f.reshape(PLANE, 128)
                u = tiles(W[rows(x + 1), :]) - splat(a) * tiles(U[8, rows(x + 1), :])
                u = u - splat(b) * tiles(U[7, rows(x + 1), :])
                U[1, rows(x + 1), :] = (splat(-y[7]) * u).reshape(PLANE, 128)
            else:
                X[rows(x), :] = f.reshape(PLANE, 128)
            return carry

        lax.fori_loop(0, 32, gather_x, 0, unroll=4)
        FS[it, 0] = X[rows(0), :]
        FS[it, 1] = X[rows(31), :]
        faces = []
        for src, dst, dev in ((1, 0, right), (0, 1, left), (3, 2, upper), (2, 3, lower)):
            copy = remote(FS.at[it, src], FR.at[it, dst], sf.at[it, dst], rf.at[it, dst], dev)
            copy.start()
            faces.append(copy)
        sends.extend(faces)
        if it == 0:
            weights_copy.wait()
            for n in range(3):
                jn = lax.rem(j + nj - 1 + n, nj)
                for sx in range(ni):

                    def fill(ty, carry, n=n, sx=sx, at=owner[sx * nj + jn]):
                        wsp[n, sx, ty] = jnp.full((8, 128), cinv_s[at, owner[i * nj + ty]], F32)
                        return carry

                    lax.fori_loop(0, nj, fill, 0, unroll=4)

        else:

            def restore(n, carry):
                field = []
                for x in range(wide):
                    for t in range(4):
                        at = pl.multiple_of((n * wide + x) * PLANE, PLANE) + t * 32
                        field.append(jnp.concatenate([X[pl.ds(at + k * 8, 8), :] for k in range(4)], axis=1))
                field = reorder(jnp.concatenate(field, axis=0), PM[...], True)
                for x in range(wide):
                    for t in range(4):
                        for c in range(4):
                            at = pl.ds((n * wide + x) * 32 + t, 8, stride=4)
                            r = x * 32 + t * 8
                            xpre[c, at, :] = field[r : r + 8, c * 128 : c * 128 + 128]
                return carry

            lax.fori_loop(0, 32 // wide, restore, 0)

        for copy in gather:
            copy.wait_recv()
        sub = lax.broadcasted_iota(jnp.int32, (8, 128), 0) < 4
        for sx in range(ni):

            def term(ty, acc, sx=sx):
                lo, hi, down, up = acc
                g01, g23 = G[it, ty, 0:8, :], G[it, ty, 8:16, :]
                g13 = jnp.where(sub, pltpu.roll(g01, 4, 0), g23)
                g02 = jnp.where(sub, g01, pltpu.roll(g23, 4, 0))
                w = wsp[1, sx, ty]
                return lo + w * g01, hi + w * g23, down + wsp[0, sx, ty] * g13, up + wsp[2, sx, ty] * g02

            lo, hi, down, up = lax.fori_loop(0, nj, term, (zero,) * 4, unroll=8)
            PB[it, sx, 0:8, :] = lo
            PB[it, sx, 8:16, :] = hi
            PB[it, (sx + 1) % ni, 16:24, :] = hi
            PB[it, (sx - 1) % ni, 24:32, :] = lo
            PB[it, sx, 32:40, :] = down
            PB[it, sx, 40:48, :] = up
        R[it, i] = PB[it, i]
        parts = []
        for d in range(1, ni):
            to = lax.rem(i + d, ni)
            copy = remote(PB.at[it, to], R.at[it, i], sr.at[it, d], rr.at[it, d], {"gx": to})
            copy.start()
            sends.append(copy)
            came = R.at[it, lax.rem(i + ni - d, ni)]
            parts.append(remote(PB.at[it, to], came, sr.at[it, d], rr.at[it, d], {"gx": to}))
        for copy in faces:
            copy.wait_recv()
        for copy in parts:
            copy.wait_recv()
        sums = R[it, 0]
        for n in range(1, ni):
            sums = sums + R[it, n]
        own = sums[0:16]
        other = [sums[16 + 8 * n : 24 + 8 * n] for n in range(4)]

        def row(block, c, chunk):
            return block[c * 4 + chunk : c * 4 + chunk + 1, :]

        def along_y(block, c0, c1):
            out = []
            for chunk in range(4):
                p = row(block, c0, chunk)[None, None]
                q = row(block, c1, chunk)[None, None]
                out.append((1.0 - wy) * p + wy * q)
            return jnp.concatenate(out, axis=1)

        def along_x(block, c0, c1):
            out = []
            for chunk in range(4):
                out.append((1.0 - wx8) * row(block, c0, chunk) + wx8 * row(block, c1, chunk))
            return jnp.concatenate(out, axis=0)

        sq = zero
        for n, (fun, c0, c1, sign, has) in enumerate((
            (along_y, 0, 1, -1.0, has_left),
            (along_y, 2, 3, 1.0, has_right),
            (along_x, 0, 2, -1.0, has_lower),
            (along_x, 1, 3, 1.0, has_upper),
        )):
            mine = FS[it, n] + fun(own, c0, c1).reshape(PLANE, 128)
            theirs = FR[it, n] + fun(other[n], 0, 1).reshape(PLANE, 128)
            jump = (mine - theirs) * (sign * has)
            JMP[n] = jump
            if sign > 0:
                sq = sq + jnp.sum((jump * jump).reshape(16, 8, 128), axis=0)
        me = i * nj + j
        row_sum = jnp.sum(sq, axis=0, keepdims=True)
        TS[it] = row_sum
        TR[it, pl.ds(me, 1), :] = row_sum

        for other_one in everyone:
            remote(TS.at[it], TR.at[it, pl.ds(me, 1)], st.at[it], rt.at[it], other_one).start()
        all_but_one = TR.at[it, pl.ds(0, ni * nj - 1)]
        told = remote(all_but_one, all_but_one, st.at[it], rt.at[it], right)
        sends.append(told)
        if it == 0:
            start = along_y(own, 0, 1)
            slope = along_y(own, 2, 3) - start
            m_start = beside_yz(start)
            m_slope = beside_yz(slope)

            def corrected(x, carry):
                wx = x.astype(F32) / 31.0
                e = start + wx * slope
                beside = m_start + wx * m_slope + 2.0 * e
                diag = tiles(U[0, rows(x + 1), :])
                U[1, rows(x + 1), :] = (
                    tiles(U[1, rows(x + 1), :]) - (diag * e - beside)
                ).reshape(PLANE, 128)
                X[rows(x), :] = (tiles(X[rows(x), :]) + e).reshape(PLANE, 128)
                return carry

            lax.fori_loop(0, 32, corrected, 0)
            U[1, rows(1), :] = U[1, rows(1), :] - (start - slope / 31.0).reshape(PLANE, 128)
            U[1, rows(32), :] = U[1, rows(32), :] - (start + slope * (32.0 / 31.0)).reshape(PLANE, 128)
        if it == ITERS - 1:
            CC[...] = jnp.zeros((8, 512), F32)
            for c in range(4):
                for k in range(4):
                    CC[pl.ds(c, 1), pl.ds(k * 128, 128)] = row(own, c, k)
            corr = reorder(CC[...], PM[...], True)
            wy2 = lax.broadcasted_iota(jnp.int32, (32, 128), 0).astype(F32) / 31.0
            for c in range(4):
                c0, c1, c2, c3 = (corr[n : n + 1, c * 128 : c * 128 + 128] for n in range(4))
                begin = (1.0 - wy2) * c0 + wy2 * c1
                end = (1.0 - wy2) * c2 + wy2 * c3

                def add(x, carry, c=c, begin=begin, end=end):
                    wx = x.astype(F32) / 31.0
                    at = pl.ds(pl.multiple_of(x * 32, 32), 32)
                    xpre[c, at, :] = xpre[c, at, :] + ((1.0 - wx) * begin + wx * end)
                    return carry

                lax.fori_loop(0, 32, add, 0, unroll=8)
        told.wait_recv()
        total = jnp.sum(TR[it].reshape(ni * nj // 8, 8, 128), axis=0)
        count = (ni - 1) * nj * 32 * 512 + ni * 32 * (nj - 1) * 512
        step = 0.5 / jnp.sqrt(total_of(total) / float(count) + 1e-6)
        for n in range(4):
            lam = (JMP[n].reshape(16, 8, 128) * step[None]).reshape(PLANE, 128)
            if it > 0:
                lam = LAM[n] + lam
            LAM[n] = lam
        if it == 0:
            U[1, rows(32), :] = U[1, rows(32), :] - LAM[1]
            U[1, rows(1), :] = U[1, rows(1), :] + LAM[0]
            for n, (t, s, sign) in ((3, (3, 7, -1.0)), (2, (0, 0, 1.0))):
                for c in range(4):
                    for h in range(4):
                        at = pl.ds(PLANE + h * 8 * PLANE + t * 32 + c * 8 + s, 8, stride=PLANE)
                        U[1, at, :] = U[1, at, :] + sign * LAM[n, pl.ds(c * 32 + h * 8, 8), :]
        else:
            lam_x = LAM[1].reshape(4, 4, 8, 128)
            lam_x = jnp.concatenate([lam_x[:, k].reshape(32, 128) for k in range(4)], axis=1)
            lam_y = jnp.concatenate([LAM[3, pl.ds(k * 32, 32), :] for k in range(4)], axis=1)
            both = reorder(jnp.concatenate([lam_x, lam_y], axis=0), PM[...], True)
            for c in range(4):
                lamy_out[pl.ds(c * 32, 32), :] = both[32:64, c * 128 : c * 128 + 128]
                for t in range(4):
                    part_of = both[t * 8 : t * 8 + 8, c * 128 : c * 128 + 128]
                    lamx_out[pl.ds(c * 32 + t, 8, stride=4), :] = part_of
    for copy in sends:
        copy.wait_send()


def finish_kernel(field, lamx, lamy, vel, mx, my, my_s, sems):
    copies = []
    for c in range(4):
        at = pl.ds(c * 128, 128)
        copies.append(pltpu.make_async_copy(field.at[c], vel.at[:, at], sems.at[0, c]))
        copies.append(pltpu.make_async_copy(lamx.at[pl.ds(c * 32, 32)], mx.at[:, at], sems.at[1, c]))
    for copy in copies:
        copy.start()
    for c in range(4):
        my_s[:, :, pl.ds(c * 128, 128)] = lamy[pl.ds(c * 32, 32), :].reshape(32, 1, 128)
    copies.append(pltpu.make_async_copy(my_s, my, sems.at[2, 0]))
    copies[-1].start()
    for copy in copies:
        copy.wait()


def on_device(ni, nj, perm_class, class_drag, force, coarse_inverse, coarse_owner):
    hbm = pl.BlockSpec(memory_space=pl.ANY)
    vmem = pl.BlockSpec(memory_space=pltpu.VMEM)
    smem = pl.BlockSpec(memory_space=pltpu.SMEM)
    dma = pltpu.SemaphoreType.DMA
    xpre, lamx, lamy = pl.pallas_call(
        functools.partial(kernel, ni, nj),
        out_shape=(
            pltpu.VMEM((4, 1024, 128), F32),
            pltpu.VMEM((128, 128), F32),
            pltpu.VMEM((128, 128), F32),
        ),
        in_specs=[hbm, smem, hbm, hbm, smem],
        out_specs=(vmem, vmem, vmem),
        scratch_shapes=[
            pltpu.VMEM((SWEEPS + 2, 34 * PLANE, 128), F32),
            pltpu.VMEM((34 * PLANE, 128), F32),
            pltpu.VMEM((32 * PLANE, 128), F32),
            pltpu.VMEM((4, 1024, 128), F32),
            pltpu.VMEM((4, 1024, 128), jnp.int32),
            pltpu.VMEM((16, 8, 128), F32),
            pltpu.VMEM((3, ni, nj, 8, 128), F32),
            pltpu.SMEM((ni * nj, ni * nj), F32),
            pltpu.VMEM((ITERS, 16, 128), F32),
            pltpu.VMEM((ITERS, nj, 16, 128), F32),
            pltpu.VMEM((ITERS, ni, 48, 128), F32),
            pltpu.VMEM((ITERS, ni, 48, 128), F32),
            pltpu.VMEM((ITERS, 4, PLANE, 128), F32),
            pltpu.VMEM((ITERS, 4, PLANE, 128), F32),
            pltpu.VMEM((ITERS, 1, 128), F32),
            pltpu.VMEM((ITERS, ni * nj, 128), F32),
            pltpu.VMEM((4, PLANE, 128), F32),
            pltpu.VMEM((4, PLANE, 128), F32),
            pltpu.VMEM((512, 512), BF16),
            pltpu.VMEM((8, 512), F32),
            dma((4, 8)), dma,
            dma((ITERS, nj)), dma((ITERS, nj)),
            dma((ITERS, ni)), dma((ITERS, ni)),
            dma((ITERS, 4)), dma((ITERS, 4)),
            dma((ITERS,)), dma((ITERS,)),
        ],
        compiler_params=pltpu.CompilerParams(
            collective_id=0, has_side_effects=True, vmem_limit_bytes=56 * 2**20
        ),
        name="solve",
    )(perm_class.reshape(1024, 512), class_drag, force.reshape(1024, 512), coarse_inverse, coarse_owner)
    velocity, mult_x, mult_y = pl.pallas_call(
        finish_kernel,
        out_shape=(
            jax.ShapeDtypeStruct((1024, 512), F32),
            jax.ShapeDtypeStruct((32, 512), F32),
            jax.ShapeDtypeStruct((32, 1, 512), F32),
        ),
        in_specs=[vmem] * 3,
        out_specs=(hbm, hbm, hbm),
        scratch_shapes=[pltpu.VMEM((32, 1, 512), F32), dma((3, 4))],
        compiler_params=pltpu.CompilerParams(vmem_limit_bytes=4 * 2**20),
        name="finish",
    )(xpre, lamx, lamy)
    return velocity.reshape(32, 32, 512), mult_x[None], mult_y


def solution(mesh):
    return jax.shard_map(
        functools.partial(on_device, mesh.shape["gx"], mesh.shape["yz"]),
        mesh=mesh,
        in_specs=(P("gx", "yz", None), P(), P("gx", "yz", None), P(), P()),
        out_specs=(P("gx", "yz", None), P("gx", "yz", None), P("gx", "yz", None)),
        check_vma=False,
    )
```

```python
import functools

import jax
import jax.numpy as jnp
from jax import lax
from jax.experimental import pallas as pl
from jax.experimental.pallas import tpu as pltpu
from jax.sharding import PartitionSpec as P

CLASSES = 8
SWEEPS = 8
ITERS = 2
F32 = jnp.float32
MESH = pl.DeviceIdType.MESH
BF16 = jnp.bfloat16
PLANE = 128
UNROLL = 32


def rows(x):
    return pl.ds(pl.multiple_of(x * PLANE, PLANE), PLANE)


def tiles(value):
    return value.reshape(4, 4, 8, 128)


def beside_yz(cur):
    lane = lax.broadcasted_iota(jnp.int32, (4, 1, 8, 128), 3)
    sub = lax.broadcasted_iota(jnp.int32, (1, 4, 8, 128), 2)
    left = jnp.where(lane == 0, 0.0, pltpu.roll(cur[:, 3:4], 1, 3))
    right = jnp.where(lane == 127, 0.0, pltpu.roll(cur[:, 0:1], 127, 3))
    before = jnp.where(sub == 0, 0.0, pltpu.roll(cur[3:4], 1, 2))
    after = jnp.where(sub == 7, 0.0, pltpu.roll(cur[0:1], 7, 2))
    low = jnp.concatenate([before, cur[0:3]], axis=0)
    high = jnp.concatenate([cur[1:4], after], axis=0)
    nearer = jnp.concatenate([left, cur[:, 0:3]], axis=1)
    further = jnp.concatenate([cur[:, 1:4], right], axis=1)
    return (high + low) + (nearer + further)


def three(a):
    high = a.astype(BF16)
    rest = a - high.astype(F32)
    middle = rest.astype(BF16)
    return high, middle, (rest - middle.astype(F32)).astype(BF16)


def reorder(a, perm, back):
    dims = (((1,), (1 if back else 0,)), ((), ()))
    out = None
    for piece in three(a):
        term = lax.dot_general(piece, perm, dims, preferred_element_type=F32)
        out = term if out is None else out + term
    return out


def total_of(a):
    a = jnp.sum(jnp.sum(a, axis=0, keepdims=True), axis=1, keepdims=True)
    return jnp.broadcast_to(a, (8, 128))


def splat(a):
    return a[None, None]


def part(x, t):
    return pl.ds(pl.multiple_of(x * PLANE, PLANE) + t * 32, 32)


def quad(value):
    return value.reshape(4, 8, 128)


def sweep_pass(k, first, a, b, U, W):
    lane = lax.broadcasted_iota(jnp.int32, (1, 8, 128), 2)
    sub = lax.broadcasted_iota(jnp.int32, (4, 8, 128), 1)

    def fresh(x, t):
        u = quad(W[part(x, t), :]) - a[None] * quad(U[k, part(x, t), :])
        u = u - b[None] * quad(U[k - 1, part(x, t), :])
        U[k + 1, part(x, t), :] = u.reshape(32, 128)
        return u

    def step(x, acc):
        uu, uw = acc
        for t in range(4):
            if first:
                above = quad(U[k + 1, part(x + 2, t), :])
            else:
                above = fresh(x + 2, t)
            cur = quad(U[k + 1, part(x + 1, t), :])
            below = quad(U[k + 1, part(x, t), :])
            low = quad(U[k + 1, part(x + 1, (t + 3) % 4), :])
            high = quad(U[k + 1, part(x + 1, (t + 1) % 4), :])
            if t == 0:
                low = jnp.where(sub == 0, 0.0, pltpu.roll(low, 1, 1))
            if t == 3:
                high = jnp.where(sub == 7, 0.0, pltpu.roll(high, 7, 1))
            left = jnp.where(lane == 0, 0.0, pltpu.roll(cur[3:4], 1, 2))
            right = jnp.where(lane == 127, 0.0, pltpu.roll(cur[0:1], 127, 2))
            left = jnp.concatenate([left, cur[0:3]], axis=0)
            right = jnp.concatenate([cur[1:4], right], axis=0)
            beside = ((above + below) + (high + low)) + (left + right)
            w = quad(U[0, part(x + 1, t), :]) * cur - beside
            W[part(x + 1, t), :] = w.reshape(32, 128)
            uu, uw = uu + cur * cur, uw + cur * w
        return uu, uw

    if not first:
        for t in range(4):
            fresh(1, t)
    zero = jnp.zeros((4, 8, 128), F32)
    uu, uw = lax.fori_loop(0, 32, step, (zero, zero), unroll=UNROLL)
    g = total_of(jnp.sum(uu, axis=0))
    return g, total_of(jnp.sum(uw, axis=0)) / g


def y_weights(width):
    t = lax.broadcasted_iota(jnp.int32, (4, 1, 8, 128), 0)
    s = lax.broadcasted_iota(jnp.int32, (4, 1, 8, 128), 2)
    return (4 * s + t).astype(F32) / (width - 1)


def kernel(
    ni, nj, perm, drag, force, cinv, owner,
    xpre, lamx_out, lamy_out,
    U, W, X, fst, pst, cf, wsp, cinv_s, cbuf, G, PB, R, FS, FR, TS, TR, LAM, JMP, PM, CC, RL,
    in_sem, ci_sem, sg, rg, sr, rr, sf, rf, st, rt,
):
    i = lax.axis_index("gx")
    j = lax.axis_index("yz")
    zero = jnp.zeros((8, 128), F32)
    plane0 = jnp.zeros((PLANE, 128), F32)

    barrier = pltpu.get_barrier_semaphore()

    wide = 8

    def chunk_copies(n):
        at = pl.ds(pl.multiple_of(n * wide * 32, wide * 32), wide * 32)
        out = []
        for c in range(4):
            cols = pl.ds(c * 128, 128)
            out.append(pltpu.make_async_copy(perm.at[at, cols], pst.at[c, at], in_sem.at[n, c]))
            out.append(pltpu.make_async_copy(force.at[at, cols], fst.at[c, at], in_sem.at[n, 4 + c]))
        return out

    for n in range(32 // wide):
        for copy in chunk_copies(n):
            copy.start()
    weights_copy = pltpu.make_async_copy(cinv, cinv_s, ci_sem)
    weights_copy.start()

    def greet(n, carry):
        dev = {"gx": lax.rem(i + n // nj, ni), "yz": lax.rem(j + n % nj, nj)}
        pl.semaphore_signal(barrier, inc=1, device_id=dev, device_id_type=MESH)
        return carry

    lax.fori_loop(1, ni * nj, greet, 0)

    for k in range(SWEEPS + 2):
        U[k, rows(0), :] = plane0
        U[k, rows(33), :] = plane0
    W[rows(33), :] = plane0

    for n in range(4):
        zin = lax.broadcasted_iota(jnp.int32, (512, 128), 0)
        lane = lax.broadcasted_iota(jnp.int32, (512, 128), 1)
        PM[:, pl.ds(n * 128, 128)] = jnp.where(zin == 4 * lane + n, 1.0, 0.0).astype(BF16)

    lane8 = lax.broadcasted_iota(jnp.int32, (8, 128), 1)
    level = zero
    for c in range(CLASSES):
        level = jnp.where(lane8 == c, 6.0 + drag[c], level)

    def stage(n, carry):
        for copy in chunk_copies(n):
            copy.wait()
        perm_matrix = PM[...]

        def gathered(ref):
            out = []
            for x in range(wide):
                for t in range(4):
                    at = pl.ds(n * wide * 32 + x * 32 + t, 8, stride=4)
                    out.append(jnp.concatenate([ref[c, at, :] for c in range(4)], axis=1))
            return jnp.concatenate(out, axis=0)

        classes = gathered(pst).astype(F32).astype(BF16)
        classes = jnp.dot(classes, perm_matrix, preferred_element_type=F32)
        field = reorder(gathered(fst), perm_matrix, False)
        for x in range(wide):
            for t in range(4):
                for k in range(4):
                    r, l = slice(x * 32 + t * 8, x * 32 + t * 8 + 8), slice(k * 128, k * 128 + 128)
                    at = pl.ds(pl.multiple_of((n * wide + x + 1) * PLANE, PLANE) + t * 32 + k * 8, 8)
                    cls = classes[r, l].astype(jnp.int32)
                    U[0, at, :] = jnp.take_along_axis(level, cls, axis=1, mode="promise_in_bounds")
                    U[1, at, :] = field[r, l]
        return carry

    lax.fori_loop(0, 32 // wide, stage, 0)

    has_right = (i < ni - 1).astype(F32)
    has_left = (i > 0).astype(F32)
    has_upper = (j < nj - 1).astype(F32)
    has_lower = (j > 0).astype(F32)
    wy = y_weights(32)
    wx8 = lax.broadcasted_iota(jnp.int32, (32, 128), 0).astype(F32) / 31.0
    right, left = {"gx": lax.rem(i + 1, ni)}, {"gx": lax.rem(i + ni - 1, ni)}
    upper, lower = {"yz": lax.rem(j + 1, nj)}, {"yz": lax.rem(j + nj - 1, nj)}
    ring = (2, 1, 3, 0)
    gx_of = [lax.rem(i // 2 + ax, ni // 2) * 2 + lax.rem(i % 2 + core, 2) for ax in ring[-ni // 2 :] for core in (1, 0)]
    yz_of = [lax.rem(j // 4 + az, nj // 4) * 4 + lax.rem(j % 4 + ay, 4) for az in ring[-nj // 4 :] for ay in ring]
    far = []
    for p in range(ni):
        for q in range(nj):
            hops = sum((2, 1, 1, 0)[n] for n in (p // 2, q // 4, q % 4))
            far.append((-hops, p, q))
    everyone = [{"gx": gx_of[p], "yz": yz_of[q]} for _, p, q in sorted(far)[:-1] if (p, q) != (ni - 1, nj - 1)]
    sends = []

    def remote(src, dst, ssem, rsem, dev):
        return pltpu.make_async_remote_copy(
            src_ref=src, dst_ref=dst, send_sem=ssem, recv_sem=rsem, device_id=dev, device_id_type=MESH
        )

    for it in range(ITERS):
        g, a = sweep_pass(0, True, zero, zero, U, W)
        one = jnp.ones((8, 128), F32)

        def body(k, carry):
            g, a, b, pivot, z = carry
            inv = 1.0 / (a - b * pivot)
            cf[k - 1] = inv
            cf[7 + k] = b
            cf[15 + k] = z
            gn, an = sweep_pass(k, False, a, b, U, W)
            return gn, an, gn / g, inv, -z * inv

        g, a, b, pivot, z = lax.fori_loop(1, SWEEPS, body, (g, a, zero, zero, one))

        y = [None] * SWEEPS
        y[SWEEPS - 1] = z / (a - b * pivot)
        above = b
        for k in range(SWEEPS - 2, -1, -1):
            y[k] = (cf[16 + k] - above * y[k + 1]) * cf[k]
            above = cf[8 + k]

        for n, x in ((0, 0), (1, 31)):
            for m, (t, r) in enumerate(((0, 0), (3, 7))):
                for c in range(4):
                    at = t * 32 + c * 8
                    f = None if it == 0 else X[pl.ds(x * PLANE + at, 8), :]
                    for k in range(SWEEPS):
                        term = y[k] * U[k + 1, pl.ds((x + 1) * PLANE + at, 8), :]
                        f = term if f is None else f + term
                    cbuf[it, pl.ds((2 * n + m) * 4 + c, 1), :] = f[r : r + 1, :]
        G[it, j] = cbuf[it]
        if it == 0:
            pl.semaphore_wait(barrier, ni * nj - 1)
        gather = []
        for d in sorted(range(1, nj), key=lambda d: -abs((d + 2) % 4 - 2) - abs((d // 4 + 2) % 4 - 2)):
            dev = {"yz": lax.rem(j + d, nj)}
            copy = remote(cbuf.at[it], G.at[it, j], sg.at[it, d], rg.at[it, d], dev)
            copy.start()
            sends.append(copy)
            came = G.at[it, lax.rem(j + nj - d, nj)]
            gather.append(remote(cbuf.at[it], came, sg.at[it, d], rg.at[it, d], dev))
        def gather_x(x, carry):
            f = None if it == 0 else tiles(X[rows(x), :])
            for k in range(SWEEPS):
                term = splat(y[k]) * tiles(U[k + 1, rows(x + 1), :])
                f = term if f is None else f + term
            for c in range(4):
                FS[it, 2, pl.ds(c * 32 + x, 1), :] = f[0, c, 0:1, :]
                FS[it, 3, pl.ds(c * 32 + x, 1), :] = f[3, c, 7:8, :]
            if it == 0:
                X[rows(x), :] = f.reshape(PLANE, 128)
                u = tiles(W[rows(x + 1), :]) - splat(a) * tiles(U[8, rows(x + 1), :])
                u = u - splat(b) * tiles(U[7, rows(x + 1), :])
                U[1, rows(x + 1), :] = (splat(-y[7]) * u).reshape(PLANE, 128)
            else:
                X[rows(x), :] = f.reshape(PLANE, 128)
            return carry

        lax.fori_loop(0, 32, gather_x, 0, unroll=4)
        FS[it, 0] = X[rows(0), :]
        FS[it, 1] = X[rows(31), :]
        faces = []
        for src, dst, dev in ((1, 0, right), (0, 1, left), (3, 2, upper), (2, 3, lower)):
            copy = remote(FS.at[it, src], FR.at[it, dst], sf.at[it, dst], rf.at[it, dst], dev)
            copy.start()
            faces.append(copy)
        sends.extend(faces)
        if it == 0:
            weights_copy.wait()
            for n in range(3):
                jn = lax.rem(j + nj - 1 + n, nj)
                for sx in range(ni):

                    def fill(ty, carry, n=n, sx=sx, at=owner[sx * nj + jn]):
                        wsp[n, sx, ty] = jnp.full((8, 128), cinv_s[at, owner[i * nj + ty]], F32)
                        return carry

                    lax.fori_loop(0, nj, fill, 0, unroll=4)

        else:

            def restore(n, carry):
                field = []
                for x in range(wide):
                    for t in range(4):
                        at = pl.multiple_of((n * wide + x) * PLANE, PLANE) + t * 32
                        field.append(jnp.concatenate([X[pl.ds(at + k * 8, 8), :] for k in range(4)], axis=1))
                field = reorder(jnp.concatenate(field, axis=0), PM[...], True)
                for x in range(wide):
                    for t in range(4):
                        for c in range(4):
                            at = pl.ds((n * wide + x) * 32 + t, 8, stride=4)
                            r = x * 32 + t * 8
                            xpre[c, at, :] = field[r : r + 8, c * 128 : c * 128 + 128]
                return carry

            lax.fori_loop(0, 32 // wide, restore, 0)

        for copy in gather:
            copy.wait_recv()
        sub = lax.broadcasted_iota(jnp.int32, (8, 128), 0) < 4
        for sx in range(ni):

            def term(ty, acc, sx=sx):
                lo, hi, down, up = acc
                g01, g23 = G[it, ty, 0:8, :], G[it, ty, 8:16, :]
                g13 = jnp.where(sub, pltpu.roll(g01, 4, 0), g23)
                g02 = jnp.where(sub, g01, pltpu.roll(g23, 4, 0))
                w = wsp[1, sx, ty]
                return lo + w * g01, hi + w * g23, down + wsp[0, sx, ty] * g13, up + wsp[2, sx, ty] * g02

            lo, hi, down, up = lax.fori_loop(0, nj, term, (zero,) * 4, unroll=8)
            PB[it, sx, 0:8, :] = lo
            PB[it, sx, 8:16, :] = hi
            PB[it, (sx + 1) % ni, 16:24, :] = hi
            PB[it, (sx - 1) % ni, 24:32, :] = lo
            PB[it, sx, 32:40, :] = down
            PB[it, sx, 40:48, :] = up
        R[it, i] = PB[it, i]
        parts = []
        for d in range(1, ni):
            to = lax.rem(i + d, ni)
            copy = remote(PB.at[it, to], R.at[it, i], sr.at[it, d], rr.at[it, d], {"gx": to})
            copy.start()
            sends.append(copy)
            came = R.at[it, lax.rem(i + ni - d, ni)]
            parts.append(remote(PB.at[it, to], came, sr.at[it, d], rr.at[it, d], {"gx": to}))
        for copy in faces:
            copy.wait_recv()
        for copy in parts:
            copy.wait_recv()
        sums = R[it, 0]
        for n in range(1, ni):
            sums = sums + R[it, n]
        own = sums[0:16]
        other = [sums[16 + 8 * n : 24 + 8 * n] for n in range(4)]

        def row(block, c, chunk):
            return block[c * 4 + chunk : c * 4 + chunk + 1, :]

        def along_y(block, c0, c1):
            out = []
            for chunk in range(4):
                p = row(block, c0, chunk)[None, None]
                q = row(block, c1, chunk)[None, None]
                out.append((1.0 - wy) * p + wy * q)
            return jnp.concatenate(out, axis=1)

        def along_x(block, c0, c1):
            out = []
            for chunk in range(4):
                out.append((1.0 - wx8) * row(block, c0, chunk) + wx8 * row(block, c1, chunk))
            return jnp.concatenate(out, axis=0)

        sq = zero
        for n, (fun, c0, c1, sign, has) in enumerate((
            (along_y, 0, 1, -1.0, has_left),
            (along_y, 2, 3, 1.0, has_right),
            (along_x, 0, 2, -1.0, has_lower),
            (along_x, 1, 3, 1.0, has_upper),
        )):
            mine = FS[it, n] + fun(own, c0, c1).reshape(PLANE, 128)
            theirs = FR[it, n] + fun(other[n], 0, 1).reshape(PLANE, 128)
            jump = (mine - theirs) * (sign * has)
            JMP[n] = jump
            if sign > 0:
                sq = sq + jnp.sum((jump * jump).reshape(16, 8, 128), axis=0)
        me = i * nj + j
        row_sum = jnp.sum(sq, axis=0, keepdims=True)
        TS[it] = row_sum
        TR[it, pl.ds(me, 1), :] = row_sum

        for other_one in everyone:
            remote(TS.at[it], TR.at[it, pl.ds(me, 1)], st.at[it], rt.at[it], other_one).start()
        all_but_one = TR.at[it, pl.ds(0, ni * nj - 1)]
        told = remote(all_but_one, all_but_one, st.at[it], rt.at[it], right)
        arrived, sends = sends, [told]
        if it == 0:
            start = along_y(own, 0, 1)
            slope = along_y(own, 2, 3) - start
            m_start = beside_yz(start)
            m_slope = beside_yz(slope)

            def corrected(x, carry):
                wx = x.astype(F32) / 31.0
                e = start + wx * slope
                beside = m_start + wx * m_slope + 2.0 * e
                diag = tiles(U[0, rows(x + 1), :])
                U[1, rows(x + 1), :] = (
                    tiles(U[1, rows(x + 1), :]) - (diag * e - beside)
                ).reshape(PLANE, 128)
                X[rows(x), :] = (tiles(X[rows(x), :]) + e).reshape(PLANE, 128)
                return carry

            lax.fori_loop(0, 32, corrected, 0)
            U[1, rows(1), :] = U[1, rows(1), :] - (start - slope / 31.0).reshape(PLANE, 128)
            U[1, rows(32), :] = U[1, rows(32), :] - (start + slope * (32.0 / 31.0)).reshape(PLANE, 128)
        if it == ITERS - 1:
            faces_in = []
            for ref in (LAM, JMP):
                face = ref[1].reshape(4, 4, 8, 128)
                faces_in.append(jnp.concatenate([face[:, k].reshape(32, 128) for k in range(4)], axis=1))
                faces_in.append(jnp.concatenate([ref[3, pl.ds(k * 32, 32), :] for k in range(4)], axis=1))
            RL[...] = reorder(jnp.concatenate(faces_in, axis=0), PM[...], True)
            CC[...] = jnp.zeros((8, 512), F32)
            for c in range(4):
                for k in range(4):
                    CC[pl.ds(c, 1), pl.ds(k * 128, 128)] = row(own, c, k)
            corr = reorder(CC[...], PM[...], True)
            wy2 = lax.broadcasted_iota(jnp.int32, (32, 128), 0).astype(F32) / 31.0
            for c in range(4):
                c0, c1, c2, c3 = (corr[n : n + 1, c * 128 : c * 128 + 128] for n in range(4))
                begin = (1.0 - wy2) * c0 + wy2 * c1
                end = (1.0 - wy2) * c2 + wy2 * c3

                def add(x, carry, c=c, begin=begin, end=end):
                    wx = x.astype(F32) / 31.0
                    at = pl.ds(pl.multiple_of(x * 32, 32), 32)
                    xpre[c, at, :] = xpre[c, at, :] + ((1.0 - wx) * begin + wx * end)
                    return carry

                lax.fori_loop(0, 32, add, 0, unroll=8)
        for copy in arrived:
            copy.wait_send()
        told.wait_recv()
        total = jnp.sum(TR[it].reshape(ni * nj // 8, 8, 128), axis=0)
        count = (ni - 1) * nj * 32 * 512 + ni * 32 * (nj - 1) * 512
        step = 0.5 / jnp.sqrt(total_of(total) / float(count) + 1e-6)
        if it == 0:
            for n in range(4):
                LAM[n] = (JMP[n].reshape(16, 8, 128) * step[None]).reshape(PLANE, 128)
            U[1, rows(32), :] = U[1, rows(32), :] - LAM[1]
            U[1, rows(1), :] = U[1, rows(1), :] + LAM[0]
            for n, (t, s, sign) in ((3, (3, 7, -1.0)), (2, (0, 0, 1.0))):
                for c in range(4):
                    for h in range(4):
                        at = pl.ds(PLANE + h * 8 * PLANE + t * 32 + c * 8 + s, 8, stride=PLANE)
                        U[1, at, :] = U[1, at, :] + sign * LAM[n, pl.ds(c * 32 + h * 8, 8), :]
        else:
            for c in range(4):
                cols = pl.ds(c * 128, 128)
                for h in range(4):
                    both = RL[pl.ds(h * 8, 8), cols] + step * RL[pl.ds(64 + h * 8, 8), cols]
                    lamx_out[pl.ds(c * 32 + h, 8, stride=4), :] = both
                    both = RL[pl.ds(32 + h * 8, 8), cols] + step * RL[pl.ds(96 + h * 8, 8), cols]
                    lamy_out[pl.ds(c * 32 + h * 8, 8), :] = both
    for copy in sends:
        copy.wait_send()


def finish_kernel(field, lamx, lamy, vel, mx, my, my_s, sems):
    copies = []
    for c in range(4):
        at = pl.ds(c * 128, 128)
        copies.append(pltpu.make_async_copy(field.at[c], vel.at[:, at], sems.at[0, c]))
        copies.append(pltpu.make_async_copy(lamx.at[pl.ds(c * 32, 32)], mx.at[:, at], sems.at[1, c]))
    for copy in copies:
        copy.start()
    for c in range(4):
        my_s[:, :, pl.ds(c * 128, 128)] = lamy[pl.ds(c * 32, 32), :].reshape(32, 1, 128)
    copies.append(pltpu.make_async_copy(my_s, my, sems.at[2, 0]))
    copies[-1].start()
    for copy in copies:
        copy.wait()


def on_device(ni, nj, perm_class, class_drag, force, coarse_inverse, coarse_owner):
    hbm = pl.BlockSpec(memory_space=pl.ANY)
    vmem = pl.BlockSpec(memory_space=pltpu.VMEM)
    smem = pl.BlockSpec(memory_space=pltpu.SMEM)
    dma = pltpu.SemaphoreType.DMA
    xpre, lamx, lamy = pl.pallas_call(
        functools.partial(kernel, ni, nj),
        out_shape=(
            pltpu.VMEM((4, 1024, 128), F32),
            pltpu.VMEM((128, 128), F32),
            pltpu.VMEM((128, 128), F32),
        ),
        in_specs=[hbm, smem, hbm, hbm, smem],
        out_specs=(vmem, vmem, vmem),
        scratch_shapes=[
            pltpu.VMEM((SWEEPS + 2, 34 * PLANE, 128), F32),
            pltpu.VMEM((34 * PLANE, 128), F32),
            pltpu.VMEM((32 * PLANE, 128), F32),
            pltpu.VMEM((4, 1024, 128), F32),
            pltpu.VMEM((4, 1024, 128), jnp.int32),
            pltpu.VMEM((24, 8, 128), F32),
            pltpu.VMEM((3, ni, nj, 8, 128), F32),
            pltpu.SMEM((ni * nj, ni * nj), F32),
            pltpu.VMEM((ITERS, 16, 128), F32),
            pltpu.VMEM((ITERS, nj, 16, 128), F32),
            pltpu.VMEM((ITERS, ni, 48, 128), F32),
            pltpu.VMEM((ITERS, ni, 48, 128), F32),
            pltpu.VMEM((ITERS, 4, PLANE, 128), F32),
            pltpu.VMEM((ITERS, 4, PLANE, 128), F32),
            pltpu.VMEM((ITERS, 1, 128), F32),
            pltpu.VMEM((ITERS, ni * nj, 128), F32),
            pltpu.VMEM((4, PLANE, 128), F32),
            pltpu.VMEM((4, PLANE, 128), F32),
            pltpu.VMEM((512, 512), BF16),
            pltpu.VMEM((8, 512), F32),
            pltpu.VMEM((128, 512), F32),
            dma((4, 8)), dma,
            dma((ITERS, nj)), dma((ITERS, nj)),
            dma((ITERS, ni)), dma((ITERS, ni)),
            dma((ITERS, 4)), dma((ITERS, 4)),
            dma((ITERS,)), dma((ITERS,)),
        ],
        compiler_params=pltpu.CompilerParams(
            collective_id=0, has_side_effects=True, vmem_limit_bytes=56 * 2**20
        ),
        name="solve",
    )(perm_class.reshape(1024, 512), class_drag, force.reshape(1024, 512), coarse_inverse, coarse_owner)
    velocity, mult_x, mult_y = pl.pallas_call(
        finish_kernel,
        out_shape=(
            jax.ShapeDtypeStruct((1024, 512), F32),
            jax.ShapeDtypeStruct((32, 512), F32),
            jax.ShapeDtypeStruct((32, 1, 512), F32),
        ),
        in_specs=[vmem] * 3,
        out_specs=(hbm, hbm, hbm),
        scratch_shapes=[pltpu.VMEM((32, 1, 512), F32), dma((3, 4))],
        compiler_params=pltpu.CompilerParams(vmem_limit_bytes=4 * 2**20),
        name="finish",
    )(xpre, lamx, lamy)
    return velocity.reshape(32, 32, 512), mult_x[None], mult_y


def solution(mesh):
    return jax.shard_map(
        functools.partial(on_device, mesh.shape["gx"], mesh.shape["yz"]),
        mesh=mesh,
        in_specs=(P("gx", "yz", None), P(), P("gx", "yz", None), P(), P()),
        out_specs=(P("gx", "yz", None), P("gx", "yz", None), P("gx", "yz", None)),
        check_vma=False,
    )
```

```python
import functools

import jax
import jax.numpy as jnp
from jax import lax
from jax.experimental import pallas as pl
from jax.experimental.pallas import tpu as pltpu
from jax.sharding import PartitionSpec as P

CLASSES = 8
SWEEPS = 8
ITERS = 2
F32 = jnp.float32
MESH = pl.DeviceIdType.MESH
BF16 = jnp.bfloat16
PLANE = 128
UNROLL = 32


def rows(x):
    return pl.ds(pl.multiple_of(x * PLANE, PLANE), PLANE)


def tiles(value):
    return value.reshape(4, 4, 8, 128)


def beside_yz(cur):
    lane = lax.broadcasted_iota(jnp.int32, (4, 1, 8, 128), 3)
    sub = lax.broadcasted_iota(jnp.int32, (1, 4, 8, 128), 2)
    left = jnp.where(lane == 0, 0.0, pltpu.roll(cur[:, 3:4], 1, 3))
    right = jnp.where(lane == 127, 0.0, pltpu.roll(cur[:, 0:1], 127, 3))
    before = jnp.where(sub == 0, 0.0, pltpu.roll(cur[3:4], 1, 2))
    after = jnp.where(sub == 7, 0.0, pltpu.roll(cur[0:1], 7, 2))
    low = jnp.concatenate([before, cur[0:3]], axis=0)
    high = jnp.concatenate([cur[1:4], after], axis=0)
    nearer = jnp.concatenate([left, cur[:, 0:3]], axis=1)
    further = jnp.concatenate([cur[:, 1:4], right], axis=1)
    return (high + low) + (nearer + further)


def three(a):
    high = a.astype(BF16)
    rest = a - high.astype(F32)
    middle = rest.astype(BF16)
    return high, middle, (rest - middle.astype(F32)).astype(BF16)


def reorder(a, perm, back):
    dims = (((1,), (1 if back else 0,)), ((), ()))
    out = None
    for piece in three(a):
        term = lax.dot_general(piece, perm, dims, preferred_element_type=F32)
        out = term if out is None else out + term
    return out


def total_of(a):
    a = jnp.sum(jnp.sum(a, axis=0, keepdims=True), axis=1, keepdims=True)
    return jnp.broadcast_to(a, (8, 128))


def splat(a):
    return a[None, None]


def part(x, t):
    return pl.ds(pl.multiple_of(x * PLANE, PLANE) + t * 32, 32)


def quad(value):
    return value.reshape(4, 8, 128)


def sweep_pass(k, first, a, b, U, W):
    lane = lax.broadcasted_iota(jnp.int32, (1, 8, 128), 2)
    sub = lax.broadcasted_iota(jnp.int32, (4, 8, 128), 1)

    def fresh(x, t):
        u = quad(W[part(x, t), :]) - a[None] * quad(U[k, part(x, t), :])
        u = u - b[None] * quad(U[k - 1, part(x, t), :])
        U[k + 1, part(x, t), :] = u.reshape(32, 128)
        return u

    def step(x, acc):
        uu, uw = acc
        for t in range(4):
            if first:
                above = quad(U[k + 1, part(x + 2, t), :])
            else:
                above = fresh(x + 2, t)
            cur = quad(U[k + 1, part(x + 1, t), :])
            below = quad(U[k + 1, part(x, t), :])
            low = quad(U[k + 1, part(x + 1, (t + 3) % 4), :])
            high = quad(U[k + 1, part(x + 1, (t + 1) % 4), :])
            if t == 0:
                low = jnp.where(sub == 0, 0.0, pltpu.roll(low, 1, 1))
            if t == 3:
                high = jnp.where(sub == 7, 0.0, pltpu.roll(high, 7, 1))
            left = jnp.where(lane == 0, 0.0, pltpu.roll(cur[3:4], 1, 2))
            right = jnp.where(lane == 127, 0.0, pltpu.roll(cur[0:1], 127, 2))
            left = jnp.concatenate([left, cur[0:3]], axis=0)
            right = jnp.concatenate([cur[1:4], right], axis=0)
            beside = ((above + below) + (high + low)) + (left + right)
            w = quad(U[0, part(x + 1, t), :]) * cur - beside
            W[part(x + 1, t), :] = w.reshape(32, 128)
            uu, uw = uu + cur * cur, uw + cur * w
        return uu, uw

    if not first:
        for t in range(4):
            fresh(1, t)
    zero = jnp.zeros((4, 8, 128), F32)
    uu, uw = lax.fori_loop(0, 32, step, (zero, zero), unroll=UNROLL)
    g = total_of(jnp.sum(uu, axis=0))
    return g, total_of(jnp.sum(uw, axis=0)) / g


def y_weights(width):
    t = lax.broadcasted_iota(jnp.int32, (4, 1, 8, 128), 0)
    s = lax.broadcasted_iota(jnp.int32, (4, 1, 8, 128), 2)
    return (4 * s + t).astype(F32) / (width - 1)


def kernel(
    ni, nj, perm, drag, force, cinv, owner,
    xpre, lamx_out, lamy_out,
    U, W, X, fst, pst, cf, wsp, cinv_s, cbuf, G, PB, R, FS, FR, TS, TR, LAM, JMP, PM, CC, RL,
    in_sem, ci_sem, sg, rg, sr, rr, sf, rf, st, rt,
):
    i = lax.axis_index("gx")
    j = lax.axis_index("yz")
    zero = jnp.zeros((8, 128), F32)
    plane0 = jnp.zeros((PLANE, 128), F32)

    barrier = pltpu.get_barrier_semaphore()

    wide = 8

    def chunk_copies(n):
        at = pl.ds(pl.multiple_of(n * wide * 32, wide * 32), wide * 32)
        out = []
        for c in range(4):
            cols = pl.ds(c * 128, 128)
            out.append(pltpu.make_async_copy(perm.at[at, cols], pst.at[c, at], in_sem.at[n, c]))
            out.append(pltpu.make_async_copy(force.at[at, cols], fst.at[c, at], in_sem.at[n, 4 + c]))
        return out

    for n in range(32 // wide):
        for copy in chunk_copies(n):
            copy.start()
    weights_copy = pltpu.make_async_copy(cinv, cinv_s, ci_sem)
    weights_copy.start()

    def greet(n, carry):
        dev = {"gx": lax.rem(i + n // nj, ni), "yz": lax.rem(j + n % nj, nj)}
        pl.semaphore_signal(barrier, inc=1, device_id=dev, device_id_type=MESH)
        return carry

    lax.fori_loop(1, ni * nj, greet, 0)

    for k in range(SWEEPS + 2):
        U[k, rows(0), :] = plane0
        U[k, rows(33), :] = plane0
    W[rows(33), :] = plane0

    for n in range(4):
        zin = lax.broadcasted_iota(jnp.int32, (512, 128), 0)
        lane = lax.broadcasted_iota(jnp.int32, (512, 128), 1)
        PM[:, pl.ds(n * 128, 128)] = jnp.where(zin == 4 * lane + n, 1.0, 0.0).astype(BF16)

    lane8 = lax.broadcasted_iota(jnp.int32, (8, 128), 1)
    level = zero
    for c in range(CLASSES):
        level = jnp.where(lane8 == c, 6.0 + drag[c], level)

    def stage(n, carry):
        for copy in chunk_copies(n):
            copy.wait()
        perm_matrix = PM[...]

        def gathered(ref):
            out = []
            for x in range(wide):
                for t in range(4):
                    at = pl.ds(n * wide * 32 + x * 32 + t, 8, stride=4)
                    out.append(jnp.concatenate([ref[c, at, :] for c in range(4)], axis=1))
            return jnp.concatenate(out, axis=0)

        pieces = (gathered(pst).astype(F32).astype(BF16),) + three(gathered(fst))
        size = wide * 32
        moved = jnp.dot(jnp.concatenate(pieces, axis=0), perm_matrix, preferred_element_type=F32)
        classes = moved[0:size]
        field = moved[size : 2 * size] + moved[2 * size : 3 * size] + moved[3 * size : 4 * size]
        for x in range(wide):
            for t in range(4):
                for k in range(4):
                    r, l = slice(x * 32 + t * 8, x * 32 + t * 8 + 8), slice(k * 128, k * 128 + 128)
                    at = pl.ds(pl.multiple_of((n * wide + x + 1) * PLANE, PLANE) + t * 32 + k * 8, 8)
                    cls = classes[r, l].astype(jnp.int32)
                    U[0, at, :] = jnp.take_along_axis(level, cls, axis=1, mode="promise_in_bounds")
                    U[1, at, :] = field[r, l]
        return carry

    lax.fori_loop(0, 32 // wide, stage, 0)

    has_right = (i < ni - 1).astype(F32)
    has_left = (i > 0).astype(F32)
    has_upper = (j < nj - 1).astype(F32)
    has_lower = (j > 0).astype(F32)
    wy = y_weights(32)
    wx8 = lax.broadcasted_iota(jnp.int32, (32, 128), 0).astype(F32) / 31.0
    right, left = {"gx": lax.rem(i + 1, ni)}, {"gx": lax.rem(i + ni - 1, ni)}
    upper, lower = {"yz": lax.rem(j + 1, nj)}, {"yz": lax.rem(j + nj - 1, nj)}
    ring = (2, 1, 3, 0)
    gx_of = [lax.rem(i // 2 + ax, ni // 2) * 2 + lax.rem(i % 2 + core, 2) for ax in ring[-ni // 2 :] for core in (1, 0)]
    yz_of = [lax.rem(j // 4 + az, nj // 4) * 4 + lax.rem(j % 4 + ay, 4) for az in ring[-nj // 4 :] for ay in ring]
    far = []
    for p in range(ni):
        for q in range(nj):
            hops = sum((2, 1, 1, 0)[n] for n in (p // 2, q // 4, q % 4))
            far.append((-hops, p, q))
    everyone = [{"gx": gx_of[p], "yz": yz_of[q]} for _, p, q in sorted(far)[:-1] if (p, q) != (ni - 1, nj - 1)]
    sends = []

    def remote(src, dst, ssem, rsem, dev):
        return pltpu.make_async_remote_copy(
            src_ref=src, dst_ref=dst, send_sem=ssem, recv_sem=rsem, device_id=dev, device_id_type=MESH
        )

    for it in range(ITERS):
        g, a = sweep_pass(0, True, zero, zero, U, W)
        one = jnp.ones((8, 128), F32)

        def body(k, carry):
            g, a, b, pivot, z = carry
            inv = 1.0 / (a - b * pivot)
            cf[k - 1] = inv
            cf[7 + k] = b
            cf[15 + k] = z
            gn, an = sweep_pass(k, False, a, b, U, W)
            return gn, an, gn / g, inv, -z * inv

        g, a, b, pivot, z = lax.fori_loop(1, SWEEPS, body, (g, a, zero, zero, one))

        y = [None] * SWEEPS
        y[SWEEPS - 1] = z / (a - b * pivot)
        above = b
        for k in range(SWEEPS - 2, -1, -1):
            y[k] = (cf[16 + k] - above * y[k + 1]) * cf[k]
            above = cf[8 + k]

        for n, x in ((0, 0), (1, 31)):
            for m, (t, r) in enumerate(((0, 0), (3, 7))):
                for c in range(4):
                    at = t * 32 + c * 8
                    f = None if it == 0 else X[pl.ds(x * PLANE + at, 8), :]
                    for k in range(SWEEPS):
                        term = y[k] * U[k + 1, pl.ds((x + 1) * PLANE + at, 8), :]
                        f = term if f is None else f + term
                    cbuf[it, pl.ds((2 * n + m) * 4 + c, 1), :] = f[r : r + 1, :]
        G[it, j] = cbuf[it]
        if it == 0:
            pl.semaphore_wait(barrier, ni * nj - 1)
        gather = []
        for d in sorted(range(1, nj), key=lambda d: -abs((d + 2) % 4 - 2) - abs((d // 4 + 2) % 4 - 2)):
            dev = {"yz": lax.rem(j + d, nj)}
            copy = remote(cbuf.at[it], G.at[it, j], sg.at[it, d], rg.at[it, d], dev)
            copy.start()
            sends.append(copy)
            came = G.at[it, lax.rem(j + nj - d, nj)]
            gather.append(remote(cbuf.at[it], came, sg.at[it, d], rg.at[it, d], dev))
        def gather_x(x, carry):
            f = None if it == 0 else tiles(X[rows(x), :])
            for k in range(SWEEPS):
                term = splat(y[k]) * tiles(U[k + 1, rows(x + 1), :])
                f = term if f is None else f + term
            for c in range(4):
                FS[it, 2, pl.ds(c * 32 + x, 1), :] = f[0, c, 0:1, :]
                FS[it, 3, pl.ds(c * 32 + x, 1), :] = f[3, c, 7:8, :]
            if it == 0:
                X[rows(x), :] = f.reshape(PLANE, 128)
                u = tiles(W[rows(x + 1), :]) - splat(a) * tiles(U[8, rows(x + 1), :])
                u = u - splat(b) * tiles(U[7, rows(x + 1), :])
                U[1, rows(x + 1), :] = (splat(-y[7]) * u).reshape(PLANE, 128)
            else:
                X[rows(x), :] = f.reshape(PLANE, 128)
            return carry

        lax.fori_loop(0, 32, gather_x, 0, unroll=4)
        FS[it, 0] = X[rows(0), :]
        FS[it, 1] = X[rows(31), :]
        faces = []
        for src, dst, dev in ((1, 0, right), (0, 1, left), (3, 2, upper), (2, 3, lower)):
            copy = remote(FS.at[it, src], FR.at[it, dst], sf.at[it, dst], rf.at[it, dst], dev)
            copy.start()
            faces.append(copy)
        sends.extend(faces)
        if it == 0:
            weights_copy.wait()
            for n in range(3):
                jn = lax.rem(j + nj - 1 + n, nj)
                for sx in range(ni):

                    def fill(ty, carry, n=n, sx=sx, at=owner[sx * nj + jn]):
                        wsp[n, sx, ty] = jnp.full((8, 128), cinv_s[at, owner[i * nj + ty]], F32)
                        return carry

                    lax.fori_loop(0, nj, fill, 0, unroll=4)

        else:

            def restore(n, carry):
                field = []
                for x in range(wide):
                    for t in range(4):
                        at = pl.multiple_of((n * wide + x) * PLANE, PLANE) + t * 32
                        field.append(jnp.concatenate([X[pl.ds(at + k * 8, 8), :] for k in range(4)], axis=1))
                field = reorder(jnp.concatenate(field, axis=0), PM[...], True)
                for x in range(wide):
                    for t in range(4):
                        for c in range(4):
                            at = pl.ds((n * wide + x) * 32 + t, 8, stride=4)
                            r = x * 32 + t * 8
                            xpre[c, at, :] = field[r : r + 8, c * 128 : c * 128 + 128]
                return carry

            lax.fori_loop(0, 32 // wide, restore, 0)

        for copy in gather:
            copy.wait_recv()
        sub = lax.broadcasted_iota(jnp.int32, (8, 128), 0) < 4
        for sx in range(ni):

            def term(ty, acc, sx=sx):
                lo, hi, down, up = acc
                g01, g23 = G[it, ty, 0:8, :], G[it, ty, 8:16, :]
                g13 = jnp.where(sub, pltpu.roll(g01, 4, 0), g23)
                g02 = jnp.where(sub, g01, pltpu.roll(g23, 4, 0))
                w = wsp[1, sx, ty]
                return lo + w * g01, hi + w * g23, down + wsp[0, sx, ty] * g13, up + wsp[2, sx, ty] * g02

            lo, hi, down, up = lax.fori_loop(0, nj, term, (zero,) * 4, unroll=8)
            PB[it, sx, 0:8, :] = lo
            PB[it, sx, 8:16, :] = hi
            PB[it, (sx + 1) % ni, 16:24, :] = hi
            PB[it, (sx - 1) % ni, 24:32, :] = lo
            PB[it, sx, 32:40, :] = down
            PB[it, sx, 40:48, :] = up
        R[it, i] = PB[it, i]
        parts = []
        for d in sorted(range(1, ni), key=lambda d: -abs((d // 2 + 2) % 4 - 2)):
            to = lax.rem(i + d, ni)
            copy = remote(PB.at[it, to], R.at[it, i], sr.at[it, d], rr.at[it, d], {"gx": to})
            copy.start()
            sends.append(copy)
            came = R.at[it, lax.rem(i + ni - d, ni)]
            parts.append(remote(PB.at[it, to], came, sr.at[it, d], rr.at[it, d], {"gx": to}))
        for copy in faces:
            copy.wait_recv()
        for copy in parts:
            copy.wait_recv()
        sums = R[it, 0]
        for n in range(1, ni):
            sums = sums + R[it, n]
        own = sums[0:16]
        other = [sums[16 + 8 * n : 24 + 8 * n] for n in range(4)]

        def row(block, c, chunk):
            return block[c * 4 + chunk : c * 4 + chunk + 1, :]

        def along_y(block, c0, c1):
            out = []
            for chunk in range(4):
                p = row(block, c0, chunk)[None, None]
                q = row(block, c1, chunk)[None, None]
                out.append((1.0 - wy) * p + wy * q)
            return jnp.concatenate(out, axis=1)

        def along_x(block, c0, c1):
            out = []
            for chunk in range(4):
                out.append((1.0 - wx8) * row(block, c0, chunk) + wx8 * row(block, c1, chunk))
            return jnp.concatenate(out, axis=0)

        sq = zero
        for n, (fun, c0, c1, sign, has) in enumerate((
            (along_y, 0, 1, -1.0, has_left),
            (along_y, 2, 3, 1.0, has_right),
            (along_x, 0, 2, -1.0, has_lower),
            (along_x, 1, 3, 1.0, has_upper),
        )):
            mine = FS[it, n] + fun(own, c0, c1).reshape(PLANE, 128)
            theirs = FR[it, n] + fun(other[n], 0, 1).reshape(PLANE, 128)
            jump = (mine - theirs) * (sign * has)
            JMP[n] = jump
            if sign > 0:
                sq = sq + jnp.sum((jump * jump).reshape(16, 8, 128), axis=0)
        me = i * nj + j
        row_sum = jnp.sum(sq, axis=0, keepdims=True)
        TS[it] = row_sum
        TR[it, pl.ds(me, 1), :] = row_sum

        for other_one in everyone:
            remote(TS.at[it], TR.at[it, pl.ds(me, 1)], st.at[it], rt.at[it], other_one).start()
        all_but_one = TR.at[it, pl.ds(0, ni * nj - 1)]
        told = remote(all_but_one, all_but_one, st.at[it], rt.at[it], right)
        arrived, sends = sends, [told]
        if it == 0:
            start = along_y(own, 0, 1)
            slope = along_y(own, 2, 3) - start
            m_start = beside_yz(start)
            m_slope = beside_yz(slope)

            def corrected(x, carry):
                wx = x.astype(F32) / 31.0
                e = start + wx * slope
                beside = m_start + wx * m_slope + 2.0 * e
                diag = tiles(U[0, rows(x + 1), :])
                U[1, rows(x + 1), :] = (
                    tiles(U[1, rows(x + 1), :]) - (diag * e - beside)
                ).reshape(PLANE, 128)
                X[rows(x), :] = (tiles(X[rows(x), :]) + e).reshape(PLANE, 128)
                return carry

            lax.fori_loop(0, 32, corrected, 0)
            U[1, rows(1), :] = U[1, rows(1), :] - (start - slope / 31.0).reshape(PLANE, 128)
            U[1, rows(32), :] = U[1, rows(32), :] - (start + slope * (32.0 / 31.0)).reshape(PLANE, 128)
        if it == ITERS - 1:
            faces_in = []
            for ref in (LAM, JMP):
                face = ref[1].reshape(4, 4, 8, 128)
                faces_in.append(jnp.concatenate([face[:, k].reshape(32, 128) for k in range(4)], axis=1))
                faces_in.append(jnp.concatenate([ref[3, pl.ds(k * 32, 32), :] for k in range(4)], axis=1))
            RL[...] = reorder(jnp.concatenate(faces_in, axis=0), PM[...], True)
            CC[...] = jnp.zeros((8, 512), F32)
            for c in range(4):
                for k in range(4):
                    CC[pl.ds(c, 1), pl.ds(k * 128, 128)] = row(own, c, k)
            corr = reorder(CC[...], PM[...], True)
            wy2 = lax.broadcasted_iota(jnp.int32, (32, 128), 0).astype(F32) / 31.0
            for c in range(4):
                c0, c1, c2, c3 = (corr[n : n + 1, c * 128 : c * 128 + 128] for n in range(4))
                begin = (1.0 - wy2) * c0 + wy2 * c1
                end = (1.0 - wy2) * c2 + wy2 * c3

                def add(x, carry, c=c, begin=begin, end=end):
                    wx = x.astype(F32) / 31.0
                    at = pl.ds(pl.multiple_of(x * 32, 32), 32)
                    xpre[c, at, :] = xpre[c, at, :] + ((1.0 - wx) * begin + wx * end)
                    return carry

                lax.fori_loop(0, 32, add, 0, unroll=8)
        for copy in arrived:
            copy.wait_send()
        told.wait_recv()
        total = jnp.sum(TR[it].reshape(ni * nj // 8, 8, 128), axis=0)
        count = (ni - 1) * nj * 32 * 512 + ni * 32 * (nj - 1) * 512
        step = 0.5 / jnp.sqrt(total_of(total) / float(count) + 1e-6)
        if it == 0:
            for n in range(4):
                LAM[n] = (JMP[n].reshape(16, 8, 128) * step[None]).reshape(PLANE, 128)
            U[1, rows(32), :] = U[1, rows(32), :] - LAM[1]
            U[1, rows(1), :] = U[1, rows(1), :] + LAM[0]
            for n, (t, s, sign) in ((3, (3, 7, -1.0)), (2, (0, 0, 1.0))):
                for c in range(4):
                    for h in range(4):
                        at = pl.ds(PLANE + h * 8 * PLANE + t * 32 + c * 8 + s, 8, stride=PLANE)
                        U[1, at, :] = U[1, at, :] + sign * LAM[n, pl.ds(c * 32 + h * 8, 8), :]
        else:
            for c in range(4):
                cols = pl.ds(c * 128, 128)
                for h in range(4):
                    both = RL[pl.ds(h * 8, 8), cols] + step * RL[pl.ds(64 + h * 8, 8), cols]
                    lamx_out[pl.ds(c * 32 + h, 8, stride=4), :] = both
                    both = RL[pl.ds(32 + h * 8, 8), cols] + step * RL[pl.ds(96 + h * 8, 8), cols]
                    lamy_out[pl.ds(c * 32 + h * 8, 8), :] = both
    for copy in sends:
        copy.wait_send()


def finish_kernel(field, lamx, lamy, vel, mx, my, my_s, sems):
    copies = []
    for c in range(4):
        at = pl.ds(c * 128, 128)
        copies.append(pltpu.make_async_copy(field.at[c], vel.at[:, at], sems.at[0, c]))
        copies.append(pltpu.make_async_copy(lamx.at[pl.ds(c * 32, 32)], mx.at[:, at], sems.at[1, c]))
    for copy in copies:
        copy.start()
    for c in range(4):
        my_s[:, :, pl.ds(c * 128, 128)] = lamy[pl.ds(c * 32, 32), :].reshape(32, 1, 128)
    copies.append(pltpu.make_async_copy(my_s, my, sems.at[2, 0]))
    copies[-1].start()
    for copy in copies:
        copy.wait()


def on_device(ni, nj, perm_class, class_drag, force, coarse_inverse, coarse_owner):
    hbm = pl.BlockSpec(memory_space=pl.ANY)
    vmem = pl.BlockSpec(memory_space=pltpu.VMEM)
    smem = pl.BlockSpec(memory_space=pltpu.SMEM)
    dma = pltpu.SemaphoreType.DMA
    xpre, lamx, lamy = pl.pallas_call(
        functools.partial(kernel, ni, nj),
        out_shape=(
            pltpu.VMEM((4, 1024, 128), F32),
            pltpu.VMEM((128, 128), F32),
            pltpu.VMEM((128, 128), F32),
        ),
        in_specs=[hbm, smem, hbm, hbm, smem],
        out_specs=(vmem, vmem, vmem),
        scratch_shapes=[
            pltpu.VMEM((SWEEPS + 2, 34 * PLANE, 128), F32),
            pltpu.VMEM((34 * PLANE, 128), F32),
            pltpu.VMEM((32 * PLANE, 128), F32),
            pltpu.VMEM((4, 1024, 128), F32),
            pltpu.VMEM((4, 1024, 128), jnp.int32),
            pltpu.VMEM((24, 8, 128), F32),
            pltpu.VMEM((3, ni, nj, 8, 128), F32),
            pltpu.SMEM((ni * nj, ni * nj), F32),
            pltpu.VMEM((ITERS, 16, 128), F32),
            pltpu.VMEM((ITERS, nj, 16, 128), F32),
            pltpu.VMEM((ITERS, ni, 48, 128), F32),
            pltpu.VMEM((ITERS, ni, 48, 128), F32),
            pltpu.VMEM((ITERS, 4, PLANE, 128), F32),
            pltpu.VMEM((ITERS, 4, PLANE, 128), F32),
            pltpu.VMEM((ITERS, 1, 128), F32),
            pltpu.VMEM((ITERS, ni * nj, 128), F32),
            pltpu.VMEM((4, PLANE, 128), F32),
            pltpu.VMEM((4, PLANE, 128), F32),
            pltpu.VMEM((512, 512), BF16),
            pltpu.VMEM((8, 512), F32),
            pltpu.VMEM((128, 512), F32),
            dma((4, 8)), dma,
            dma((ITERS, nj)), dma((ITERS, nj)),
            dma((ITERS, ni)), dma((ITERS, ni)),
            dma((ITERS, 4)), dma((ITERS, 4)),
            dma((ITERS,)), dma((ITERS,)),
        ],
        compiler_params=pltpu.CompilerParams(
            collective_id=0, has_side_effects=True, vmem_limit_bytes=56 * 2**20
        ),
        name="solve",
    )(perm_class.reshape(1024, 512), class_drag, force.reshape(1024, 512), coarse_inverse, coarse_owner)
    velocity, mult_x, mult_y = pl.pallas_call(
        finish_kernel,
        out_shape=(
            jax.ShapeDtypeStruct((1024, 512), F32),
            jax.ShapeDtypeStruct((32, 512), F32),
            jax.ShapeDtypeStruct((32, 1, 512), F32),
        ),
        in_specs=[vmem] * 3,
        out_specs=(hbm, hbm, hbm),
        scratch_shapes=[pltpu.VMEM((32, 1, 512), F32), dma((3, 4))],
        compiler_params=pltpu.CompilerParams(vmem_limit_bytes=4 * 2**20),
        name="finish",
    )(xpre, lamx, lamy)
    return velocity.reshape(32, 32, 512), mult_x[None], mult_y


def solution(mesh):
    return jax.shard_map(
        functools.partial(on_device, mesh.shape["gx"], mesh.shape["yz"]),
        mesh=mesh,
        in_specs=(P("gx", "yz", None), P(), P("gx", "yz", None), P(), P()),
        out_specs=(P("gx", "yz", None), P("gx", "yz", None), P("gx", "yz", None)),
        check_vma=False,
    )
```

```python
import functools

import jax
import jax.numpy as jnp
from jax import lax
from jax.experimental import pallas as pl
from jax.experimental.pallas import tpu as pltpu
from jax.sharding import PartitionSpec as P

CLASSES = 8
SWEEPS = 8
ITERS = 2
F32 = jnp.float32
MESH = pl.DeviceIdType.MESH
BF16 = jnp.bfloat16
PLANE = 128
UNROLL = 32


def rows(x):
    return pl.ds(pl.multiple_of(x * PLANE, PLANE), PLANE)


def tiles(value):
    return value.reshape(4, 4, 8, 128)


def beside_yz(cur):
    lane = lax.broadcasted_iota(jnp.int32, (4, 1, 8, 128), 3)
    sub = lax.broadcasted_iota(jnp.int32, (1, 4, 8, 128), 2)
    left = jnp.where(lane == 0, 0.0, pltpu.roll(cur[:, 3:4], 1, 3))
    right = jnp.where(lane == 127, 0.0, pltpu.roll(cur[:, 0:1], 127, 3))
    before = jnp.where(sub == 0, 0.0, pltpu.roll(cur[3:4], 1, 2))
    after = jnp.where(sub == 7, 0.0, pltpu.roll(cur[0:1], 7, 2))
    low = jnp.concatenate([before, cur[0:3]], axis=0)
    high = jnp.concatenate([cur[1:4], after], axis=0)
    nearer = jnp.concatenate([left, cur[:, 0:3]], axis=1)
    further = jnp.concatenate([cur[:, 1:4], right], axis=1)
    return (high + low) + (nearer + further)


def three(a):
    high = a.astype(BF16)
    rest = a - high.astype(F32)
    middle = rest.astype(BF16)
    return high, middle, (rest - middle.astype(F32)).astype(BF16)


def reorder(a, perm, back):
    dims = (((1,), (1 if back else 0,)), ((), ()))
    out = None
    for piece in three(a):
        term = lax.dot_general(piece, perm, dims, preferred_element_type=F32)
        out = term if out is None else out + term
    return out


def total_of(a):
    a = jnp.sum(jnp.sum(a, axis=0, keepdims=True), axis=1, keepdims=True)
    return jnp.broadcast_to(a, (8, 128))


def splat(a):
    return a[None, None]


def part(x, t):
    return pl.ds(pl.multiple_of(x * PLANE, PLANE) + t * 32, 32)


def quad(value):
    return value.reshape(4, 8, 128)


def sweep_pass(k, first, a, b, U, W):
    lane = lax.broadcasted_iota(jnp.int32, (1, 8, 128), 2)
    sub = lax.broadcasted_iota(jnp.int32, (4, 8, 128), 1)

    def fresh(x, t):
        u = quad(W[part(x, t), :]) - a[None] * quad(U[k, part(x, t), :])
        u = u - b[None] * quad(U[k - 1, part(x, t), :])
        U[k + 1, part(x, t), :] = u.reshape(32, 128)
        return u

    def step(x, acc):
        uu, uw = acc
        for t in range(4):
            if first:
                above = quad(U[k + 1, part(x + 2, t), :])
            else:
                above = fresh(x + 2, t)
            cur = quad(U[k + 1, part(x + 1, t), :])
            below = quad(U[k + 1, part(x, t), :])
            low = quad(U[k + 1, part(x + 1, (t + 3) % 4), :])
            high = quad(U[k + 1, part(x + 1, (t + 1) % 4), :])
            if t == 0:
                low = jnp.where(sub == 0, 0.0, pltpu.roll(low, 1, 1))
            if t == 3:
                high = jnp.where(sub == 7, 0.0, pltpu.roll(high, 7, 1))
            left = jnp.where(lane == 0, 0.0, pltpu.roll(cur[3:4], 1, 2))
            right = jnp.where(lane == 127, 0.0, pltpu.roll(cur[0:1], 127, 2))
            left = jnp.concatenate([left, cur[0:3]], axis=0)
            right = jnp.concatenate([cur[1:4], right], axis=0)
            beside = ((above + below) + (high + low)) + (left + right)
            w = quad(U[0, part(x + 1, t), :]) * cur - beside
            W[part(x + 1, t), :] = w.reshape(32, 128)
            uu, uw = uu + cur * cur, uw + cur * w
        return uu, uw

    if not first:
        for t in range(4):
            fresh(1, t)
    zero = jnp.zeros((4, 8, 128), F32)
    uu, uw = lax.fori_loop(0, 32, step, (zero, zero), unroll=UNROLL)
    g = total_of(jnp.sum(uu, axis=0))
    return g, total_of(jnp.sum(uw, axis=0)) / g


def y_weights(width):
    t = lax.broadcasted_iota(jnp.int32, (4, 1, 8, 128), 0)
    s = lax.broadcasted_iota(jnp.int32, (4, 1, 8, 128), 2)
    return (4 * s + t).astype(F32) / (width - 1)


def kernel(
    ni, nj, perm, drag, force, cinv, owner,
    xpre, lamx_out, lamy_out,
    U, W, X, fst, pst, cf, wsp, cinv_s, cbuf, G, PB, R, FS, FR, TS, TR, LAM, JMP, PM, CC, RL,
    in_sem, ci_sem, sg, rg, sr, rr, sf, rf, st, rt,
):
    i = lax.axis_index("gx")
    j = lax.axis_index("yz")
    zero = jnp.zeros((8, 128), F32)
    plane0 = jnp.zeros((PLANE, 128), F32)

    barrier = pltpu.get_barrier_semaphore()

    wide = 8

    def chunk_copies(n):
        at = pl.ds(pl.multiple_of(n * wide * 32, wide * 32), wide * 32)
        out = []
        for c in range(4):
            cols = pl.ds(c * 128, 128)
            out.append(pltpu.make_async_copy(perm.at[at, cols], pst.at[c, at], in_sem.at[n, c]))
            out.append(pltpu.make_async_copy(force.at[at, cols], fst.at[c, at], in_sem.at[n, 4 + c]))
        return out

    for n in range(32 // wide):
        for copy in chunk_copies(n):
            copy.start()
    weights_copy = pltpu.make_async_copy(cinv, cinv_s, ci_sem)
    weights_copy.start()

    for d in range(1, ni):
        pl.semaphore_signal(barrier, inc=1, device_id={"gx": lax.rem(i + d, ni)}, device_id_type=MESH)
    for d in range(1, nj):
        pl.semaphore_signal(barrier, inc=1, device_id={"yz": lax.rem(j + d, nj)}, device_id_type=MESH)

    for k in range(SWEEPS + 2):
        U[k, rows(0), :] = plane0
        U[k, rows(33), :] = plane0
    W[rows(33), :] = plane0

    for n in range(4):
        zin = lax.broadcasted_iota(jnp.int32, (512, 128), 0)
        lane = lax.broadcasted_iota(jnp.int32, (512, 128), 1)
        PM[:, pl.ds(n * 128, 128)] = jnp.where(zin == 4 * lane + n, 1.0, 0.0).astype(BF16)

    lane8 = lax.broadcasted_iota(jnp.int32, (8, 128), 1)
    level = zero
    for c in range(CLASSES):
        level = jnp.where(lane8 == c, 6.0 + drag[c], level)

    def stage(n, carry):
        for copy in chunk_copies(n):
            copy.wait()
        perm_matrix = PM[...]

        def gathered(ref):
            out = []
            for x in range(wide):
                for t in range(4):
                    at = pl.ds(n * wide * 32 + x * 32 + t, 8, stride=4)
                    out.append(jnp.concatenate([ref[c, at, :] for c in range(4)], axis=1))
            return jnp.concatenate(out, axis=0)

        pieces = (gathered(pst).astype(F32).astype(BF16),) + three(gathered(fst))
        size = wide * 32
        moved = jnp.dot(jnp.concatenate(pieces, axis=0), perm_matrix, preferred_element_type=F32)
        classes = moved[0:size]
        field = moved[size : 2 * size] + moved[2 * size : 3 * size] + moved[3 * size : 4 * size]
        for x in range(wide):
            for t in range(4):
                for k in range(4):
                    r, l = slice(x * 32 + t * 8, x * 32 + t * 8 + 8), slice(k * 128, k * 128 + 128)
                    at = pl.ds(pl.multiple_of((n * wide + x + 1) * PLANE, PLANE) + t * 32 + k * 8, 8)
                    cls = classes[r, l].astype(jnp.int32)
                    U[0, at, :] = jnp.take_along_axis(level, cls, axis=1, mode="promise_in_bounds")
                    U[1, at, :] = field[r, l]
        return carry

    lax.fori_loop(0, 32 // wide, stage, 0)

    has_right = (i < ni - 1).astype(F32)
    has_left = (i > 0).astype(F32)
    has_upper = (j < nj - 1).astype(F32)
    has_lower = (j > 0).astype(F32)
    wy = y_weights(32)
    wx8 = lax.broadcasted_iota(jnp.int32, (32, 128), 0).astype(F32) / 31.0
    right, left = {"gx": lax.rem(i + 1, ni)}, {"gx": lax.rem(i + ni - 1, ni)}
    upper, lower = {"yz": lax.rem(j + 1, nj)}, {"yz": lax.rem(j + nj - 1, nj)}
    ring = (2, 1, 3, 0)
    gx_of = [lax.rem(i // 2 + ax, ni // 2) * 2 + lax.rem(i % 2 + core, 2) for ax in ring[-ni // 2 :] for core in (1, 0)]
    yz_of = [lax.rem(j // 4 + az, nj // 4) * 4 + lax.rem(j % 4 + ay, 4) for az in ring[-nj // 4 :] for ay in ring]
    far = []
    for p in range(ni):
        for q in range(nj):
            hops = sum((2, 1, 1, 0)[n] for n in (p // 2, q // 4, q % 4))
            far.append((-hops, p, q))
    everyone = [{"gx": gx_of[p], "yz": yz_of[q]} for _, p, q in sorted(far)[:-1] if (p, q) != (ni - 1, nj - 1)]
    sends = []

    def remote(src, dst, ssem, rsem, dev):
        return pltpu.make_async_remote_copy(
            src_ref=src, dst_ref=dst, send_sem=ssem, recv_sem=rsem, device_id=dev, device_id_type=MESH
        )

    for it in range(ITERS):
        g, a = sweep_pass(0, True, zero, zero, U, W)
        one = jnp.ones((8, 128), F32)

        def body(k, carry):
            g, a, b, pivot, z = carry
            inv = 1.0 / (a - b * pivot)
            cf[k - 1] = inv
            cf[7 + k] = b
            cf[15 + k] = z
            gn, an = sweep_pass(k, False, a, b, U, W)
            return gn, an, gn / g, inv, -z * inv

        g, a, b, pivot, z = lax.fori_loop(1, SWEEPS, body, (g, a, zero, zero, one))

        y = [None] * SWEEPS
        y[SWEEPS - 1] = z / (a - b * pivot)
        above = b
        for k in range(SWEEPS - 2, -1, -1):
            y[k] = (cf[16 + k] - above * y[k + 1]) * cf[k]
            above = cf[8 + k]

        for n, x in ((0, 0), (1, 31)):
            for m, (t, r) in enumerate(((0, 0), (3, 7))):
                for c in range(4):
                    at = t * 32 + c * 8
                    f = None if it == 0 else X[pl.ds(x * PLANE + at, 8), :]
                    for k in range(SWEEPS):
                        term = y[k] * U[k + 1, pl.ds((x + 1) * PLANE + at, 8), :]
                        f = term if f is None else f + term
                    cbuf[it, pl.ds((2 * n + m) * 4 + c, 1), :] = f[r : r + 1, :]
        G[it, j] = cbuf[it]
        if it == 0:
            pl.semaphore_wait(barrier, ni + nj - 2)
        gather = []
        for d in sorted(range(1, nj), key=lambda d: -abs((d + 2) % 4 - 2) - abs((d // 4 + 2) % 4 - 2)):
            dev = {"yz": lax.rem(j + d, nj)}
            copy = remote(cbuf.at[it], G.at[it, j], sg.at[it, d], rg.at[it, d], dev)
            copy.start()
            sends.append(copy)
            came = G.at[it, lax.rem(j + nj - d, nj)]
            gather.append(remote(cbuf.at[it], came, sg.at[it, d], rg.at[it, d], dev))
        def gather_x(x, carry):
            f = None if it == 0 else tiles(X[rows(x), :])
            for k in range(SWEEPS):
                term = splat(y[k]) * tiles(U[k + 1, rows(x + 1), :])
                f = term if f is None else f + term
            for c in range(4):
                FS[it, 2, pl.ds(c * 32 + x, 1), :] = f[0, c, 0:1, :]
                FS[it, 3, pl.ds(c * 32 + x, 1), :] = f[3, c, 7:8, :]
            if it == 0:
                X[rows(x), :] = f.reshape(PLANE, 128)
                u = tiles(W[rows(x + 1), :]) - splat(a) * tiles(U[8, rows(x + 1), :])
                u = u - splat(b) * tiles(U[7, rows(x + 1), :])
                U[1, rows(x + 1), :] = (splat(-y[7]) * u).reshape(PLANE, 128)
            else:
                X[rows(x), :] = f.reshape(PLANE, 128)
            return carry

        lax.fori_loop(0, 32, gather_x, 0, unroll=4)
        FS[it, 0] = X[rows(0), :]
        FS[it, 1] = X[rows(31), :]
        faces = []
        for src, dst, dev in ((1, 0, right), (0, 1, left), (3, 2, upper), (2, 3, lower)):
            copy = remote(FS.at[it, src], FR.at[it, dst], sf.at[it, dst], rf.at[it, dst], dev)
            copy.start()
            faces.append(copy)
        sends.extend(faces)
        if it == 0:
            weights_copy.wait()
            for n in range(3):
                jn = lax.rem(j + nj - 1 + n, nj)
                for sx in range(ni):

                    def fill(ty, carry, n=n, sx=sx, at=owner[sx * nj + jn]):
                        wsp[n, sx, ty] = jnp.full((8, 128), cinv_s[at, owner[i * nj + ty]], F32)
                        return carry

                    lax.fori_loop(0, nj, fill, 0, unroll=4)

        else:

            def restore(n, carry):
                field = []
                for x in range(wide):
                    for t in range(4):
                        at = pl.multiple_of((n * wide + x) * PLANE, PLANE) + t * 32
                        field.append(jnp.concatenate([X[pl.ds(at + k * 8, 8), :] for k in range(4)], axis=1))
                field = reorder(jnp.concatenate(field, axis=0), PM[...], True)
                for x in range(wide):
                    for t in range(4):
                        for c in range(4):
                            at = pl.ds((n * wide + x) * 32 + t, 8, stride=4)
                            r = x * 32 + t * 8
                            xpre[c, at, :] = field[r : r + 8, c * 128 : c * 128 + 128]
                return carry

            lax.fori_loop(0, 32 // wide, restore, 0)

        for copy in gather:
            copy.wait_recv()
        sub = lax.broadcasted_iota(jnp.int32, (8, 128), 0) < 4
        for sx in range(ni):

            def term(ty, acc, sx=sx):
                lo, hi, down, up = acc
                g01, g23 = G[it, ty, 0:8, :], G[it, ty, 8:16, :]
                g13 = jnp.where(sub, pltpu.roll(g01, 4, 0), g23)
                g02 = jnp.where(sub, g01, pltpu.roll(g23, 4, 0))
                w = wsp[1, sx, ty]
                return lo + w * g01, hi + w * g23, down + wsp[0, sx, ty] * g13, up + wsp[2, sx, ty] * g02

            lo, hi, down, up = lax.fori_loop(0, nj, term, (zero,) * 4, unroll=8)
            PB[it, sx, 0:8, :] = lo
            PB[it, sx, 8:16, :] = hi
            PB[it, (sx + 1) % ni, 16:24, :] = hi
            PB[it, (sx - 1) % ni, 24:32, :] = lo
            PB[it, sx, 32:40, :] = down
            PB[it, sx, 40:48, :] = up
        R[it, i] = PB[it, i]
        parts = []
        for d in sorted(range(1, ni), key=lambda d: -abs((d // 2 + 2) % 4 - 2)):
            to = lax.rem(i + d, ni)
            copy = remote(PB.at[it, to], R.at[it, i], sr.at[it, d], rr.at[it, d], {"gx": to})
            copy.start()
            sends.append(copy)
            came = R.at[it, lax.rem(i + ni - d, ni)]
            parts.append(remote(PB.at[it, to], came, sr.at[it, d], rr.at[it, d], {"gx": to}))
        for copy in faces:
            copy.wait_recv()
        for copy in parts:
            copy.wait_recv()
        sums = R[it, 0]
        for n in range(1, ni):
            sums = sums + R[it, n]
        own = sums[0:16]
        other = [sums[16 + 8 * n : 24 + 8 * n] for n in range(4)]

        def row(block, c, chunk):
            return block[c * 4 + chunk : c * 4 + chunk + 1, :]

        def along_y(block, c0, c1):
            out = []
            for chunk in range(4):
                p = row(block, c0, chunk)[None, None]
                q = row(block, c1, chunk)[None, None]
                out.append((1.0 - wy) * p + wy * q)
            return jnp.concatenate(out, axis=1)

        def along_x(block, c0, c1):
            out = []
            for chunk in range(4):
                out.append((1.0 - wx8) * row(block, c0, chunk) + wx8 * row(block, c1, chunk))
            return jnp.concatenate(out, axis=0)

        sq = zero
        for n, (fun, c0, c1, sign, has) in enumerate((
            (along_y, 0, 1, -1.0, has_left),
            (along_y, 2, 3, 1.0, has_right),
            (along_x, 0, 2, -1.0, has_lower),
            (along_x, 1, 3, 1.0, has_upper),
        )):
            mine = FS[it, n] + fun(own, c0, c1).reshape(PLANE, 128)
            theirs = FR[it, n] + fun(other[n], 0, 1).reshape(PLANE, 128)
            jump = (mine - theirs) * (sign * has)
            JMP[n] = jump
            if sign > 0:
                sq = sq + jnp.sum((jump * jump).reshape(16, 8, 128), axis=0)
        me = i * nj + j
        row_sum = jnp.sum(sq, axis=0, keepdims=True)
        TS[it] = row_sum
        TR[it, pl.ds(me, 1), :] = row_sum

        for other_one in everyone:
            remote(TS.at[it], TR.at[it, pl.ds(me, 1)], st.at[it], rt.at[it], other_one).start()
        all_but_one = TR.at[it, pl.ds(0, ni * nj - 1)]
        told = remote(all_but_one, all_but_one, st.at[it], rt.at[it], right)
        arrived, sends = sends, [told]
        if it == 0:
            start = along_y(own, 0, 1)
            slope = along_y(own, 2, 3) - start
            m_start = beside_yz(start)
            m_slope = beside_yz(slope)

            def corrected(x, carry):
                wx = x.astype(F32) / 31.0
                e = start + wx * slope
                beside = m_start + wx * m_slope + 2.0 * e
                diag = tiles(U[0, rows(x + 1), :])
                U[1, rows(x + 1), :] = (
                    tiles(U[1, rows(x + 1), :]) - (diag * e - beside)
                ).reshape(PLANE, 128)
                X[rows(x), :] = (tiles(X[rows(x), :]) + e).reshape(PLANE, 128)
                return carry

            lax.fori_loop(0, 32, corrected, 0)
            U[1, rows(1), :] = U[1, rows(1), :] - (start - slope / 31.0).reshape(PLANE, 128)
            U[1, rows(32), :] = U[1, rows(32), :] - (start + slope * (32.0 / 31.0)).reshape(PLANE, 128)
        if it == ITERS - 1:
            faces_in = []
            for ref in (LAM, JMP):
                face = ref[1].reshape(4, 4, 8, 128)
                faces_in.append(jnp.concatenate([face[:, k].reshape(32, 128) for k in range(4)], axis=1))
                faces_in.append(jnp.concatenate([ref[3, pl.ds(k * 32, 32), :] for k in range(4)], axis=1))
            RL[...] = reorder(jnp.concatenate(faces_in, axis=0), PM[...], True)
            CC[...] = jnp.zeros((8, 512), F32)
            for c in range(4):
                for k in range(4):
                    CC[pl.ds(c, 1), pl.ds(k * 128, 128)] = row(own, c, k)
            corr = reorder(CC[...], PM[...], True)
            wy2 = lax.broadcasted_iota(jnp.int32, (32, 128), 0).astype(F32) / 31.0
            for c in range(4):
                c0, c1, c2, c3 = (corr[n : n + 1, c * 128 : c * 128 + 128] for n in range(4))
                begin = (1.0 - wy2) * c0 + wy2 * c1
                end = (1.0 - wy2) * c2 + wy2 * c3

                def add(x, carry, c=c, begin=begin, end=end):
                    wx = x.astype(F32) / 31.0
                    at = pl.ds(pl.multiple_of(x * 32, 32), 32)
                    xpre[c, at, :] = xpre[c, at, :] + ((1.0 - wx) * begin + wx * end)
                    return carry

                lax.fori_loop(0, 32, add, 0, unroll=8)
        for copy in arrived:
            copy.wait_send()
        told.wait_recv()
        total = jnp.sum(TR[it].reshape(ni * nj // 8, 8, 128), axis=0)
        count = (ni - 1) * nj * 32 * 512 + ni * 32 * (nj - 1) * 512
        step = 0.5 / jnp.sqrt(total_of(total) / float(count) + 1e-6)
        if it == 0:
            for n in range(4):
                LAM[n] = (JMP[n].reshape(16, 8, 128) * step[None]).reshape(PLANE, 128)
            U[1, rows(32), :] = U[1, rows(32), :] - LAM[1]
            U[1, rows(1), :] = U[1, rows(1), :] + LAM[0]
            for n, (t, s, sign) in ((3, (3, 7, -1.0)), (2, (0, 0, 1.0))):
                for c in range(4):
                    for h in range(4):
                        at = pl.ds(PLANE + h * 8 * PLANE + t * 32 + c * 8 + s, 8, stride=PLANE)
                        U[1, at, :] = U[1, at, :] + sign * LAM[n, pl.ds(c * 32 + h * 8, 8), :]
        else:
            for c in range(4):
                cols = pl.ds(c * 128, 128)
                for h in range(4):
                    both = RL[pl.ds(h * 8, 8), cols] + step * RL[pl.ds(64 + h * 8, 8), cols]
                    lamx_out[pl.ds(c * 32 + h, 8, stride=4), :] = both
                    both = RL[pl.ds(32 + h * 8, 8), cols] + step * RL[pl.ds(96 + h * 8, 8), cols]
                    lamy_out[pl.ds(c * 32 + h * 8, 8), :] = both
    for copy in sends:
        copy.wait_send()


def finish_kernel(field, lamx, lamy, vel, mx, my, my_s, sems):
    copies = []
    for c in range(4):
        at = pl.ds(c * 128, 128)
        copies.append(pltpu.make_async_copy(field.at[c], vel.at[:, at], sems.at[0, c]))
        copies.append(pltpu.make_async_copy(lamx.at[pl.ds(c * 32, 32)], mx.at[:, at], sems.at[1, c]))
    for copy in copies:
        copy.start()
    for c in range(4):
        my_s[:, :, pl.ds(c * 128, 128)] = lamy[pl.ds(c * 32, 32), :].reshape(32, 1, 128)
    copies.append(pltpu.make_async_copy(my_s, my, sems.at[2, 0]))
    copies[-1].start()
    for copy in copies:
        copy.wait()


def on_device(ni, nj, perm_class, class_drag, force, coarse_inverse, coarse_owner):
    hbm = pl.BlockSpec(memory_space=pl.ANY)
    vmem = pl.BlockSpec(memory_space=pltpu.VMEM)
    smem = pl.BlockSpec(memory_space=pltpu.SMEM)
    dma = pltpu.SemaphoreType.DMA
    xpre, lamx, lamy = pl.pallas_call(
        functools.partial(kernel, ni, nj),
        out_shape=(
            pltpu.VMEM((4, 1024, 128), F32),
            pltpu.VMEM((128, 128), F32),
            pltpu.VMEM((128, 128), F32),
        ),
        in_specs=[hbm, smem, hbm, hbm, smem],
        out_specs=(vmem, vmem, vmem),
        scratch_shapes=[
            pltpu.VMEM((SWEEPS + 2, 34 * PLANE, 128), F32),
            pltpu.VMEM((34 * PLANE, 128), F32),
            pltpu.VMEM((32 * PLANE, 128), F32),
            pltpu.VMEM((4, 1024, 128), F32),
            pltpu.VMEM((4, 1024, 128), jnp.int32),
            pltpu.VMEM((24, 8, 128), F32),
            pltpu.VMEM((3, ni, nj, 8, 128), F32),
            pltpu.SMEM((ni * nj, ni * nj), F32),
            pltpu.VMEM((ITERS, 16, 128), F32),
            pltpu.VMEM((ITERS, nj, 16, 128), F32),
            pltpu.VMEM((ITERS, ni, 48, 128), F32),
            pltpu.VMEM((ITERS, ni, 48, 128), F32),
            pltpu.VMEM((ITERS, 4, PLANE, 128), F32),
            pltpu.VMEM((ITERS, 4, PLANE, 128), F32),
            pltpu.VMEM((ITERS, 1, 128), F32),
            pltpu.VMEM((ITERS, ni * nj, 128), F32),
            pltpu.VMEM((4, PLANE, 128), F32),
            pltpu.VMEM((4, PLANE, 128), F32),
            pltpu.VMEM((512, 512), BF16),
            pltpu.VMEM((8, 512), F32),
            pltpu.VMEM((128, 512), F32),
            dma((4, 8)), dma,
            dma((ITERS, nj)), dma((ITERS, nj)),
            dma((ITERS, ni)), dma((ITERS, ni)),
            dma((ITERS, 4)), dma((ITERS, 4)),
            dma((ITERS,)), dma((ITERS,)),
        ],
        compiler_params=pltpu.CompilerParams(
            collective_id=0, has_side_effects=True, vmem_limit_bytes=56 * 2**20
        ),
        name="solve",
    )(perm_class.reshape(1024, 512), class_drag, force.reshape(1024, 512), coarse_inverse, coarse_owner)
    velocity, mult_x, mult_y = pl.pallas_call(
        finish_kernel,
        out_shape=(
            jax.ShapeDtypeStruct((1024, 512), F32),
            jax.ShapeDtypeStruct((32, 512), F32),
            jax.ShapeDtypeStruct((32, 1, 512), F32),
        ),
        in_specs=[vmem] * 3,
        out_specs=(hbm, hbm, hbm),
        scratch_shapes=[pltpu.VMEM((32, 1, 512), F32), dma((3, 4))],
        compiler_params=pltpu.CompilerParams(vmem_limit_bytes=4 * 2**20),
        name="finish",
    )(xpre, lamx, lamy)
    return velocity.reshape(32, 32, 512), mult_x[None], mult_y


def solution(mesh):
    return jax.shard_map(
        functools.partial(on_device, mesh.shape["gx"], mesh.shape["yz"]),
        mesh=mesh,
        in_specs=(P("gx", "yz", None), P(), P("gx", "yz", None), P(), P()),
        out_specs=(P("gx", "yz", None), P("gx", "yz", None), P("gx", "yz", None)),
        check_vma=False,
    )
```

```python
import functools

import jax
import jax.numpy as jnp
from jax import lax
from jax.experimental import pallas as pl
from jax.experimental.pallas import tpu as pltpu
from jax.sharding import PartitionSpec as P

CLASSES = 8
SWEEPS = 8
ITERS = 2
F32 = jnp.float32
MESH = pl.DeviceIdType.MESH
BF16 = jnp.bfloat16
PLANE = 128
UNROLL = 32


def rows(x):
    return pl.ds(pl.multiple_of(x * PLANE, PLANE), PLANE)


def tiles(value):
    return value.reshape(4, 4, 8, 128)


def beside_yz(cur):
    lane = lax.broadcasted_iota(jnp.int32, (4, 1, 8, 128), 3)
    sub = lax.broadcasted_iota(jnp.int32, (1, 4, 8, 128), 2)
    left = jnp.where(lane == 0, 0.0, pltpu.roll(cur[:, 3:4], 1, 3))
    right = jnp.where(lane == 127, 0.0, pltpu.roll(cur[:, 0:1], 127, 3))
    before = jnp.where(sub == 0, 0.0, pltpu.roll(cur[3:4], 1, 2))
    after = jnp.where(sub == 7, 0.0, pltpu.roll(cur[0:1], 7, 2))
    low = jnp.concatenate([before, cur[0:3]], axis=0)
    high = jnp.concatenate([cur[1:4], after], axis=0)
    nearer = jnp.concatenate([left, cur[:, 0:3]], axis=1)
    further = jnp.concatenate([cur[:, 1:4], right], axis=1)
    return (high + low) + (nearer + further)


def three(a):
    high = a.astype(BF16)
    rest = a - high.astype(F32)
    middle = rest.astype(BF16)
    return high, middle, (rest - middle.astype(F32)).astype(BF16)


def reorder(a, perm, back):
    dims = (((1,), (1 if back else 0,)), ((), ()))
    out = None
    for piece in three(a):
        term = lax.dot_general(piece, perm, dims, preferred_element_type=F32)
        out = term if out is None else out + term
    return out


def total_of(a):
    a = jnp.sum(jnp.sum(a, axis=0, keepdims=True), axis=1, keepdims=True)
    return jnp.broadcast_to(a, (8, 128))


def splat(a):
    return a[None, None]


def part(x, t):
    return pl.ds(pl.multiple_of(x * PLANE, PLANE) + t * 32, 32)


def quad(value):
    return value.reshape(4, 8, 128)


def sweep_pass(k, first, a, b, U, W):
    lane = lax.broadcasted_iota(jnp.int32, (1, 8, 128), 2)
    sub = lax.broadcasted_iota(jnp.int32, (4, 8, 128), 1)

    def fresh(x, t):
        u = quad(W[part(x, t), :]) - a[None] * quad(U[k, part(x, t), :])
        u = u - b[None] * quad(U[k - 1, part(x, t), :])
        U[k + 1, part(x, t), :] = u.reshape(32, 128)
        return u

    def step(x, acc):
        uu, uw = acc
        for t in range(4):
            if first:
                above = quad(U[k + 1, part(x + 2, t), :])
            else:
                above = fresh(x + 2, t)
            cur = quad(U[k + 1, part(x + 1, t), :])
            below = quad(U[k + 1, part(x, t), :])
            low = quad(U[k + 1, part(x + 1, (t + 3) % 4), :])
            high = quad(U[k + 1, part(x + 1, (t + 1) % 4), :])
            if t == 0:
                low = jnp.where(sub == 0, 0.0, pltpu.roll(low, 1, 1))
            if t == 3:
                high = jnp.where(sub == 7, 0.0, pltpu.roll(high, 7, 1))
            edge_l = pltpu.roll(jnp.where(lane == 127, 0.0, cur[3:4]), 1, 2)
            edge_r = pltpu.roll(jnp.where(lane == 0, 0.0, cur[0:1]), 127, 2)
            left = jnp.concatenate([edge_l, cur[0:3]], axis=0)
            right = jnp.concatenate([cur[1:4], edge_r], axis=0)
            beside = ((above + below) + (high + low)) + (left + right)
            w = quad(U[0, part(x + 1, t), :]) * cur - beside
            W[part(x + 1, t), :] = w.reshape(32, 128)
            uu, uw = uu + cur * cur, uw + cur * w
        return uu, uw

    if not first:
        for t in range(4):
            fresh(1, t)
    zero = jnp.zeros((4, 8, 128), F32)
    uu, uw = lax.fori_loop(0, 32, step, (zero, zero), unroll=UNROLL)
    g = total_of(jnp.sum(uu, axis=0))
    return g, total_of(jnp.sum(uw, axis=0)) / g


def y_weights(width):
    t = lax.broadcasted_iota(jnp.int32, (4, 1, 8, 128), 0)
    s = lax.broadcasted_iota(jnp.int32, (4, 1, 8, 128), 2)
    return (4 * s + t).astype(F32) / (width - 1)


def kernel(
    ni, nj, perm, drag, force, cinv, owner,
    xpre, lamx_out, lamy_out,
    U, W, X, fst, pst, cf, wsp, cinv_s, cbuf, G, PB, R, FS, FR, TS, TR, LAM, JMP, PM, CC, RL,
    in_sem, ci_sem, sg, rg, sr, rr, sf, rf, st, rt,
):
    i = lax.axis_index("gx")
    j = lax.axis_index("yz")
    zero = jnp.zeros((8, 128), F32)
    plane0 = jnp.zeros((PLANE, 128), F32)

    barrier = pltpu.get_barrier_semaphore()

    wide = 8

    def chunk_copies(n):
        at = pl.ds(pl.multiple_of(n * wide * 32, wide * 32), wide * 32)
        out = []
        for c in range(4):
            cols = pl.ds(c * 128, 128)
            out.append(pltpu.make_async_copy(perm.at[at, cols], pst.at[c, at], in_sem.at[n, c]))
            out.append(pltpu.make_async_copy(force.at[at, cols], fst.at[c, at], in_sem.at[n, 4 + c]))
        return out

    for n in range(32 // wide):
        for copy in chunk_copies(n):
            copy.start()
    weights_copy = pltpu.make_async_copy(cinv, cinv_s, ci_sem)
    weights_copy.start()

    for d in range(1, ni):
        pl.semaphore_signal(barrier, inc=1, device_id={"gx": lax.rem(i + d, ni)}, device_id_type=MESH)
    for d in range(1, nj):
        pl.semaphore_signal(barrier, inc=1, device_id={"yz": lax.rem(j + d, nj)}, device_id_type=MESH)

    for k in range(SWEEPS + 2):
        U[k, rows(0), :] = plane0
        U[k, rows(33), :] = plane0
    W[rows(33), :] = plane0

    for n in range(4):
        zin = lax.broadcasted_iota(jnp.int32, (512, 128), 0)
        lane = lax.broadcasted_iota(jnp.int32, (512, 128), 1)
        PM[:, pl.ds(n * 128, 128)] = jnp.where(zin == 4 * lane + n, 1.0, 0.0).astype(BF16)

    lane8 = lax.broadcasted_iota(jnp.int32, (8, 128), 1)
    level = zero
    for c in range(CLASSES):
        level = jnp.where(lane8 == c, 6.0 + drag[c], level)

    def stage(n, carry):
        for copy in chunk_copies(n):
            copy.wait()
        perm_matrix = PM[...]

        def gathered(ref):
            out = []
            for x in range(wide):
                for t in range(4):
                    at = pl.ds(n * wide * 32 + x * 32 + t, 8, stride=4)
                    out.append(jnp.concatenate([ref[c, at, :] for c in range(4)], axis=1))
            return jnp.concatenate(out, axis=0)

        pieces = (gathered(pst).astype(F32).astype(BF16),) + three(gathered(fst))
        size = wide * 32
        moved = jnp.dot(jnp.concatenate(pieces, axis=0), perm_matrix, preferred_element_type=F32)
        classes = moved[0:size]
        field = moved[size : 2 * size] + moved[2 * size : 3 * size] + moved[3 * size : 4 * size]
        for x in range(wide):
            for t in range(4):
                for k in range(4):
                    r, l = slice(x * 32 + t * 8, x * 32 + t * 8 + 8), slice(k * 128, k * 128 + 128)
                    at = pl.ds(pl.multiple_of((n * wide + x + 1) * PLANE, PLANE) + t * 32 + k * 8, 8)
                    cls = classes[r, l].astype(jnp.int32)
                    U[0, at, :] = jnp.take_along_axis(level, cls, axis=1, mode="promise_in_bounds")
                    U[1, at, :] = field[r, l]
        return carry

    lax.fori_loop(0, 32 // wide, stage, 0)

    has_right = (i < ni - 1).astype(F32)
    has_left = (i > 0).astype(F32)
    has_upper = (j < nj - 1).astype(F32)
    has_lower = (j > 0).astype(F32)
    wy = y_weights(32)
    wx8 = lax.broadcasted_iota(jnp.int32, (32, 128), 0).astype(F32) / 31.0
    right, left = {"gx": lax.rem(i + 1, ni)}, {"gx": lax.rem(i + ni - 1, ni)}
    upper, lower = {"yz": lax.rem(j + 1, nj)}, {"yz": lax.rem(j + nj - 1, nj)}
    ring = (2, 1, 3, 0)
    gx_of = [lax.rem(i // 2 + ax, ni // 2) * 2 + lax.rem(i % 2 + core, 2) for ax in ring[-ni // 2 :] for core in (1, 0)]
    yz_of = [lax.rem(j // 4 + az, nj // 4) * 4 + lax.rem(j % 4 + ay, 4) for az in ring[-nj // 4 :] for ay in ring]
    far = []
    for p in range(ni):
        for q in range(nj):
            hops = sum((2, 1, 1, 0)[n] for n in (p // 2, q // 4, q % 4))
            far.append((-hops, p, q))
    everyone = [{"gx": gx_of[p], "yz": yz_of[q]} for _, p, q in sorted(far)[:-1] if (p, q) != (ni - 1, nj - 1)]
    sends = []

    def remote(src, dst, ssem, rsem, dev):
        return pltpu.make_async_remote_copy(
            src_ref=src, dst_ref=dst, send_sem=ssem, recv_sem=rsem, device_id=dev, device_id_type=MESH
        )

    for it in range(ITERS):
        g, a = sweep_pass(0, True, zero, zero, U, W)
        one = jnp.ones((8, 128), F32)

        def body(k, carry):
            g, a, b, pivot, z = carry
            inv = 1.0 / (a - b * pivot)
            cf[k - 1] = inv
            cf[7 + k] = b
            cf[15 + k] = z
            gn, an = sweep_pass(k, False, a, b, U, W)
            return gn, an, gn / g, inv, -z * inv

        g, a, b, pivot, z = lax.fori_loop(1, SWEEPS, body, (g, a, zero, zero, one))

        y = [None] * SWEEPS
        y[SWEEPS - 1] = z / (a - b * pivot)
        above = b
        for k in range(SWEEPS - 2, -1, -1):
            y[k] = (cf[16 + k] - above * y[k + 1]) * cf[k]
            above = cf[8 + k]

        for n, x in ((0, 0), (1, 31)):
            for m, (t, r) in enumerate(((0, 0), (3, 7))):
                for c in range(4):
                    at = t * 32 + c * 8
                    f = None if it == 0 else X[pl.ds(x * PLANE + at, 8), :]
                    for k in range(SWEEPS):
                        term = y[k] * U[k + 1, pl.ds((x + 1) * PLANE + at, 8), :]
                        f = term if f is None else f + term
                    cbuf[it, pl.ds((2 * n + m) * 4 + c, 1), :] = f[r : r + 1, :]
        G[it, j] = cbuf[it]
        if it == 0:
            pl.semaphore_wait(barrier, ni + nj - 2)
        gather = []
        for d in sorted(range(1, nj), key=lambda d: -abs((d + 2) % 4 - 2) - abs((d // 4 + 2) % 4 - 2)):
            dev = {"yz": lax.rem(j + d, nj)}
            copy = remote(cbuf.at[it], G.at[it, j], sg.at[it, d], rg.at[it, d], dev)
            copy.start()
            sends.append(copy)
            came = G.at[it, lax.rem(j + nj - d, nj)]
            gather.append(remote(cbuf.at[it], came, sg.at[it, d], rg.at[it, d], dev))
        def gather_x(x, carry):
            f = None if it == 0 else tiles(X[rows(x), :])
            for k in range(SWEEPS):
                term = splat(y[k]) * tiles(U[k + 1, rows(x + 1), :])
                f = term if f is None else f + term
            for c in range(4):
                FS[it, 2, pl.ds(c * 32 + x, 1), :] = f[0, c, 0:1, :]
                FS[it, 3, pl.ds(c * 32 + x, 1), :] = f[3, c, 7:8, :]
            if it == 0:
                X[rows(x), :] = f.reshape(PLANE, 128)
                u = tiles(W[rows(x + 1), :]) - splat(a) * tiles(U[8, rows(x + 1), :])
                u = u - splat(b) * tiles(U[7, rows(x + 1), :])
                U[1, rows(x + 1), :] = (splat(-y[7]) * u).reshape(PLANE, 128)
            else:
                X[rows(x), :] = f.reshape(PLANE, 128)
            return carry

        lax.fori_loop(0, 32, gather_x, 0, unroll=4)
        FS[it, 0] = X[rows(0), :]
        FS[it, 1] = X[rows(31), :]
        faces = []
        for src, dst, dev in ((1, 0, right), (0, 1, left), (3, 2, upper), (2, 3, lower)):
            copy = remote(FS.at[it, src], FR.at[it, dst], sf.at[it, dst], rf.at[it, dst], dev)
            copy.start()
            faces.append(copy)
        sends.extend(faces)
        if it == 0:
            weights_copy.wait()
            for n in range(3):
                jn = lax.rem(j + nj - 1 + n, nj)
                for sx in range(ni):

                    def fill(ty, carry, n=n, sx=sx, at=owner[sx * nj + jn]):
                        wsp[n, sx, ty] = jnp.full((8, 128), cinv_s[at, owner[i * nj + ty]], F32)
                        return carry

                    lax.fori_loop(0, nj, fill, 0, unroll=4)

        else:

            def restore(n, carry):
                field = []
                for x in range(wide):
                    for t in range(4):
                        at = pl.multiple_of((n * wide + x) * PLANE, PLANE) + t * 32
                        field.append(jnp.concatenate([X[pl.ds(at + k * 8, 8), :] for k in range(4)], axis=1))
                field = reorder(jnp.concatenate(field, axis=0), PM[...], True)
                for x in range(wide):
                    for t in range(4):
                        for c in range(4):
                            at = pl.ds((n * wide + x) * 32 + t, 8, stride=4)
                            r = x * 32 + t * 8
                            xpre[c, at, :] = field[r : r + 8, c * 128 : c * 128 + 128]
                return carry

            lax.fori_loop(0, 32 // wide, restore, 0)

        for copy in gather:
            copy.wait_recv()
        sub = lax.broadcasted_iota(jnp.int32, (8, 128), 0) < 4
        for sx in range(ni):

            def term(ty, acc, sx=sx):
                lo, hi, down, up = acc
                g01, g23 = G[it, ty, 0:8, :], G[it, ty, 8:16, :]
                g13 = jnp.where(sub, pltpu.roll(g01, 4, 0), g23)
                g02 = jnp.where(sub, g01, pltpu.roll(g23, 4, 0))
                w = wsp[1, sx, ty]
                return lo + w * g01, hi + w * g23, down + wsp[0, sx, ty] * g13, up + wsp[2, sx, ty] * g02

            lo, hi, down, up = lax.fori_loop(0, nj, term, (zero,) * 4, unroll=8)
            PB[it, sx, 0:8, :] = lo
            PB[it, sx, 8:16, :] = hi
            PB[it, (sx + 1) % ni, 16:24, :] = hi
            PB[it, (sx - 1) % ni, 24:32, :] = lo
            PB[it, sx, 32:40, :] = down
            PB[it, sx, 40:48, :] = up
        R[it, i] = PB[it, i]
        parts = []
        for d in sorted(range(1, ni), key=lambda d: -abs((d // 2 + 2) % 4 - 2)):
            to = lax.rem(i + d, ni)
            copy = remote(PB.at[it, to], R.at[it, i], sr.at[it, d], rr.at[it, d], {"gx": to})
            copy.start()
            sends.append(copy)
            came = R.at[it, lax.rem(i + ni - d, ni)]
            parts.append(remote(PB.at[it, to], came, sr.at[it, d], rr.at[it, d], {"gx": to}))
        for copy in faces:
            copy.wait_recv()
        for copy in parts:
            copy.wait_recv()
        sums = R[it, 0]
        for n in range(1, ni):
            sums = sums + R[it, n]
        own = sums[0:16]
        other = [sums[16 + 8 * n : 24 + 8 * n] for n in range(4)]

        def row(block, c, chunk):
            return block[c * 4 + chunk : c * 4 + chunk + 1, :]

        def along_y(block, c0, c1):
            out = []
            for chunk in range(4):
                p = row(block, c0, chunk)[None, None]
                q = row(block, c1, chunk)[None, None]
                out.append((1.0 - wy) * p + wy * q)
            return jnp.concatenate(out, axis=1)

        def along_x(block, c0, c1):
            out = []
            for chunk in range(4):
                out.append((1.0 - wx8) * row(block, c0, chunk) + wx8 * row(block, c1, chunk))
            return jnp.concatenate(out, axis=0)

        sq = zero
        for n, (fun, c0, c1, sign, has) in enumerate((
            (along_y, 0, 1, -1.0, has_left),
            (along_y, 2, 3, 1.0, has_right),
            (along_x, 0, 2, -1.0, has_lower),
            (along_x, 1, 3, 1.0, has_upper),
        )):
            mine = FS[it, n] + fun(own, c0, c1).reshape(PLANE, 128)
            theirs = FR[it, n] + fun(other[n], 0, 1).reshape(PLANE, 128)
            jump = (mine - theirs) * (sign * has)
            JMP[n] = jump
            if sign > 0:
                sq = sq + jnp.sum((jump * jump).reshape(16, 8, 128), axis=0)
        me = i * nj + j
        row_sum = jnp.sum(sq, axis=0, keepdims=True)
        TS[it] = row_sum
        TR[it, pl.ds(me, 1), :] = row_sum

        for other_one in everyone:
            remote(TS.at[it], TR.at[it, pl.ds(me, 1)], st.at[it], rt.at[it], other_one).start()
        all_but_one = TR.at[it, pl.ds(0, ni * nj - 1)]
        told = remote(all_but_one, all_but_one, st.at[it], rt.at[it], right)
        arrived, sends = sends, [told]
        if it == 0:
            start = along_y(own, 0, 1)
            slope = along_y(own, 2, 3) - start
            m_start = beside_yz(start)
            m_slope = beside_yz(slope)

            def corrected(x, carry):
                wx = x.astype(F32) / 31.0
                e = start + wx * slope
                beside = m_start + wx * m_slope + 2.0 * e
                diag = tiles(U[0, rows(x + 1), :])
                U[1, rows(x + 1), :] = (
                    tiles(U[1, rows(x + 1), :]) - (diag * e - beside)
                ).reshape(PLANE, 128)
                X[rows(x), :] = (tiles(X[rows(x), :]) + e).reshape(PLANE, 128)
                return carry

            lax.fori_loop(0, 32, corrected, 0)
            U[1, rows(1), :] = U[1, rows(1), :] - (start - slope / 31.0).reshape(PLANE, 128)
            U[1, rows(32), :] = U[1, rows(32), :] - (start + slope * (32.0 / 31.0)).reshape(PLANE, 128)
        if it == ITERS - 1:
            faces_in = []
            for ref in (LAM, JMP):
                face = ref[1].reshape(4, 4, 8, 128)
                faces_in.append(jnp.concatenate([face[:, k].reshape(32, 128) for k in range(4)], axis=1))
                faces_in.append(jnp.concatenate([ref[3, pl.ds(k * 32, 32), :] for k in range(4)], axis=1))
            RL[...] = reorder(jnp.concatenate(faces_in, axis=0), PM[...], True)
            CC[...] = jnp.zeros((8, 512), F32)
            for c in range(4):
                for k in range(4):
                    CC[pl.ds(c, 1), pl.ds(k * 128, 128)] = row(own, c, k)
            corr = reorder(CC[...], PM[...], True)
            wy2 = lax.broadcasted_iota(jnp.int32, (32, 128), 0).astype(F32) / 31.0
            for c in range(4):
                c0, c1, c2, c3 = (corr[n : n + 1, c * 128 : c * 128 + 128] for n in range(4))
                begin = (1.0 - wy2) * c0 + wy2 * c1
                end = (1.0 - wy2) * c2 + wy2 * c3

                def add(x, carry, c=c, begin=begin, end=end):
                    wx = x.astype(F32) / 31.0
                    at = pl.ds(pl.multiple_of(x * 32, 32), 32)
                    xpre[c, at, :] = xpre[c, at, :] + ((1.0 - wx) * begin + wx * end)
                    return carry

                lax.fori_loop(0, 32, add, 0, unroll=8)
        for copy in arrived:
            copy.wait_send()
        told.wait_recv()
        total = jnp.sum(TR[it].reshape(ni * nj // 8, 8, 128), axis=0)
        count = (ni - 1) * nj * 32 * 512 + ni * 32 * (nj - 1) * 512
        step = 0.5 / jnp.sqrt(total_of(total) / float(count) + 1e-6)
        if it == 0:
            for n in range(4):
                LAM[n] = (JMP[n].reshape(16, 8, 128) * step[None]).reshape(PLANE, 128)
            U[1, rows(32), :] = U[1, rows(32), :] - LAM[1]
            U[1, rows(1), :] = U[1, rows(1), :] + LAM[0]
            for n, (t, s, sign) in ((3, (3, 7, -1.0)), (2, (0, 0, 1.0))):
                for c in range(4):
                    for h in range(4):
                        at = pl.ds(PLANE + h * 8 * PLANE + t * 32 + c * 8 + s, 8, stride=PLANE)
                        U[1, at, :] = U[1, at, :] + sign * LAM[n, pl.ds(c * 32 + h * 8, 8), :]
        else:
            for c in range(4):
                cols = pl.ds(c * 128, 128)
                for h in range(4):
                    both = RL[pl.ds(h * 8, 8), cols] + step * RL[pl.ds(64 + h * 8, 8), cols]
                    lamx_out[pl.ds(c * 32 + h, 8, stride=4), :] = both
                    both = RL[pl.ds(32 + h * 8, 8), cols] + step * RL[pl.ds(96 + h * 8, 8), cols]
                    lamy_out[pl.ds(c * 32 + h * 8, 8), :] = both
    for copy in sends:
        copy.wait_send()


def finish_kernel(field, lamx, lamy, vel, mx, my, my_s, sems):
    copies = []
    for c in range(4):
        at = pl.ds(c * 128, 128)
        for h in range(4):
            some = pl.ds(h * 256, 256)
            copies.append(pltpu.make_async_copy(field.at[c, some], vel.at[some, at], sems.at[2 + h, c]))
        copies.append(pltpu.make_async_copy(lamx.at[pl.ds(c * 32, 32)], mx.at[:, at], sems.at[1, c]))
    for copy in copies:
        copy.start()
    for c in range(4):
        my_s[:, :, pl.ds(c * 128, 128)] = lamy[pl.ds(c * 32, 32), :].reshape(32, 1, 128)
    copies.append(pltpu.make_async_copy(my_s, my, sems.at[0, 0]))
    copies[-1].start()
    for copy in copies:
        copy.wait()


def on_device(ni, nj, perm_class, class_drag, force, coarse_inverse, coarse_owner):
    hbm = pl.BlockSpec(memory_space=pl.ANY)
    vmem = pl.BlockSpec(memory_space=pltpu.VMEM)
    smem = pl.BlockSpec(memory_space=pltpu.SMEM)
    dma = pltpu.SemaphoreType.DMA
    xpre, lamx, lamy = pl.pallas_call(
        functools.partial(kernel, ni, nj),
        out_shape=(
            pltpu.VMEM((4, 1024, 128), F32),
            pltpu.VMEM((128, 128), F32),
            pltpu.VMEM((128, 128), F32),
        ),
        in_specs=[hbm, smem, hbm, hbm, smem],
        out_specs=(vmem, vmem, vmem),
        scratch_shapes=[
            pltpu.VMEM((SWEEPS + 2, 34 * PLANE, 128), F32),
            pltpu.VMEM((34 * PLANE, 128), F32),
            pltpu.VMEM((32 * PLANE, 128), F32),
            pltpu.VMEM((4, 1024, 128), F32),
            pltpu.VMEM((4, 1024, 128), jnp.int32),
            pltpu.VMEM((24, 8, 128), F32),
            pltpu.VMEM((3, ni, nj, 8, 128), F32),
            pltpu.SMEM((ni * nj, ni * nj), F32),
            pltpu.VMEM((ITERS, 16, 128), F32),
            pltpu.VMEM((ITERS, nj, 16, 128), F32),
            pltpu.VMEM((ITERS, ni, 48, 128), F32),
            pltpu.VMEM((ITERS, ni, 48, 128), F32),
            pltpu.VMEM((ITERS, 4, PLANE, 128), F32),
            pltpu.VMEM((ITERS, 4, PLANE, 128), F32),
            pltpu.VMEM((ITERS, 1, 128), F32),
            pltpu.VMEM((ITERS, ni * nj, 128), F32),
            pltpu.VMEM((4, PLANE, 128), F32),
            pltpu.VMEM((4, PLANE, 128), F32),
            pltpu.VMEM((512, 512), BF16),
            pltpu.VMEM((8, 512), F32),
            pltpu.VMEM((128, 512), F32),
            dma((4, 8)), dma,
            dma((ITERS, nj)), dma((ITERS, nj)),
            dma((ITERS, ni)), dma((ITERS, ni)),
            dma((ITERS, 4)), dma((ITERS, 4)),
            dma((ITERS,)), dma((ITERS,)),
        ],
        compiler_params=pltpu.CompilerParams(
            collective_id=0, has_side_effects=True, vmem_limit_bytes=56 * 2**20
        ),
        name="solve",
    )(perm_class.reshape(1024, 512), class_drag, force.reshape(1024, 512), coarse_inverse, coarse_owner)
    velocity, mult_x, mult_y = pl.pallas_call(
        finish_kernel,
        out_shape=(
            jax.ShapeDtypeStruct((1024, 512), F32),
            jax.ShapeDtypeStruct((32, 512), F32),
            jax.ShapeDtypeStruct((32, 1, 512), F32),
        ),
        in_specs=[vmem] * 3,
        out_specs=(hbm, hbm, hbm),
        scratch_shapes=[pltpu.VMEM((32, 1, 512), F32), dma((6, 4))],
        compiler_params=pltpu.CompilerParams(vmem_limit_bytes=4 * 2**20),
        name="finish",
    )(xpre, lamx, lamy)
    return velocity.reshape(32, 32, 512), mult_x[None], mult_y


def solution(mesh):
    return jax.shard_map(
        functools.partial(on_device, mesh.shape["gx"], mesh.shape["yz"]),
        mesh=mesh,
        in_specs=(P("gx", "yz", None), P(), P("gx", "yz", None), P(), P()),
        out_specs=(P("gx", "yz", None), P("gx", "yz", None), P("gx", "yz", None)),
        check_vma=False,
    )
```
